128 devices in a mesh: seq: 16 (over y, x), head: 8 (over z, core).
Axes of the slice: x: 4, y: 4, z: 4, core: 2. Of those that a mesh axis runs over, the one named last changes fastest.
Arguments:
- token_ids: int32 [2, 24], replicated, may hold values from 0 to 64127
- lengths: int32 [24], replicated, may hold values from 4096 to 16384, as said below
- embedding: bfloat16 [64128, 8192], P('head', 'seq'), may hold values from -100 to 100
- norm_gain: bfloat16 [8192], P('seq'), may hold values from 0.099609375 to 1.8984375
- w_qkv: bfloat16 [8192, 8, 1280], P('seq', 'head'), may hold values from -0.0625 to 0.0625
- k_cache: bfloat16 [24, 8, 16384, 128], P(None, 'head', 'seq'), may hold values from -110 to 110
- v_cache: bfloat16 [24, 8, 16384, 128], P(None, 'head', 'seq'), may hold values from -24 to 24
- w_out: bfloat16 [8, 1024, 8192], P('head', None, 'seq'), may hold values from -0.0625 to 0.0625
Outputs:
- attn_out: bfloat16 [2, 24, 8192], P(None, None, 'seq')
The draws below stay inside these ranges and needn't reach their ends.
Inputs may be any that keep to these rules, and one draw needn't show every extreme that they name: `lengths`: at least one sequence has 16384 cached positions.
All inputs are finite; a program needn't handle non-finite values.
Results may differ from the reference program's by a relative error of at most 0.012.
The reference program's roundings to bfloat16 on the way count: a program that leaves them out, or rounds other values in their place, can miss the bound.
Values may be sent and summed in bfloat16 or wider, within the bound.
No kernel may reach another device: no remote copies, remote signals or barrier semaphores. Data moves between devices by JAX's collectives and lax.ppermute only.
A program may use at most 128 MiB of HBM per device.

```python
import jax
import jax.numpy as jnp
from jax import lax

D = 8192
HD = 128
KVH = 8
GROUP = 8
VOCAB = 64128
ROWS = 24
CTX = 16384


def draw_lengths(key, part):
    key = jax.random.fold_in(key, 14)
    first_key, second_key = jax.random.split(key, 2)
    values = jax.random.randint(first_key, (ROWS,), CTX // 4, CTX + 1, dtype=jnp.int32)
    chosen = jax.random.randint(second_key, (), 0, ROWS, dtype=jnp.int32)
    return jnp.where(jnp.arange(ROWS, dtype=jnp.int32) == chosen, CTX, values).astype(jnp.int32)


def draw_embedding(key, part):
    key = jax.random.fold_in(key, 11)
    first_key = jax.random.fold_in(key, 0)
    column = jnp.arange(D, dtype=jnp.float32) / D
    rising = jnp.power(3.0, 0.5 * column)[None, :]
    values = jnp.clip(jax.random.normal(first_key, (VOCAB, D), jnp.float32), -4.0, 4.0) * rising
    return values.astype(jnp.bfloat16)


def draw_k_cache(key, part):
    key = jax.random.fold_in(key, 12)
    first_key = jax.random.fold_in(key, 0)
    values = jnp.clip(jax.random.normal(first_key, (ROWS, KVH, CTX, HD), jnp.float32), -4.0, 4.0) * 1.5
    return values.astype(jnp.bfloat16)


def draw_v_cache(key, part):
    key = jax.random.fold_in(key, 13)
    first_key, second_key = jax.random.split(key, 2)
    place = (jnp.arange(CTX, dtype=jnp.float32) / CTX * 2.0 - 1.0)[None, None, :, None]
    trend = jnp.clip(jax.random.normal(second_key, (ROWS, KVH, 1, HD), jnp.float32), -1.5, 1.5)
    noise = jnp.clip(jax.random.normal(first_key, (ROWS, KVH, CTX, HD), jnp.float32), -4.0, 4.0)
    return (noise + 6.0 * trend * place).astype(jnp.bfloat16)


def set_ends(result, stream_key, smallest, high):
    longest = result.shape.index(max(result.shape))
    spots = []
    for shift in (0, 1):
        where = [jax.random.randint(jax.random.fold_in(stream_key, axis), (), 0, length) for axis, length in enumerate(result.shape)]
        where[longest] = (where[longest] + shift) % result.shape[longest]
        spots.append(tuple(where))
    return result.at[spots[0]].set(smallest).at[spots[1]].set(high)


def block_levels(key, shape, shards, low, top_value):
    def one(dim, blocks):
        draws = jax.random.uniform(jax.random.fold_in(jax.random.fold_in(key, 6), dim), (blocks,), jnp.float32, low / len(shards), top_value / len(shards))
        return jnp.repeat(jnp.exp(draws), shape[dim] // blocks).reshape((-1,) + (1,) * (len(shape) - dim - 1))

    loudness = one(*shards[0])
    for cut in shards[1:]:
        loudness = loudness * one(*cut)
    return loudness


def gaussian(rng, dims, scale, reach, pieces=(), held_as=jnp.bfloat16):
    factor_of = block_levels(rng, dims, pieces, -0.22, 0.18) if pieces else 1.0
    result = jax.random.normal(rng, dims, jnp.float32) * scale * factor_of
    return jnp.minimum(jnp.maximum(result, -reach), reach).astype(held_as)


def setup_inputs(seed: int = 0) -> dict:
    arg_keys = jax.random.split(jax.random.key(seed), 9)
    token_ids = set_ends(jax.random.randint(arg_keys[0], (2, ROWS), 0, VOCAB), jax.random.fold_in(arg_keys[0], 1), 0, VOCAB - 1).astype(jnp.int32)
    lengths = draw_lengths(jax.random.fold_in(arg_keys[8], 71), 0)
    embedding = draw_embedding(jax.random.fold_in(arg_keys[8], 71), 0)
    norm_gain = jnp.clip(1.0 + 0.18 * jax.random.normal(arg_keys[3], (D,), jnp.float32), 0.099609375, 1.8984375).astype(jnp.bfloat16)
    w_qkv = gaussian(arg_keys[4], (D, KVH, (GROUP + 2) * HD), D ** -0.5, 0.0625, ((0, 16), (1, 8)))
    k_cache = draw_k_cache(jax.random.fold_in(arg_keys[8], 71), 0)
    v_cache = draw_v_cache(jax.random.fold_in(arg_keys[8], 71), 0)
    w_out = gaussian(arg_keys[7], (KVH, GROUP * HD, D), (KVH * GROUP * HD) ** -0.5, 0.0625, ((0, 8), (2, 16)))
    return dict(token_ids=token_ids, lengths=lengths, embedding=embedding, norm_gain=norm_gain, w_qkv=w_qkv, k_cache=k_cache, v_cache=v_cache, w_out=w_out)


rope_base = 500000.0
epsilon = 1e-05
negative = -1e+30

def rope_tables(positions, head_dim):
    half_dim = head_dim // 2
    exponent = jnp.arange(half_dim, dtype=jnp.float32) * (2.0 / head_dim)
    frequency = jnp.power(jnp.float32(rope_base), -exponent)
    angles = positions.astype(jnp.float32)[:, None] * frequency[None, :]
    return (jnp.cos(angles), jnp.sin(angles))

def rotate(block, cosine, sine_part):
    half_dim = block.shape[-1] // 2
    first_half = block[..., :half_dim]
    second_half = block[..., half_dim:]
    return jnp.concatenate([first_half * cosine - second_half * sine_part, second_half * cosine + first_half * sine_part], axis=-1)

def finish(summed, squares, positions, group, head_dim):
    count_rows = summed.shape[0]
    normed = summed * lax.rsqrt(squares / D + epsilon)
    normed = normed.reshape(count_rows, -1, group + 2, head_dim)
    cosine, sine_part = rope_tables(positions, head_dim)
    query_rows = rotate(normed[:, :, :group], cosine[:, None, None, :], sine_part[:, None, None, :]) * head_dim ** (-0.5)
    new_key = rotate(normed[:, :, group], cosine[:, None, :], sine_part[:, None, :])
    new_value = normed[:, :, group + 1]
    return (query_rows.astype(jnp.bfloat16), new_key.astype(jnp.bfloat16), new_value.astype(jnp.bfloat16))

def reference(token_ids, lengths, embedding, norm_gain, w_qkv, k_cache, v_cache, w_out):
    gathered = embedding[token_ids.reshape(-1)]
    widened = gathered.astype(jnp.float32)
    squares = lax.optimization_barrier(jnp.sum(widened * widened, axis=1, keepdims=True))
    scaled = (widened * norm_gain.astype(jnp.float32)[None, :]).astype(jnp.bfloat16)
    summed = jnp.dot(scaled, w_qkv.reshape(D, -1), preferred_element_type=jnp.float32)
    positions = (lengths[None, :] + jnp.arange(2, dtype=jnp.int32)[:, None]).reshape(-1)
    query_rows, new_key, new_value = finish(summed, squares, positions, GROUP, HD)
    query_rows = query_rows.reshape(2, ROWS, KVH, GROUP, HD).transpose(1, 2, 0, 3, 4).reshape(ROWS, KVH, 2 * GROUP, HD)
    new_key = new_key.reshape(2, ROWS, KVH, HD).transpose(1, 2, 0, 3)
    new_value = new_value.reshape(2, ROWS, KVH, HD).transpose(1, 2, 0, 3)
    step_of_query = jnp.arange(2 * GROUP, dtype=jnp.int32) // GROUP
    allowed = jnp.arange(2, dtype=jnp.int32)[None, :] <= step_of_query[:, None]
    cache_positions = jnp.arange(CTX, dtype=jnp.int32)

    def one_row(inputs):
        queries, keys_new, values_new, keys_old, values_old, length = inputs
        keys_all = jnp.concatenate([keys_old, keys_new], axis=1).astype(jnp.float32)
        values_all = jnp.concatenate([values_old, values_new], axis=1).astype(jnp.float32)
        logits = jnp.einsum('gqd,gpd->gqp', queries.astype(jnp.float32), keys_all)
        cache_live = jnp.broadcast_to((cache_positions < length)[None, :], (2 * GROUP, CTX))
        visible = jnp.concatenate([cache_live, allowed], axis=1)[None]
        masked = jnp.where(visible, logits, negative)
        largest = lax.optimization_barrier(jnp.max(masked, axis=2, keepdims=True))
        exponentials = jnp.where(visible, jnp.exp(masked - largest), 0.0)
        denominator = lax.optimization_barrier(jnp.sum(exponentials, axis=2, keepdims=True))
        rounded = lax.optimization_barrier(exponentials.astype(jnp.bfloat16)).astype(jnp.float32)
        numerator = jnp.einsum('gqp,gpd->gqd', rounded, values_all)
        return (numerator / denominator).astype(jnp.bfloat16)
    attention = lax.map(one_row, (query_rows, new_key, new_value, k_cache, v_cache, lengths))
    attention = attention.reshape(ROWS, KVH, 2, GROUP, HD).transpose(2, 0, 1, 3, 4).reshape(2 * ROWS, KVH * GROUP * HD)
    projected = jnp.dot(attention, w_out.reshape(KVH * GROUP * HD, D), preferred_element_type=jnp.float32)
    return projected.astype(jnp.bfloat16).reshape(2, ROWS, D)
```

```python
import functools

import jax
import jax.numpy as jnp
from jax import lax
from jax.experimental import pallas as pl
from jax.experimental.pallas import tpu as pltpu
from jax.sharding import PartitionSpec as P

D = 8192
TILE = 16
LANES = 128
SUB = 8

rope_base = 500000.0
epsilon = 1e-05
negative = -1e30

VMEM = pl.BlockSpec(memory_space=pltpu.VMEM)
SMEM = pl.BlockSpec(memory_space=pltpu.SMEM)
ANY = pl.BlockSpec(memory_space=pl.ANY)


def in_vmem(array):
    return pltpu.with_memory_space_constraint(array, pltpu.VMEM)


def in_hbm(array):
    return pltpu.with_memory_space_constraint(array, pltpu.HBM)


def call(kernel, name, out, in_specs, scratch=(), limit=4):
    return pl.pallas_call(
        kernel,
        out_shape=jax.ShapeDtypeStruct(*out),
        in_specs=in_specs,
        out_specs=VMEM,
        scratch_shapes=list(scratch),
        compiler_params=pltpu.CompilerParams(vmem_limit_bytes=limit << 20),
        name=name,
    )


def swap(array, axis_name):
    return lax.all_to_all(array, axis_name, 0, 0, tiled=True)


SEQ_MASKS = (1, 3, 4, 12)


def place_of(me, source):
    differ = me ^ source
    return differ ^ ((differ >> 1) & 5)


def rope_frequency(head_dim):
    exponent = jnp.arange(head_dim // 2, dtype=jnp.float32) * (2.0 / head_dim)
    frequency = jnp.power(jnp.float32(rope_base), -exponent)
    return jnp.concatenate([frequency, frequency])[None, :]


def cos_sin(angles):
    turn = jnp.floor(angles * 0.6366197723675814 + 0.5)
    rest = ((angles - turn * 1.5703125) - turn * 0.00048351287841796875) - turn * 3.13916478589249e-07
    square = rest * rest
    sine = ((-1.9515295891e-4 * square + 8.3321608736e-3) * square - 1.6666654611e-1) * square
    sine = sine * rest + rest
    cosine = (2.443315711809948e-5 * square - 1.388731625493765e-3) * square
    cosine = (cosine + 4.166664568298827e-2) * square * square - 0.5 * square + 1.0
    quarter = turn.astype(jnp.int32) & 3
    odd = (quarter & 1) == 1
    first, second = jnp.where(odd, sine, cosine), jnp.where(odd, cosine, sine)
    return (
        jnp.where((quarter == 1) | (quarter == 2), -first, first),
        jnp.where(quarter >= 2, -second, second),
    )


def pick_kernel(
    cache_dev, ids_ref, lengths_ref, frequency_ref, table_ref, far_w_ref,
    x_ref, rope_ref, limits_ref, w_ref, held, sem, w_sem,
):
    vocab_dev, feat = table_ref.shape
    steps, rows = ids_ref.shape
    tokens = steps * rows
    first = lax.axis_index("head") * vocab_dev
    places = []
    for i in range(tokens):
        local = ids_ref[i // rows, i % rows] - first
        inside = (local >= 0) & (local < vocab_dev)
        local = jnp.clip(local, 0, vocab_dev - 1)
        within = local & (TILE - 1)
        pltpu.make_async_copy(
            table_ref.at[pl.ds(pl.multiple_of(local - within, TILE), TILE)],
            held.at[pl.ds(i * TILE, TILE)],
            sem,
        ).start()
        places.append(jnp.where(inside, i * TILE + within, -1))
    w_copy = pltpu.make_async_copy(far_w_ref, w_ref, w_sem)
    w_copy.start()

    me = lax.axis_index("seq")
    near = LANES // (2 * SUB)
    sub = lax.broadcasted_iota(jnp.int32, (SUB, LANES), 0)
    lane = lax.broadcasted_iota(jnp.int32, (SUB, LANES), 1)
    position = jnp.zeros((SUB, LANES), jnp.int32)
    limits = jnp.zeros((SUB, LANES), jnp.int32)
    for g in range(rows // near):
        position = jnp.where(sub == g, lengths_ref[g * near + me // 2] + me % 2, position)
        for r in range(near):
            here = (sub == g) & (lane // (2 * SUB) == r)
            limits = jnp.where(here, lengths_ref[g * near + r], limits)
    limits_ref[...] = limits - me * cache_dev
    cosine, sine = cos_sin(position.astype(jnp.float32) * frequency_ref[...])
    rope_ref[:SUB] = cosine
    rope_ref[SUB:] = jnp.where(lane < LANES // 2, -sine, sine)

    row = lax.broadcasted_iota(jnp.int32, (tokens, 1), 0)
    choice = jnp.full((tokens, 1), -1, jnp.int32)
    for i in range(tokens):
        choice = jnp.where(row == i, places[i], choice)
    column = lax.broadcasted_iota(jnp.int32, (tokens, tokens * TILE), 1)
    select = jnp.where(column == choice, 1.0, 0.0).astype(jnp.bfloat16)
    pltpu.make_async_copy(table_ref.at[pl.ds(0, tokens * TILE)], held, sem).wait()
    picked = jnp.dot(select, held[...], preferred_element_type=jnp.float32)
    x_ref[...] = picked.astype(jnp.bfloat16)
    w_copy.wait()


def project_kernel(x_ref, gain_ref, w_ref, out_ref):
    tokens = x_ref.shape[0]
    count, own, width = out_ref.shape
    width -= LANES
    row = lax.broadcasted_iota(jnp.int32, (count * SUB, tokens), 0)
    column = lax.broadcasted_iota(jnp.int32, (count * SUB, tokens), 1)
    owner, k = row // SUB, row % SUB
    token = (owner % 2) * (tokens // 2) + owner // 2 + (count // 2) * k
    spread = jnp.where((column == token) & (k < own), 1.0, 0.0).astype(jnp.bfloat16)
    x = jnp.dot(spread, x_ref[...], preferred_element_type=jnp.float32)
    squares = jnp.sum(x * x, axis=1, keepdims=True)
    scaled = (x * gain_ref[...]).astype(jnp.bfloat16)
    partial = jnp.dot(scaled, w_ref[...], preferred_element_type=jnp.float32)
    squares = jnp.broadcast_to(squares, (count * SUB, LANES))
    for j in range(count):
        out_ref[j, :, :width] = partial[j * SUB : j * SUB + own]
        out_ref[j, :, width:] = squares[j * SUB : j * SUB + own]


def finish_kernel(parts_ref, rope_ref, out_ref):
    _, own, width = parts_ref.shape
    head_dim = out_ref.shape[1]
    summed = parts_ref[0]
    for j in range(1, parts_ref.shape[0]):
        summed = summed + parts_ref[j]
    scale = lax.rsqrt(summed[:, width - LANES :] / D + epsilon)
    cosine, sine_part = rope_ref[:own], rope_ref[SUB : SUB + own]
    group = (width - LANES) // head_dim - 2
    blocks = []
    for b in range(group + 2):
        block = summed[:, b * head_dim : (b + 1) * head_dim] * scale
        if b <= group:
            block = block * cosine + pltpu.roll(block, head_dim // 2, 1) * sine_part
        if b < group:
            block = block * head_dim ** (-0.5)
        blocks.append(block)
    rows = [blocks[b][k : k + 1] for k in range(own) for b in range(group)]
    rows += [blocks[group], blocks[group + 1]]
    rows.append(jnp.zeros((out_ref.shape[0] - own * (group + 2), head_dim), jnp.float32))
    out_ref[...] = jnp.concatenate(rows, axis=0).astype(jnp.bfloat16)


def attend_kernel(
    limits_ref, first_ref, second_ref, k_ref, v_ref, out_ref, rows_ref, scores_ref
):
    row_count, cache_dev, head_dim = k_ref.shape
    count = rows_ref.shape[0]
    rows_ref[: count // 2] = first_ref[...]
    rows_ref[count // 2 :] = second_ref[...]
    per_row = 2 * SUB
    near = LANES // per_row
    groups = row_count // near
    chunk = 256
    me = lax.axis_index("seq")
    lane = lax.broadcasted_iota(jnp.int32, (1, LANES), 1)
    position = lax.broadcasted_iota(jnp.int32, (chunk, LANES), 0)
    slot = lax.broadcasted_iota(jnp.int32, (LANES, LANES), 0)
    rows = [rows_ref[place_of(me, j)].astype(jnp.float32) for j in range(count)]
    new_keys = jnp.concatenate([part[groups * SUB :] for part in rows], axis=0)
    new_values = pltpu.roll(new_keys, LANES - groups, 0).astype(jnp.bfloat16)
    new_keys = new_keys.astype(jnp.bfloat16)
    tops, totals = [], []
    for g in range(groups):
        turned = jnp.concatenate([part[g * SUB : (g + 1) * SUB] for part in rows], axis=0).T
        blocks = [
            jnp.where(lane // per_row == r, turned, 0.0).astype(jnp.bfloat16) for r in range(near)
        ]
        weights = jnp.concatenate(blocks, axis=0)
        limit = limits_ref[g : g + 1]

        fresh = jnp.dot(new_keys, turned.astype(jnp.bfloat16), preferred_element_type=jnp.float32)
        seen = (
            (slot % SUB == g)
            & (slot // per_row == lane // per_row)
            & (slot // SUB <= lane // SUB)
            & (me == 0)
        )
        fresh = jnp.where(seen, fresh, negative)
        top = jnp.max(fresh, axis=0, keepdims=True)
        for c in range(cache_dev // chunk):
            keys = jnp.concatenate(
                [k_ref[g * near + r, pl.ds(c * chunk, chunk)] for r in range(near)], axis=1
            )
            scores = jnp.dot(keys, weights, preferred_element_type=jnp.float32)
            scores = jnp.where(position < limit - c * chunk, scores, negative)
            scores_ref[g, pl.ds(c * chunk, chunk)] = scores
            top = jnp.maximum(top, jnp.max(scores, axis=0, keepdims=True))

        fresh = jnp.exp(fresh - top)
        total = jnp.sum(fresh, axis=0, keepdims=True)
        parts = []
        for c in range(cache_dev // chunk):
            weight = jnp.exp(scores_ref[g, pl.ds(c * chunk, chunk)] - top)
            total = total + jnp.sum(weight, axis=0, keepdims=True)
            parts.append(weight.astype(jnp.bfloat16).T)
        parts = jnp.concatenate(parts, axis=1)
        value = []
        for r in range(0, near, 2):
            both = jnp.dot(
                parts[r * per_row : (r + 2) * per_row],
                jnp.concatenate([v_ref[g * near + r], v_ref[g * near + r + 1]], axis=1),
                preferred_element_type=jnp.float32,
            )
            value += [both[:per_row, :head_dim], both[per_row:, head_dim:]]
        value = jnp.concatenate(value, axis=0) + jnp.dot(
            fresh.T.astype(jnp.bfloat16), new_values, preferred_element_type=jnp.float32
        )
        for j in range(count):
            out_ref[j, pl.ds(g * SUB, SUB)] = value[j * SUB : (j + 1) * SUB]
        tops.append(top)
        totals.append(total)
    spare = jnp.zeros((SUB - 2 * groups, LANES), jnp.float32)
    stats = jnp.concatenate(tops + totals + [spare], axis=0)
    for j in range(count):
        turn = (LANES - SUB * j) % LANES
        out_ref[j, pl.ds(groups * SUB, SUB)] = pltpu.roll(stats, turn, 1) if turn else stats


def merge_kernel(parts_ref, out_ref):
    count, rows, head_dim = parts_ref.shape
    groups = rows // SUB - 1
    stats = parts_ref[:, groups * SUB :]
    top = stats[0]
    for j in range(1, count):
        top = jnp.maximum(top, stats[j])
    factors = [jnp.exp(stats[j] - top) for j in range(count)]
    denominator = factors[0] * pltpu.roll(stats[0], SUB - groups, 0)
    for j in range(1, count):
        denominator = denominator + factors[j] * pltpu.roll(stats[j], SUB - groups, 0)
    shares = jnp.concatenate([factor / denominator for factor in factors], axis=0).T[:SUB]
    merged = []
    for g in range(groups):
        total = jnp.zeros((SUB, head_dim), jnp.float32)
        for j in range(count):
            column = j * SUB + g
            total = total + parts_ref[j, pl.ds(g * SUB, SUB)] * shares[:, column : column + 1]
        merged.append(total)
    out_ref[...] = jnp.concatenate(merged, axis=1).astype(jnp.bfloat16)


def output_kernel(first_ref, second_ref, w_ref, out_ref, attention_ref, held):
    count, heads, width = attention_ref.shape
    attention_ref[: count // 2] = first_ref[...]
    attention_ref[count // 2 :] = second_ref[...]
    head_dim = width // (out_ref.shape[0] // count)
    me = lax.axis_index("seq")
    for j in range(count):
        part = attention_ref[place_of(me, j)].astype(jnp.float32)
        for g in range(width // head_dim):
            held[g, pl.ds(j * heads, heads)] = part[:, g * head_dim : (g + 1) * head_dim]
    left = jnp.concatenate(
        [
            jnp.concatenate(
                [
                    held[g, pl.ds(step * heads + i, count // 2, stride=2 * heads)]
                    for i in range(heads)
                ],
                axis=1,
            )
            for step in range(2)
            for g in range(width // head_dim)
        ],
        axis=0,
    )
    out_ref[...] = jnp.dot(left.astype(jnp.bfloat16), w_ref[...], preferred_element_type=jnp.float32)


def spread(array, axis_name, masks, size):
    halves = (array[None],)
    for mask in masks:
        held = jnp.concatenate(halves, axis=0) if len(halves) == 2 else halves[0]
        halves = (held, lax.ppermute(held, axis_name, [(i, i ^ mask) for i in range(size)]))
    return halves


def double(array, axis_name, mask, size):
    pairs = [(i, i ^ mask) for i in range(size)]
    return array + lax.ppermute(array, axis_name, pairs)


def body(token_ids, lengths, embedding, norm_gain, w_qkv, k_cache, v_cache, w_out):
    n_seq, n_head = lax.axis_size("seq"), lax.axis_size("head")
    feat = embedding.shape[1]
    row_count, _, cache_dev, head_dim = k_cache.shape
    tokens = 2 * row_count
    own = tokens // n_seq
    width = w_qkv.shape[2]
    block = (own + 1) * SUB

    picked, rope, limits, w_near = pl.pallas_call(
        functools.partial(pick_kernel, cache_dev),
        out_shape=[
            jax.ShapeDtypeStruct((tokens, feat), jnp.bfloat16),
            jax.ShapeDtypeStruct((2 * SUB, LANES), jnp.float32),
            jax.ShapeDtypeStruct((SUB, LANES), jnp.int32),
            pltpu.VMEM((feat, width), jnp.bfloat16),
        ],
        in_specs=[SMEM, SMEM, VMEM, ANY, ANY],
        out_specs=[VMEM] * 4,
        scratch_shapes=[
            pltpu.VMEM((tokens * TILE, feat), jnp.bfloat16),
            pltpu.SemaphoreType.DMA,
            pltpu.SemaphoreType.DMA,
        ],
        compiler_params=pltpu.CompilerParams(vmem_limit_bytes=8 << 20),
        name="pick",
    )(
        in_hbm(token_ids),
        in_hbm(lengths),
        rope_frequency(head_dim),
        in_hbm(embedding),
        in_hbm(w_qkv.reshape(feat, width)),
    )
    for mask in (1, 2, 6):
        picked = double(picked, "head", mask, n_head)
    gain = norm_gain.astype(jnp.float32).reshape(1, feat)

    partial = call(
        project_kernel, "project", ((n_seq, own, width + LANES), jnp.float32), [VMEM] * 3
    )(picked, gain, in_vmem(w_near))
    partial = swap(partial, "seq")
    rows = call(finish_kernel, "finish", ((block, head_dim), jnp.bfloat16), [VMEM] * 2)(
        partial, rope
    )
    rows = spread(rows, "seq", SEQ_MASKS, n_seq)

    partial = call(
        attend_kernel,
        "attend",
        ((n_seq, block, head_dim), jnp.float32),
        [VMEM] * 5,
        [
            pltpu.VMEM((n_seq, block, head_dim), jnp.bfloat16),
            pltpu.VMEM((own, cache_dev, LANES), jnp.float32),
        ],
        8,
    )(limits, *rows, in_vmem(k_cache[:, 0]), in_vmem(v_cache[:, 0]))
    partial = swap(partial, "seq")
    attention = call(merge_kernel, "merge", ((SUB, own * head_dim), jnp.bfloat16), [VMEM])(
        partial
    )
    attention = spread(attention, "seq", SEQ_MASKS, n_seq)

    terms = call(
        output_kernel,
        "output",
        ((tokens, w_out.shape[2]), jnp.float32),
        [VMEM] * 3,
        [
            pltpu.VMEM((n_seq, SUB, own * head_dim), jnp.bfloat16),
            pltpu.VMEM((own, n_seq * SUB, head_dim), jnp.float32),
        ],
    )(*attention, in_vmem(w_out[0]))
    for mask in (1, 2, 6):
        terms = double(terms, "head", mask, n_head)
    return terms.astype(jnp.bfloat16).reshape(2, row_count, -1)


def solution(mesh):
    return jax.shard_map(
        body,
        mesh=mesh,
        in_specs=(
            P(),
            P(),
            P("head", "seq"),
            P("seq"),
            P("seq", "head", None),
            P(None, "head", "seq", None),
            P(None, "head", "seq", None),
            P("head", None, "seq"),
        ),
        out_specs=P(None, None, "seq"),
        check_vma=False,
    )
```

```python
import functools

import jax
import jax.numpy as jnp
from jax import lax
from jax.experimental import pallas as pl
from jax.experimental.pallas import tpu as pltpu
from jax.sharding import PartitionSpec as P

D = 8192
TILE = 16
LANES = 128
SUB = 8
BLOCK = 32
SPAN = 32

rope_base = 500000.0
epsilon = 1e-05
negative = -1e30

VMEM = pl.BlockSpec(memory_space=pltpu.VMEM)
SMEM = pl.BlockSpec(memory_space=pltpu.SMEM)
ANY = pl.BlockSpec(memory_space=pl.ANY)


def in_vmem(array):
    return pltpu.with_memory_space_constraint(array, pltpu.VMEM)


def in_hbm(array):
    return pltpu.with_memory_space_constraint(array, pltpu.HBM)


def call(kernel, name, out, in_specs, scratch=(), limit=4):
    return pl.pallas_call(
        kernel,
        out_shape=jax.ShapeDtypeStruct(*out),
        in_specs=in_specs,
        out_specs=VMEM,
        scratch_shapes=list(scratch),
        compiler_params=pltpu.CompilerParams(vmem_limit_bytes=limit << 20),
        name=name,
    )


def swap(array, axis_name):
    return lax.all_to_all(array, axis_name, 0, 0, tiled=True)


def rope_frequency(head_dim):
    exponent = jnp.arange(head_dim // 2, dtype=jnp.float32) * (2.0 / head_dim)
    frequency = jnp.power(jnp.float32(rope_base), -exponent)
    return jnp.concatenate([frequency, frequency])[None, :]


def cos_sin(angles):
    turn = jnp.floor(angles * 0.6366197723675814 + 0.5)
    rest = ((angles - turn * 1.5703125) - turn * 0.00048351287841796875) - turn * 3.13916478589249e-07
    square = rest * rest
    sine = ((-1.9515295891e-4 * square + 8.3321608736e-3) * square - 1.6666654611e-1) * square
    sine = sine * rest + rest
    cosine = (2.443315711809948e-5 * square - 1.388731625493765e-3) * square
    cosine = (cosine + 4.166664568298827e-2) * square * square - 0.5 * square + 1.0
    quarter = turn.astype(jnp.int32) & 3
    odd = (quarter & 1) == 1
    first, second = jnp.where(odd, sine, cosine), jnp.where(odd, cosine, sine)
    return (
        jnp.where((quarter == 1) | (quarter == 2), -first, first),
        jnp.where(quarter >= 2, -second, second),
    )


def pick_kernel(
    cache_dev, ids_ref, lengths_ref, frequency_ref, table_ref, far_w_ref,
    x_ref, rope_ref, limits_ref, w_ref, held, sem, w_sem,
):
    vocab_dev, feat = table_ref.shape
    steps, rows = ids_ref.shape
    tokens = steps * rows
    first = lax.axis_index("head") * vocab_dev
    places = []
    for i in range(tokens):
        local = ids_ref[i // rows, i % rows] - first
        inside = (local >= 0) & (local < vocab_dev)
        local = jnp.clip(local, 0, vocab_dev - 1)
        within = local & (TILE - 1)
        pltpu.make_async_copy(
            table_ref.at[pl.ds(pl.multiple_of(local - within, TILE), TILE)],
            held.at[pl.ds(i * TILE, TILE)],
            sem,
        ).start()
        places.append(jnp.where(inside, i * TILE + within, -1))
    w_copy = pltpu.make_async_copy(far_w_ref, w_ref, w_sem)
    w_copy.start()

    me = lax.axis_index("seq")
    near = LANES // (2 * SUB)
    sub = lax.broadcasted_iota(jnp.int32, (SUB, LANES), 0)
    lane = lax.broadcasted_iota(jnp.int32, (SUB, LANES), 1)
    own = rows // near
    block = rope_ref.shape[0] // 2
    line = lax.broadcasted_iota(jnp.int32, (block, LANES), 0)
    position = jnp.zeros((block, LANES), jnp.int32)
    limits = jnp.zeros((SUB, LANES), jnp.int32)
    for g in range(own):
        here = (line // SUB == g) | (line == own * SUB + g)
        position = jnp.where(here, lengths_ref[g * near + me // 2] + me % 2, position)
        for r in range(near):
            here = (sub == g) & (lane // (2 * SUB) == r)
            limits = jnp.where(here, lengths_ref[g * near + r], limits)
    limits_ref[...] = limits - me * cache_dev
    cosine, sine = cos_sin(position.astype(jnp.float32) * frequency_ref[...])
    turned = line < own * SUB + own
    first_half = lax.broadcasted_iota(jnp.int32, (block, LANES), 1) < LANES // 2
    rope_ref[:block] = jnp.where(turned, cosine, 1.0)
    rope_ref[block:] = jnp.where(turned, jnp.where(first_half, -sine, sine), 0.0)

    row = lax.broadcasted_iota(jnp.int32, (tokens, 1), 0)
    choice = jnp.full((tokens, 1), -1, jnp.int32)
    for i in range(tokens):
        choice = jnp.where(row == i, places[i], choice)
    column = lax.broadcasted_iota(jnp.int32, (tokens, tokens * TILE), 1)
    select = jnp.where(column == choice, 1.0, 0.0).astype(jnp.bfloat16)
    pltpu.make_async_copy(table_ref.at[pl.ds(0, tokens * TILE)], held, sem).wait()
    picked = jnp.dot(select, held[...], preferred_element_type=jnp.float32)
    x_ref[...] = picked.astype(jnp.bfloat16)
    w_copy.wait()


def project_kernel(x_ref, gain_ref, w_ref, out_ref):
    tokens = x_ref.shape[0]
    count = out_ref.shape[0] // BLOCK
    own = tokens // count
    row = lax.broadcasted_iota(jnp.int32, (tokens, tokens), 0)
    column = lax.broadcasted_iota(jnp.int32, (tokens, tokens), 1)
    owner, k = row % count, row // count
    token = (owner % 2) * (tokens // 2) + owner // 2 + (count // 2) * k
    order = jnp.where(column == token, 1.0, 0.0).astype(jnp.bfloat16)
    x = jnp.dot(order, x_ref[...], preferred_element_type=jnp.float32)
    squares = jnp.sum(x * x, axis=1, keepdims=True)
    scaled = (x * gain_ref[...]).astype(jnp.bfloat16)
    partial = jnp.dot(scaled, w_ref[...], preferred_element_type=jnp.float32)
    lane = lax.broadcasted_iota(jnp.int32, (count, LANES), 1)
    last = jnp.zeros((count, LANES), jnp.float32)
    for k in range(own):
        part = slice(k * count, (k + 1) * count)
        for b in range(SUB + 2):
            line = k * SUB + b if b < SUB else (own * (b - SUB) + own * SUB + k)
            out_ref[pl.ds(line, count, stride=BLOCK)] = partial[part, b * LANES : (b + 1) * LANES]
        last = jnp.where(lane // SPAN == k, squares[part], last)
    out_ref[pl.ds(BLOCK - 2, count, stride=BLOCK)] = last
    out_ref[pl.ds(BLOCK - 1, count, stride=BLOCK)] = jnp.zeros((count, LANES), jnp.float32)


def finish_kernel(parts_ref, rope_ref, out_ref):
    count, block, head_dim = parts_ref.shape
    own = block // SUB - 1
    summed = parts_ref[0]
    for j in range(1, count):
        summed = summed + parts_ref[j]
    inverse = lax.rsqrt(summed[block - 2 : block - 1] / D + epsilon)
    line = lax.broadcasted_iota(jnp.int32, (block, head_dim), 0)
    scale = jnp.zeros((block, head_dim), jnp.float32)
    for k in range(own):
        here = (line // SUB == k) | (line == own * SUB + k) | (line == own * SUB + own + k)
        here = here & ((line < own * SUB) | (line % SUB < 2 * own))
        scale = jnp.where(here, inverse[:, k * SPAN : k * SPAN + 1], scale)
    normed = summed * scale
    turned = normed * rope_ref[:block] + pltpu.roll(normed, head_dim // 2, 1) * rope_ref[block:]
    turned = jnp.where(line < own * SUB, turned * head_dim ** (-0.5), turned).astype(jnp.bfloat16)
    for j in range(out_ref.shape[0]):
        out_ref[j] = turned


def attend_kernel(limits_ref, rows_ref, k_ref, v_ref, out_ref, scores_ref):
    row_count, cache_dev, head_dim = k_ref.shape
    count = rows_ref.shape[0]
    per_row = 2 * SUB
    near = LANES // per_row
    groups = row_count // near
    chunk = 256
    me = lax.axis_index("seq")
    lane = lax.broadcasted_iota(jnp.int32, (1, LANES), 1)
    position = lax.broadcasted_iota(jnp.int32, (chunk, LANES), 0)
    slot = lax.broadcasted_iota(jnp.int32, (LANES, LANES), 0)
    rows = rows_ref[...].astype(jnp.float32)
    new_keys = rows[:, groups * SUB :].reshape(count * SUB, head_dim)
    new_values = pltpu.roll(new_keys, LANES - groups, 0).astype(jnp.bfloat16)
    new_keys = new_keys.astype(jnp.bfloat16)

    def score(g):
        turned = rows[:, g * SUB : (g + 1) * SUB].reshape(count * SUB, head_dim).T
        blocks = [
            jnp.where(lane // per_row == r, turned, 0.0).astype(jnp.bfloat16) for r in range(near)
        ]
        weights = jnp.concatenate(blocks, axis=0)
        limit = limits_ref[g : g + 1]
        fresh = jnp.dot(new_keys, turned.astype(jnp.bfloat16), preferred_element_type=jnp.float32)
        seen = (
            (slot % SUB == g)
            & (slot // per_row == lane // per_row)
            & (slot // SUB <= lane // SUB)
            & (me == 0)
        )
        fresh = jnp.where(seen, fresh, negative)
        top = jnp.max(fresh, axis=0, keepdims=True)
        for c in range(cache_dev // chunk):
            keys = jnp.concatenate(
                [k_ref[g * near + r, pl.ds(c * chunk, chunk)] for r in range(near)], axis=1
            )
            scores = jnp.dot(keys, weights, preferred_element_type=jnp.float32)
            scores = jnp.where(position < limit - c * chunk, scores, negative)
            scores_ref[g, pl.ds(c * chunk, chunk)] = scores
            top = jnp.maximum(top, jnp.max(scores, axis=0, keepdims=True))
        return top, fresh

    def weigh(g, top, fresh):
        fresh = jnp.exp(fresh - top)
        total = jnp.sum(fresh, axis=0, keepdims=True)
        parts = []
        for c in range(cache_dev // chunk):
            weight = jnp.exp(scores_ref[g, pl.ds(c * chunk, chunk)] - top)
            total = total + jnp.sum(weight, axis=0, keepdims=True)
            parts.append(weight.astype(jnp.bfloat16).T)
        parts = jnp.concatenate(parts, axis=1)
        value = jnp.concatenate(
            [
                jnp.dot(
                    parts[r * per_row : (r + 1) * per_row],
                    v_ref[g * near + r],
                    preferred_element_type=jnp.float32,
                )
                for r in range(near)
            ],
            axis=0,
        ) + jnp.dot(fresh.T.astype(jnp.bfloat16), new_values, preferred_element_type=jnp.float32)
        for j in range(count):
            out_ref[j, pl.ds(g * SUB, SUB)] = value[j * SUB : (j + 1) * SUB]
        return total

    tops, totals = [], []
    ready = score(0)
    for g in range(groups):
        later = score(g + 1) if g + 1 < groups else None
        tops.append(ready[0])
        totals.append(weigh(g, *ready))
        ready = later
    spare = jnp.zeros((SUB - 2 * groups, LANES), jnp.float32)
    stats = jnp.concatenate(tops + totals + [spare], axis=0)
    for j in range(count):
        turn = (LANES - SUB * j) % LANES
        out_ref[j, pl.ds(groups * SUB, SUB)] = pltpu.roll(stats, turn, 1) if turn else stats


def merge_kernel(parts_ref, out_ref):
    count, rows, head_dim = parts_ref.shape
    groups = rows // SUB - 1
    stats = parts_ref[:, groups * SUB :]
    top = stats[0]
    for j in range(1, count):
        top = jnp.maximum(top, stats[j])
    factors = [jnp.exp(stats[j] - top) for j in range(count)]
    denominator = factors[0] * pltpu.roll(stats[0], SUB - groups, 0)
    for j in range(1, count):
        denominator = denominator + factors[j] * pltpu.roll(stats[j], SUB - groups, 0)
    shares = jnp.concatenate([factor / denominator for factor in factors], axis=0).T[:SUB]
    merged = []
    for g in range(groups):
        total = jnp.zeros((SUB, head_dim), jnp.float32)
        for j in range(count):
            column = j * SUB + g
            total = total + parts_ref[j, pl.ds(g * SUB, SUB)] * shares[:, column : column + 1]
        merged.append(total)
    merged = jnp.concatenate(merged, axis=1).astype(jnp.bfloat16)
    for j in range(out_ref.shape[0]):
        out_ref[j] = merged


def output_kernel(attention_ref, w_ref, out_ref, held):
    count, heads, width = attention_ref.shape
    groups, _, head_dim = held.shape
    for g in range(groups):
        part = attention_ref[:, :, g * head_dim : (g + 1) * head_dim]
        held[g] = part.astype(jnp.float32).reshape(count * heads, head_dim)
    left = jnp.concatenate(
        [
            jnp.concatenate(
                [
                    held[g, pl.ds(step * heads + i, count // 2, stride=2 * heads)]
                    for i in range(heads)
                ],
                axis=1,
            )
            for step in range(2)
            for g in range(groups)
        ],
        axis=0,
    )
    out_ref[...] = jnp.dot(left.astype(jnp.bfloat16), w_ref[...], preferred_element_type=jnp.float32)


def double(array, axis_name, mask, size):
    pairs = [(i, i ^ mask) for i in range(size)]
    return array + lax.ppermute(array, axis_name, pairs)


def body(token_ids, lengths, embedding, norm_gain, w_qkv, k_cache, v_cache, w_out):
    n_seq, n_head = lax.axis_size("seq"), lax.axis_size("head")
    feat = embedding.shape[1]
    row_count, _, cache_dev, head_dim = k_cache.shape
    tokens = 2 * row_count
    own = tokens // n_seq
    width = w_qkv.shape[2]

    picked, rope, limits, w_near = pl.pallas_call(
        functools.partial(pick_kernel, cache_dev),
        out_shape=[
            jax.ShapeDtypeStruct((tokens, feat), jnp.bfloat16),
            jax.ShapeDtypeStruct((2 * BLOCK, LANES), jnp.float32),
            jax.ShapeDtypeStruct((SUB, LANES), jnp.int32),
            pltpu.VMEM((feat, width), jnp.bfloat16),
        ],
        in_specs=[SMEM, SMEM, VMEM, ANY, ANY],
        out_specs=[VMEM] * 4,
        scratch_shapes=[
            pltpu.VMEM((tokens * TILE, feat), jnp.bfloat16),
            pltpu.SemaphoreType.DMA,
            pltpu.SemaphoreType.DMA,
        ],
        compiler_params=pltpu.CompilerParams(vmem_limit_bytes=8 << 20),
        name="pick",
    )(
        in_hbm(token_ids),
        in_hbm(lengths),
        rope_frequency(head_dim),
        in_hbm(embedding),
        in_hbm(w_qkv.reshape(feat, width)),
    )
    for mask in (1, 2, 6):
        picked = double(picked, "head", mask, n_head)
    gain = norm_gain.astype(jnp.float32).reshape(1, feat)

    partial = call(
        project_kernel, "project", ((n_seq * BLOCK, head_dim), jnp.float32), [VMEM] * 3
    )(picked, gain, in_vmem(w_near))
    partial = swap(partial.reshape(n_seq, BLOCK, head_dim), "seq")
    rows = call(finish_kernel, "finish", ((n_seq, BLOCK, head_dim), jnp.bfloat16), [VMEM] * 2)(
        partial, rope
    )
    rows = swap(rows, "seq")

    partial = call(
        attend_kernel,
        "attend",
        ((n_seq, BLOCK, head_dim), jnp.float32),
        [VMEM] * 4,
        [pltpu.VMEM((own, cache_dev, LANES), jnp.float32)],
        8,
    )(limits, rows, in_vmem(k_cache[:, 0]), in_vmem(v_cache[:, 0]))
    partial = swap(partial, "seq")
    attention = call(merge_kernel, "merge", ((n_seq, SUB, own * head_dim), jnp.bfloat16), [VMEM])(
        partial
    )
    attention = swap(attention, "seq")

    terms = call(
        output_kernel,
        "output",
        ((tokens, w_out.shape[2]), jnp.float32),
        [VMEM] * 2,
        [pltpu.VMEM((own, n_seq * SUB, head_dim), jnp.float32)],
    )(attention, in_vmem(w_out[0]))
    for mask in (2, 6, 1):
        terms = double(terms, "head", mask, n_head)
    return terms.astype(jnp.bfloat16).reshape(2, row_count, -1)


def solution(mesh):
    return jax.shard_map(
        body,
        mesh=mesh,
        in_specs=(
            P(),
            P(),
            P("head", "seq"),
            P("seq"),
            P("seq", "head", None),
            P(None, "head", "seq", None),
            P(None, "head", "seq", None),
            P("head", None, "seq"),
        ),
        out_specs=P(None, None, "seq"),
        check_vma=False,
    )
```

```python
import functools

import jax
import jax.numpy as jnp
from jax import lax
from jax.experimental import pallas as pl
from jax.experimental.pallas import tpu as pltpu
from jax.sharding import PartitionSpec as P

D = 8192
TILE = 16
LANES = 128
SUB = 8
BLOCK = 32
SPAN = 32

rope_base = 500000.0
epsilon = 1e-05
negative = -1e30

VMEM = pl.BlockSpec(memory_space=pltpu.VMEM)
SMEM = pl.BlockSpec(memory_space=pltpu.SMEM)
ANY = pl.BlockSpec(memory_space=pl.ANY)


def in_vmem(array):
    return pltpu.with_memory_space_constraint(array, pltpu.VMEM)


def in_hbm(array):
    return pltpu.with_memory_space_constraint(array, pltpu.HBM)


def call(kernel, name, out, in_specs, scratch=(), limit=4):
    return pl.pallas_call(
        kernel,
        out_shape=jax.ShapeDtypeStruct(*out),
        in_specs=in_specs,
        out_specs=VMEM,
        scratch_shapes=list(scratch),
        compiler_params=pltpu.CompilerParams(vmem_limit_bytes=limit << 20),
        name=name,
    )


def swap(array, axis_name):
    return lax.all_to_all(array, axis_name, 0, 0, tiled=True)


def rope_frequency(head_dim):
    exponent = jnp.arange(head_dim // 2, dtype=jnp.float32) * (2.0 / head_dim)
    frequency = jnp.power(jnp.float32(rope_base), -exponent)
    return jnp.concatenate([frequency, frequency])[None, :]


def cos_sin(angles):
    turn = jnp.floor(angles * 0.6366197723675814 + 0.5)
    rest = ((angles - turn * 1.5703125) - turn * 0.00048351287841796875) - turn * 3.13916478589249e-07
    square = rest * rest
    sine = ((-1.9515295891e-4 * square + 8.3321608736e-3) * square - 1.6666654611e-1) * square
    sine = sine * rest + rest
    cosine = (2.443315711809948e-5 * square - 1.388731625493765e-3) * square
    cosine = (cosine + 4.166664568298827e-2) * square * square - 0.5 * square + 1.0
    quarter = turn.astype(jnp.int32) & 3
    odd = (quarter & 1) == 1
    first, second = jnp.where(odd, sine, cosine), jnp.where(odd, cosine, sine)
    return (
        jnp.where((quarter == 1) | (quarter == 2), -first, first),
        jnp.where(quarter >= 2, -second, second),
    )


def pick_kernel(
    cache_dev, ids_ref, lengths_ref, frequency_ref, table_ref, far_w_ref,
    x_ref, rope_ref, limits_ref, w_ref, held, sem, w_sem,
):
    vocab_dev, feat = table_ref.shape
    steps, rows = ids_ref.shape
    tokens = steps * rows
    first = lax.axis_index("head") * vocab_dev
    held[...] = jnp.zeros_like(held)
    places = []
    found = 0
    for i in range(tokens):
        local = ids_ref[i // rows, i % rows] - first
        inside = (local >= 0) & (local < vocab_dev)
        local = jnp.clip(local, 0, vocab_dev - 1)
        within = local & (TILE - 1)

        @pl.when(inside)
        def _(start=local - within, i=i):
            pltpu.make_async_copy(
                table_ref.at[pl.ds(pl.multiple_of(start, TILE), TILE)],
                held.at[pl.ds(i * TILE, TILE)],
                sem,
            ).start()

        found = found + inside.astype(jnp.int32)
        places.append(jnp.where(inside, i * TILE + within, -1))
    w_copy = pltpu.make_async_copy(far_w_ref, w_ref, w_sem)
    w_copy.start()

    me = lax.axis_index("seq")
    near = LANES // (2 * SUB)
    sub = lax.broadcasted_iota(jnp.int32, (SUB, LANES), 0)
    lane = lax.broadcasted_iota(jnp.int32, (SUB, LANES), 1)
    own = rows // near
    block = rope_ref.shape[0] // 2
    line = lax.broadcasted_iota(jnp.int32, (block, LANES), 0)
    position = jnp.zeros((block, LANES), jnp.int32)
    limits = jnp.zeros((SUB, LANES), jnp.int32)
    for g in range(own):
        here = (line // SUB == g) | (line == own * SUB + g)
        position = jnp.where(here, lengths_ref[g * near + me // 2] + me % 2, position)
        for r in range(near):
            here = (sub == g) & (lane // (2 * SUB) == r)
            limits = jnp.where(here, lengths_ref[g * near + r], limits)
    limits_ref[...] = limits - me * cache_dev
    cosine, sine = cos_sin(position.astype(jnp.float32) * frequency_ref[...])
    turned = line < own * SUB + own
    first_half = lax.broadcasted_iota(jnp.int32, (block, LANES), 1) < LANES // 2
    rope_ref[:block] = jnp.where(turned, cosine, 1.0)
    rope_ref[block:] = jnp.where(turned, jnp.where(first_half, -sine, sine), 0.0)

    row = lax.broadcasted_iota(jnp.int32, (tokens, 1), 0)
    choice = jnp.full((tokens, 1), -1, jnp.int32)
    for i in range(tokens):
        step, r = i // rows, i % rows
        choice = jnp.where(row == r // near * 2 * near + r % near * 2 + step, places[i], choice)
    column = lax.broadcasted_iota(jnp.int32, (tokens, tokens * TILE), 1)
    select = jnp.where(column == choice, 1.0, 0.0).astype(jnp.bfloat16)
    def wait(i, carry):
        pltpu.make_async_copy(table_ref.at[pl.ds(0, TILE)], held.at[pl.ds(0, TILE)], sem).wait()
        return carry

    lax.fori_loop(0, found, wait, 0)
    picked = jnp.dot(select, held[...], preferred_element_type=jnp.float32)
    x_ref[...] = picked.astype(jnp.bfloat16)
    w_copy.wait()


def project_kernel(x_ref, gain_ref, w_ref, out_ref):
    tokens = x_ref.shape[0]
    count = out_ref.shape[0] // BLOCK
    own = tokens // count
    x = x_ref[...].astype(jnp.float32)
    squares = jnp.sum(x * x, axis=1, keepdims=True)
    scaled = (x * gain_ref[...]).astype(jnp.bfloat16)
    partial = jnp.dot(scaled, w_ref[...], preferred_element_type=jnp.float32)
    lane = lax.broadcasted_iota(jnp.int32, (count, LANES), 1)
    last = jnp.zeros((count, LANES), jnp.float32)
    for k in range(own):
        part = slice(k * count, (k + 1) * count)
        for b in range(SUB + 2):
            line = k * SUB + b if b < SUB else (own * (b - SUB) + own * SUB + k)
            out_ref[pl.ds(line, count, stride=BLOCK)] = partial[part, b * LANES : (b + 1) * LANES]
        last = jnp.where(lane // SPAN == k, squares[part], last)
    out_ref[pl.ds(BLOCK - 2, count, stride=BLOCK)] = last
    out_ref[pl.ds(BLOCK - 1, count, stride=BLOCK)] = jnp.zeros((count, LANES), jnp.float32)


def finish_kernel(parts_ref, rope_ref, out_ref):
    count, block, head_dim = parts_ref.shape
    own = block // SUB - 1
    summed = parts_ref[0]
    for j in range(1, count):
        summed = summed + parts_ref[j]
    inverse = lax.rsqrt(summed[block - 2 : block - 1] / D + epsilon)
    line = lax.broadcasted_iota(jnp.int32, (block, head_dim), 0)
    scale = jnp.zeros((block, head_dim), jnp.float32)
    for k in range(own):
        here = (line // SUB == k) | (line == own * SUB + k) | (line == own * SUB + own + k)
        here = here & ((line < own * SUB) | (line % SUB < 2 * own))
        scale = jnp.where(here, inverse[:, k * SPAN : k * SPAN + 1], scale)
    normed = summed * scale
    turned = normed * rope_ref[:block] + pltpu.roll(normed, head_dim // 2, 1) * rope_ref[block:]
    turned = jnp.where(line < own * SUB, turned * head_dim ** (-0.5), turned).astype(jnp.bfloat16)
    for j in range(out_ref.shape[0]):
        out_ref[j] = turned


def attend_kernel(limits_ref, rows_ref, k_ref, v_ref, out_ref, scores_ref):
    row_count, cache_dev, head_dim = k_ref.shape
    count = rows_ref.shape[0]
    per_row = 2 * SUB
    near = LANES // per_row
    groups = row_count // near
    chunk = 256
    me = lax.axis_index("seq")
    lane = lax.broadcasted_iota(jnp.int32, (1, LANES), 1)
    position = lax.broadcasted_iota(jnp.int32, (chunk, LANES), 0)
    slot = lax.broadcasted_iota(jnp.int32, (LANES, LANES), 0)
    rows = rows_ref[...].astype(jnp.float32)
    new_keys = rows[:, groups * SUB :].reshape(count * SUB, head_dim)
    new_values = pltpu.roll(new_keys, LANES - groups, 0).astype(jnp.bfloat16)
    new_keys = new_keys.astype(jnp.bfloat16)

    def score(g):
        turned = rows[:, g * SUB : (g + 1) * SUB].reshape(count * SUB, head_dim).T
        blocks = [
            jnp.where(lane // per_row == r, turned, 0.0).astype(jnp.bfloat16) for r in range(near)
        ]
        weights = jnp.concatenate(blocks, axis=0)
        limit = limits_ref[g : g + 1]
        fresh = jnp.dot(new_keys, turned.astype(jnp.bfloat16), preferred_element_type=jnp.float32)
        seen = (
            (slot % SUB == g)
            & (slot // per_row == lane // per_row)
            & (slot // SUB <= lane // SUB)
            & (me == 0)
        )
        fresh = jnp.where(seen, fresh, negative)
        top = jnp.max(fresh, axis=0, keepdims=True)
        for c in range(cache_dev // chunk):
            keys = jnp.concatenate(
                [k_ref[g * near + r, pl.ds(c * chunk, chunk)] for r in range(near)], axis=1
            )
            scores = jnp.dot(keys, weights, preferred_element_type=jnp.float32)
            scores = jnp.where(position < limit - c * chunk, scores, negative)
            scores_ref[g, pl.ds(c * chunk, chunk)] = scores
            top = jnp.maximum(top, jnp.max(scores, axis=0, keepdims=True))
        return top, fresh

    def weigh(g, top, fresh):
        fresh = jnp.exp(fresh - top)
        total = jnp.sum(fresh, axis=0, keepdims=True)
        parts = []
        for c in range(cache_dev // chunk):
            weight = jnp.exp(scores_ref[g, pl.ds(c * chunk, chunk)] - top)
            total = total + jnp.sum(weight, axis=0, keepdims=True)
            parts.append(weight.astype(jnp.bfloat16).T)
        parts = jnp.concatenate(parts, axis=1)
        value = jnp.concatenate(
            [
                jnp.dot(
                    parts[r * per_row : (r + 1) * per_row],
                    v_ref[g * near + r],
                    preferred_element_type=jnp.float32,
                )
                for r in range(near)
            ],
            axis=0,
        ) + jnp.dot(fresh.T.astype(jnp.bfloat16), new_values, preferred_element_type=jnp.float32)
        for j in range(count):
            out_ref[j, pl.ds(g * SUB, SUB)] = value[j * SUB : (j + 1) * SUB]
        return total

    tops, totals = [], []
    ready = score(0)
    for g in range(groups):
        later = score(g + 1) if g + 1 < groups else None
        tops.append(ready[0])
        totals.append(weigh(g, *ready))
        ready = later
    spare = jnp.zeros((SUB - 2 * groups, LANES), jnp.float32)
    stats = jnp.concatenate(tops + totals + [spare], axis=0)
    for j in range(count):
        turn = (LANES - SUB * j) % LANES
        out_ref[j, pl.ds(groups * SUB, SUB)] = pltpu.roll(stats, turn, 1) if turn else stats


def merge_kernel(parts_ref, out_ref):
    count, rows, head_dim = parts_ref.shape
    groups = rows // SUB - 1
    stats = parts_ref[:, groups * SUB :]
    top = stats[0]
    for j in range(1, count):
        top = jnp.maximum(top, stats[j])
    factors = [jnp.exp(stats[j] - top) for j in range(count)]
    denominator = factors[0] * pltpu.roll(stats[0], SUB - groups, 0)
    for j in range(1, count):
        denominator = denominator + factors[j] * pltpu.roll(stats[j], SUB - groups, 0)
    shares = jnp.concatenate([factor / denominator for factor in factors], axis=0).T[:SUB]
    merged = []
    for g in range(groups):
        total = jnp.zeros((SUB, head_dim), jnp.float32)
        for j in range(count):
            column = j * SUB + g
            total = total + parts_ref[j, pl.ds(g * SUB, SUB)] * shares[:, column : column + 1]
        merged.append(total)
    merged = jnp.concatenate(merged, axis=1).astype(jnp.bfloat16)
    for j in range(out_ref.shape[0]):
        out_ref[j] = merged


def output_kernel(attention_ref, w_ref, out_ref, held):
    count, heads, width = attention_ref.shape
    groups, _, head_dim = held.shape
    for g in range(groups):
        part = attention_ref[:, :, g * head_dim : (g + 1) * head_dim]
        held[g] = part.astype(jnp.float32).reshape(count * heads, head_dim)
    left = jnp.concatenate(
        [
            jnp.concatenate(
                [
                    held[g, pl.ds(step * heads + i, count // 2, stride=2 * heads)]
                    for i in range(heads)
                ],
                axis=1,
            )
            for step in range(2)
            for g in range(groups)
        ],
        axis=0,
    )
    out_ref[...] = jnp.dot(left.astype(jnp.bfloat16), w_ref[...], preferred_element_type=jnp.float32)


def double(array, axis_name, mask, size):
    pairs = [(i, i ^ mask) for i in range(size)]
    return array + lax.ppermute(array, axis_name, pairs)


def body(token_ids, lengths, embedding, norm_gain, w_qkv, k_cache, v_cache, w_out):
    n_seq, n_head = lax.axis_size("seq"), lax.axis_size("head")
    feat = embedding.shape[1]
    row_count, _, cache_dev, head_dim = k_cache.shape
    tokens = 2 * row_count
    own = tokens // n_seq
    width = w_qkv.shape[2]

    picked, rope, limits, w_near = pl.pallas_call(
        functools.partial(pick_kernel, cache_dev),
        out_shape=[
            jax.ShapeDtypeStruct((tokens, feat), jnp.bfloat16),
            jax.ShapeDtypeStruct((2 * BLOCK, LANES), jnp.float32),
            jax.ShapeDtypeStruct((SUB, LANES), jnp.int32),
            pltpu.VMEM((feat, width), jnp.bfloat16),
        ],
        in_specs=[SMEM, SMEM, VMEM, ANY, ANY],
        out_specs=[VMEM] * 4,
        scratch_shapes=[
            pltpu.VMEM((tokens * TILE, feat), jnp.bfloat16),
            pltpu.SemaphoreType.DMA,
            pltpu.SemaphoreType.DMA,
        ],
        compiler_params=pltpu.CompilerParams(vmem_limit_bytes=8 << 20),
        name="pick",
    )(
        in_hbm(token_ids),
        in_hbm(lengths),
        rope_frequency(head_dim),
        in_hbm(embedding),
        in_hbm(w_qkv.reshape(feat, width)),
    )
    for mask in (1, 2, 6):
        picked = double(picked, "head", mask, n_head)
    gain = norm_gain.astype(jnp.float32).reshape(1, feat)

    partial = call(
        project_kernel, "project", ((n_seq * BLOCK, head_dim), jnp.float32), [VMEM] * 3
    )(picked, gain, in_vmem(w_near))
    partial = swap(partial.reshape(n_seq, BLOCK, head_dim), "seq")
    rows = call(finish_kernel, "finish", ((n_seq, BLOCK, head_dim), jnp.bfloat16), [VMEM] * 2)(
        partial, rope
    )
    rows = swap(rows, "seq")

    partial = call(
        attend_kernel,
        "attend",
        ((n_seq, BLOCK, head_dim), jnp.float32),
        [VMEM] * 4,
        [pltpu.VMEM((own, cache_dev, LANES), jnp.float32)],
        8,
    )(limits, rows, in_vmem(k_cache[:, 0]), in_vmem(v_cache[:, 0]))
    partial = swap(partial, "seq")
    attention = call(merge_kernel, "merge", ((n_seq, SUB, own * head_dim), jnp.bfloat16), [VMEM])(
        partial
    )
    attention = swap(attention, "seq")

    terms = call(
        output_kernel,
        "output",
        ((tokens, w_out.shape[2]), jnp.float32),
        [VMEM] * 2,
        [pltpu.VMEM((own, n_seq * SUB, head_dim), jnp.float32)],
    )(attention, in_vmem(w_out[0]))
    for mask in (2, 6, 1):
        terms = double(terms, "head", mask, n_head)
    return terms.astype(jnp.bfloat16).reshape(2, row_count, -1)


def solution(mesh):
    return jax.shard_map(
        body,
        mesh=mesh,
        in_specs=(
            P(),
            P(),
            P("head", "seq"),
            P("seq"),
            P("seq", "head", None),
            P(None, "head", "seq", None),
            P(None, "head", "seq", None),
            P("head", None, "seq"),
        ),
        out_specs=P(None, None, "seq"),
        check_vma=False,
    )
```

```python
import functools

import jax
import jax.numpy as jnp
from jax import lax
from jax.experimental import pallas as pl
from jax.experimental.pallas import tpu as pltpu
from jax.sharding import PartitionSpec as P

D = 8192
TILE = 16
LANES = 128
SUB = 8
BLOCK = 32
SPAN = 32

rope_base = 500000.0
epsilon = 1e-05
negative = -1e30

VMEM = pl.BlockSpec(memory_space=pltpu.VMEM)
SMEM = pl.BlockSpec(memory_space=pltpu.SMEM)
ANY = pl.BlockSpec(memory_space=pl.ANY)


def in_vmem(array):
    return pltpu.with_memory_space_constraint(array, pltpu.VMEM)


def in_hbm(array):
    return pltpu.with_memory_space_constraint(array, pltpu.HBM)


def call(kernel, name, out, in_specs, scratch=(), limit=4):
    return pl.pallas_call(
        kernel,
        out_shape=jax.ShapeDtypeStruct(*out),
        in_specs=in_specs,
        out_specs=VMEM,
        scratch_shapes=list(scratch),
        compiler_params=pltpu.CompilerParams(vmem_limit_bytes=limit << 20),
        name=name,
    )


def swap(array, axis_name):
    return lax.all_to_all(array, axis_name, 0, 0, tiled=True)


def rope_frequency(head_dim):
    exponent = jnp.arange(head_dim // 2, dtype=jnp.float32) * (2.0 / head_dim)
    frequency = jnp.power(jnp.float32(rope_base), -exponent)
    return jnp.concatenate([frequency, frequency])[None, :]


def cos_sin(angles):
    turn = jnp.floor(angles * 0.6366197723675814 + 0.5)
    rest = ((angles - turn * 1.5703125) - turn * 0.00048351287841796875) - turn * 3.13916478589249e-07
    square = rest * rest
    sine = ((-1.9515295891e-4 * square + 8.3321608736e-3) * square - 1.6666654611e-1) * square
    sine = sine * rest + rest
    cosine = (2.443315711809948e-5 * square - 1.388731625493765e-3) * square
    cosine = (cosine + 4.166664568298827e-2) * square * square - 0.5 * square + 1.0
    quarter = turn.astype(jnp.int32) & 3
    odd = (quarter & 1) == 1
    first, second = jnp.where(odd, sine, cosine), jnp.where(odd, cosine, sine)
    return (
        jnp.where((quarter == 1) | (quarter == 2), -first, first),
        jnp.where(quarter >= 2, -second, second),
    )


def pick_kernel(
    cache_dev, ids_ref, lengths_ref, frequency_ref, table_ref, far_w_ref,
    x_ref, rope_ref, limits_ref, w_ref, held, sem, w_sem,
):
    vocab_dev, feat = table_ref.shape
    steps, rows = ids_ref.shape
    tokens = steps * rows
    first = lax.axis_index("head") * vocab_dev
    held[...] = jnp.zeros_like(held)
    places = []
    found = 0
    for i in range(tokens):
        local = ids_ref[i // rows, i % rows] - first
        inside = (local >= 0) & (local < vocab_dev)
        local = jnp.clip(local, 0, vocab_dev - 1)
        within = local & (TILE - 1)

        @pl.when(inside)
        def _(start=local - within, i=i):
            pltpu.make_async_copy(
                table_ref.at[pl.ds(pl.multiple_of(start, TILE), TILE)],
                held.at[pl.ds(i * TILE, TILE)],
                sem,
            ).start(priority=1)

        found = found + inside.astype(jnp.int32)
        places.append(jnp.where(inside, i * TILE + within, -1))
    w_copy = pltpu.make_async_copy(far_w_ref, w_ref, w_sem)
    w_copy.start(priority=1)

    me = lax.axis_index("seq")
    near = LANES // (2 * SUB)
    sub = lax.broadcasted_iota(jnp.int32, (SUB, LANES), 0)
    lane = lax.broadcasted_iota(jnp.int32, (SUB, LANES), 1)
    own = rows // near
    block = rope_ref.shape[0] // 2
    line = lax.broadcasted_iota(jnp.int32, (block, LANES), 0)
    position = jnp.zeros((block, LANES), jnp.int32)
    limits = jnp.zeros((SUB, LANES), jnp.int32)
    for g in range(own):
        here = (line // SUB == g) | (line == own * SUB + g)
        position = jnp.where(here, lengths_ref[g * near + me // 2] + me % 2, position)
        for r in range(near):
            here = (sub == g) & (lane // (2 * SUB) == r)
            limits = jnp.where(here, lengths_ref[g * near + r], limits)
    limits_ref[...] = limits - me * cache_dev
    cosine, sine = cos_sin(position.astype(jnp.float32) * frequency_ref[...])
    turned = line < own * SUB + own
    first_half = lax.broadcasted_iota(jnp.int32, (block, LANES), 1) < LANES // 2
    rope_ref[:block] = jnp.where(turned, cosine, 1.0)
    rope_ref[block:] = jnp.where(turned, jnp.where(first_half, -sine, sine), 0.0)

    row = lax.broadcasted_iota(jnp.int32, (tokens, 1), 0)
    choice = jnp.full((tokens, 1), -1, jnp.int32)
    for i in range(tokens):
        step, r = i // rows, i % rows
        choice = jnp.where(row == r // near * 2 * near + r % near * 2 + step, places[i], choice)
    column = lax.broadcasted_iota(jnp.int32, (tokens, tokens * TILE), 1)
    select = jnp.where(column == choice, 1.0, 0.0).astype(jnp.bfloat16)
    def wait(i, carry):
        pltpu.make_async_copy(table_ref.at[pl.ds(0, TILE)], held.at[pl.ds(0, TILE)], sem).wait()
        return carry

    lax.fori_loop(0, found, wait, 0)
    picked = jnp.dot(select, held[...], preferred_element_type=jnp.float32)
    x_ref[...] = picked.astype(jnp.bfloat16)
    w_copy.wait()


def project_kernel(x_ref, gain_ref, w_ref, out_ref):
    tokens = x_ref.shape[0]
    count = out_ref.shape[0] // BLOCK
    own = tokens // count
    x = x_ref[...].astype(jnp.float32)
    squares = jnp.sum(x * x, axis=1, keepdims=True)
    scaled = (x * gain_ref[...]).astype(jnp.bfloat16)
    partial = jnp.dot(scaled, w_ref[...], preferred_element_type=jnp.float32)
    lane = lax.broadcasted_iota(jnp.int32, (count, LANES), 1)
    last = jnp.zeros((count, LANES), jnp.float32)
    for k in range(own):
        part = slice(k * count, (k + 1) * count)
        for b in range(SUB + 2):
            line = k * SUB + b if b < SUB else (own * (b - SUB) + own * SUB + k)
            out_ref[pl.ds(line, count, stride=BLOCK)] = partial[part, b * LANES : (b + 1) * LANES]
        last = jnp.where(lane // SPAN == k, squares[part], last)
    out_ref[pl.ds(BLOCK - 2, count, stride=BLOCK)] = last
    out_ref[pl.ds(BLOCK - 1, count, stride=BLOCK)] = jnp.zeros((count, LANES), jnp.float32)


def finish_kernel(parts_ref, rope_ref, out_ref):
    count, block, head_dim = parts_ref.shape
    own = block // SUB - 1
    summed = parts_ref[0]
    for j in range(1, count):
        summed = summed + parts_ref[j]
    inverse = lax.rsqrt(summed[block - 2 : block - 1] / D + epsilon)
    line = lax.broadcasted_iota(jnp.int32, (block, head_dim), 0)
    scale = jnp.zeros((block, head_dim), jnp.float32)
    for k in range(own):
        here = (line // SUB == k) | (line == own * SUB + k) | (line == own * SUB + own + k)
        here = here & ((line < own * SUB) | (line % SUB < 2 * own))
        scale = jnp.where(here, inverse[:, k * SPAN : k * SPAN + 1], scale)
    normed = summed * scale
    turned = normed * rope_ref[:block] + pltpu.roll(normed, head_dim // 2, 1) * rope_ref[block:]
    turned = jnp.where(line < own * SUB, turned * head_dim ** (-0.5), turned).astype(jnp.bfloat16)
    for j in range(out_ref.shape[0]):
        out_ref[j] = turned


def attend_kernel(limits_ref, rows_ref, k_ref, v_ref, out_ref, scores_ref):
    row_count, cache_dev, head_dim = k_ref.shape
    count = rows_ref.shape[0]
    per_row = 2 * SUB
    near = LANES // per_row
    groups = row_count // near
    chunk = 512
    me = lax.axis_index("seq")
    lane = lax.broadcasted_iota(jnp.int32, (1, LANES), 1)
    position = lax.broadcasted_iota(jnp.int32, (chunk, LANES), 0)
    slot = lax.broadcasted_iota(jnp.int32, (LANES, LANES), 0)
    rows = rows_ref[...].astype(jnp.float32)
    new_keys = rows[:, groups * SUB :].reshape(count * SUB, head_dim)
    new_values = pltpu.roll(new_keys, LANES - groups, 0).astype(jnp.bfloat16)
    new_keys = new_keys.astype(jnp.bfloat16)

    def score(g):
        turned = rows[:, g * SUB : (g + 1) * SUB].reshape(count * SUB, head_dim).T
        blocks = [
            jnp.where(lane // per_row == r, turned, 0.0).astype(jnp.bfloat16) for r in range(near)
        ]
        weights = jnp.concatenate(blocks, axis=0)
        limit = limits_ref[g : g + 1]
        fresh = jnp.dot(new_keys, turned.astype(jnp.bfloat16), preferred_element_type=jnp.float32)
        seen = (
            (slot % SUB == g)
            & (slot // per_row == lane // per_row)
            & (slot // SUB <= lane // SUB)
            & (me == 0)
        )
        fresh = jnp.where(seen, fresh, negative)
        top = jnp.max(fresh, axis=0, keepdims=True)
        for c in range(cache_dev // chunk):
            keys = jnp.concatenate(
                [k_ref[g * near + r, pl.ds(c * chunk, chunk)] for r in range(near)], axis=1
            )
            scores = jnp.dot(keys, weights, preferred_element_type=jnp.float32)
            scores = jnp.where(position < limit - c * chunk, scores, negative)
            scores_ref[g, pl.ds(c * chunk, chunk)] = scores
            top = jnp.maximum(top, jnp.max(scores, axis=0, keepdims=True))
        return top, fresh

    def weigh(g, top, fresh):
        fresh = jnp.exp(fresh - top)
        total = jnp.sum(fresh, axis=0, keepdims=True)
        parts = []
        for c in range(cache_dev // chunk):
            weight = jnp.exp(scores_ref[g, pl.ds(c * chunk, chunk)] - top)
            total = total + jnp.sum(weight, axis=0, keepdims=True)
            parts.append(weight.astype(jnp.bfloat16).T)
        parts = jnp.concatenate(parts, axis=1)
        value = jnp.concatenate(
            [
                jnp.dot(
                    parts[r * per_row : (r + 1) * per_row],
                    v_ref[g * near + r],
                    preferred_element_type=jnp.float32,
                )
                for r in range(near)
            ],
            axis=0,
        ) + jnp.dot(fresh.T.astype(jnp.bfloat16), new_values, preferred_element_type=jnp.float32)
        for j in range(count):
            out_ref[j, pl.ds(g * SUB, SUB)] = value[j * SUB : (j + 1) * SUB]
        return total

    tops, totals = [], []
    ready = score(0)
    for g in range(groups):
        later = score(g + 1) if g + 1 < groups else None
        tops.append(ready[0])
        totals.append(weigh(g, *ready))
        ready = later
    spare = jnp.zeros((SUB - 2 * groups, LANES), jnp.float32)
    stats = jnp.concatenate(tops + totals + [spare], axis=0)
    for j in range(count):
        turn = (LANES - SUB * j) % LANES
        out_ref[j, pl.ds(groups * SUB, SUB)] = pltpu.roll(stats, turn, 1) if turn else stats


def merge_kernel(parts_ref, out_ref):
    count, rows, head_dim = parts_ref.shape
    groups = rows // SUB - 1
    stats = parts_ref[:, groups * SUB :]
    top = stats[0]
    for j in range(1, count):
        top = jnp.maximum(top, stats[j])
    factors = [jnp.exp(stats[j] - top) for j in range(count)]
    denominator = factors[0] * pltpu.roll(stats[0], SUB - groups, 0)
    for j in range(1, count):
        denominator = denominator + factors[j] * pltpu.roll(stats[j], SUB - groups, 0)
    shares = jnp.concatenate([factor / denominator for factor in factors], axis=0).T[:SUB]
    merged = []
    for g in range(groups):
        total = jnp.zeros((SUB, head_dim), jnp.float32)
        for j in range(count):
            column = j * SUB + g
            total = total + parts_ref[j, pl.ds(g * SUB, SUB)] * shares[:, column : column + 1]
        merged.append(total)
    merged = jnp.concatenate(merged, axis=1).astype(jnp.bfloat16)
    for j in range(out_ref.shape[0]):
        out_ref[j] = merged


def output_kernel(attention_ref, w_ref, out_ref, held):
    count, heads, width = attention_ref.shape
    groups, _, head_dim = held.shape
    for g in range(groups):
        part = attention_ref[:, :, g * head_dim : (g + 1) * head_dim]
        held[g] = part.astype(jnp.float32).reshape(count * heads, head_dim)
    left = jnp.concatenate(
        [
            jnp.concatenate(
                [
                    held[g, pl.ds(step * heads + i, count // 2, stride=2 * heads)]
                    for i in range(heads)
                ],
                axis=1,
            )
            for step in range(2)
            for g in range(groups)
        ],
        axis=0,
    )
    out_ref[...] = jnp.dot(left.astype(jnp.bfloat16), w_ref[...], preferred_element_type=jnp.float32)


def double(array, axis_name, mask, size):
    pairs = [(i, i ^ mask) for i in range(size)]
    return array + lax.ppermute(array, axis_name, pairs)


def body(token_ids, lengths, embedding, norm_gain, w_qkv, k_cache, v_cache, w_out):
    n_seq, n_head = lax.axis_size("seq"), lax.axis_size("head")
    feat = embedding.shape[1]
    row_count, _, cache_dev, head_dim = k_cache.shape
    tokens = 2 * row_count
    own = tokens // n_seq
    width = w_qkv.shape[2]

    picked, rope, limits, w_near = pl.pallas_call(
        functools.partial(pick_kernel, cache_dev),
        out_shape=[
            jax.ShapeDtypeStruct((tokens, feat), jnp.bfloat16),
            jax.ShapeDtypeStruct((2 * BLOCK, LANES), jnp.float32),
            jax.ShapeDtypeStruct((SUB, LANES), jnp.int32),
            pltpu.VMEM((feat, width), jnp.bfloat16),
        ],
        in_specs=[SMEM, SMEM, VMEM, ANY, ANY],
        out_specs=[VMEM] * 4,
        scratch_shapes=[
            pltpu.VMEM((tokens * TILE, feat), jnp.bfloat16),
            pltpu.SemaphoreType.DMA,
            pltpu.SemaphoreType.DMA,
        ],
        compiler_params=pltpu.CompilerParams(vmem_limit_bytes=8 << 20),
        name="pick",
    )(
        in_hbm(token_ids),
        in_hbm(lengths),
        rope_frequency(head_dim),
        in_hbm(embedding),
        in_hbm(w_qkv.reshape(feat, width)),
    )
    for mask in (1, 2, 6):
        picked = double(picked, "head", mask, n_head)
    gain = norm_gain.astype(jnp.float32).reshape(1, feat)

    partial = call(
        project_kernel, "project", ((n_seq * BLOCK, head_dim), jnp.float32), [VMEM] * 3
    )(picked, gain, in_vmem(w_near))
    partial = swap(partial.reshape(n_seq, BLOCK, head_dim), "seq")
    rows = call(finish_kernel, "finish", ((n_seq, BLOCK, head_dim), jnp.bfloat16), [VMEM] * 2)(
        partial, rope
    )
    rows = swap(rows, "seq")

    partial = call(
        attend_kernel,
        "attend",
        ((n_seq, BLOCK, head_dim), jnp.float32),
        [VMEM] * 4,
        [pltpu.VMEM((own, cache_dev, LANES), jnp.float32)],
        8,
    )(limits, rows, in_vmem(k_cache[:, 0]), in_vmem(v_cache[:, 0]))
    partial = swap(partial, "seq")
    attention = call(merge_kernel, "merge", ((n_seq, SUB, own * head_dim), jnp.bfloat16), [VMEM])(
        partial
    )
    attention = swap(attention, "seq")

    terms = call(
        output_kernel,
        "output",
        ((tokens, w_out.shape[2]), jnp.float32),
        [VMEM] * 2,
        [pltpu.VMEM((own, n_seq * SUB, head_dim), jnp.float32)],
    )(attention, in_vmem(w_out[0]))
    for mask in (2, 6, 1):
        terms = double(terms, "head", mask, n_head)
    return terms.astype(jnp.bfloat16).reshape(2, row_count, -1)


def solution(mesh):
    return jax.shard_map(
        body,
        mesh=mesh,
        in_specs=(
            P(),
            P(),
            P("head", "seq"),
            P("seq"),
            P("seq", "head", None),
            P(None, "head", "seq", None),
            P(None, "head", "seq", None),
            P("head", None, "seq"),
        ),
        out_specs=P(None, None, "seq"),
        check_vma=False,
    )
```

```python
import functools

import jax
import jax.numpy as jnp
from jax import lax
from jax.experimental import pallas as pl
from jax.experimental.pallas import tpu as pltpu
from jax.sharding import PartitionSpec as P

D = 8192
TILE = 16
LANES = 128
SUB = 8
BLOCK = 32
SPAN = 32
CORE, NEAR, FAR = 1, 2, 6

rope_base = 500000.0
epsilon = 1e-05
negative = -1e30

VMEM = pl.BlockSpec(memory_space=pltpu.VMEM)
SMEM = pl.BlockSpec(memory_space=pltpu.SMEM)
ANY = pl.BlockSpec(memory_space=pl.ANY)


def in_vmem(array):
    return pltpu.with_memory_space_constraint(array, pltpu.VMEM)


def in_hbm(array):
    return pltpu.with_memory_space_constraint(array, pltpu.HBM)


def call(kernel, name, out, in_specs, scratch=(), limit=4):
    return pl.pallas_call(
        kernel,
        out_shape=jax.ShapeDtypeStruct(*out),
        in_specs=in_specs,
        out_specs=VMEM,
        scratch_shapes=list(scratch),
        compiler_params=pltpu.CompilerParams(vmem_limit_bytes=limit << 20),
        name=name,
    )


def swap(array, axis_name):
    return lax.all_to_all(array, axis_name, 0, 0, tiled=True)


def rope_frequency(head_dim):
    exponent = jnp.arange(head_dim // 2, dtype=jnp.float32) * (2.0 / head_dim)
    frequency = jnp.power(jnp.float32(rope_base), -exponent)
    return jnp.concatenate([frequency, frequency])[None, :]


def cos_sin(angles):
    turn = jnp.floor(angles * 0.6366197723675814 + 0.5)
    rest = ((angles - turn * 1.5703125) - turn * 0.00048351287841796875) - turn * 3.13916478589249e-07
    square = rest * rest
    sine = ((-1.9515295891e-4 * square + 8.3321608736e-3) * square - 1.6666654611e-1) * square
    sine = sine * rest + rest
    cosine = (2.443315711809948e-5 * square - 1.388731625493765e-3) * square
    cosine = (cosine + 4.166664568298827e-2) * square * square - 0.5 * square + 1.0
    quarter = turn.astype(jnp.int32) & 3
    odd = (quarter & 1) == 1
    first, second = jnp.where(odd, sine, cosine), jnp.where(odd, cosine, sine)
    return (
        jnp.where((quarter == 1) | (quarter == 2), -first, first),
        jnp.where(quarter >= 2, -second, second),
    )


def pick_kernel(
    cache_dev, ids_ref, lengths_ref, frequency_ref, table_ref, far_w_ref,
    x_ref, rope_ref, limits_ref, w_ref, held, sem, w_sem,
):
    vocab_dev, feat = table_ref.shape
    steps, rows = ids_ref.shape
    tokens = steps * rows
    first = lax.axis_index("head") * vocab_dev
    held[...] = jnp.zeros_like(held)
    places = []
    found = 0
    for i in range(tokens):
        local = ids_ref[i // rows, i % rows] - first
        inside = (local >= 0) & (local < vocab_dev)
        local = jnp.clip(local, 0, vocab_dev - 1)
        within = local & (TILE - 1)

        @pl.when(inside)
        def _(start=local - within, i=i):
            pltpu.make_async_copy(
                table_ref.at[pl.ds(pl.multiple_of(start, TILE), TILE)],
                held.at[pl.ds(i * TILE, TILE)],
                sem,
            ).start(priority=1)

        found = found + inside.astype(jnp.int32)
        places.append(jnp.where(inside, i * TILE + within, -1))
    w_copy = pltpu.make_async_copy(far_w_ref, w_ref, w_sem)
    w_copy.start(priority=1)

    me = lax.axis_index("seq")
    near = LANES // (2 * SUB)
    sub = lax.broadcasted_iota(jnp.int32, (SUB, LANES), 0)
    lane = lax.broadcasted_iota(jnp.int32, (SUB, LANES), 1)
    own = rows // near
    block = rope_ref.shape[0] // 2
    line = lax.broadcasted_iota(jnp.int32, (block, LANES), 0)
    position = jnp.zeros((block, LANES), jnp.int32)
    limits = jnp.zeros((SUB, LANES), jnp.int32)
    for g in range(own):
        here = (line // SUB == g) | (line == own * SUB + g)
        position = jnp.where(here, lengths_ref[g * near + me // 2] + me % 2, position)
        for r in range(near):
            here = (sub == g) & (lane // (2 * SUB) == r)
            limits = jnp.where(here, lengths_ref[g * near + r], limits)
    limits_ref[...] = limits - me * cache_dev
    cosine, sine = cos_sin(position.astype(jnp.float32) * frequency_ref[...])
    turned = line < own * SUB + own
    first_half = lax.broadcasted_iota(jnp.int32, (block, LANES), 1) < LANES // 2
    rope_ref[:block] = jnp.where(turned, cosine, 1.0)
    rope_ref[block:] = jnp.where(turned, jnp.where(first_half, -sine, sine), 0.0)

    row = lax.broadcasted_iota(jnp.int32, (tokens, 1), 0)
    choice = jnp.full((tokens, 1), -1, jnp.int32)
    for i in range(tokens):
        step, r = i // rows, i % rows
        choice = jnp.where(row == r // near * 2 * near + r % near * 2 + step, places[i], choice)
    column = lax.broadcasted_iota(jnp.int32, (tokens, tokens * TILE), 1)
    select = jnp.where(column == choice, 1.0, 0.0).astype(jnp.bfloat16)
    def wait(i, carry):
        pltpu.make_async_copy(table_ref.at[pl.ds(0, TILE)], held.at[pl.ds(0, TILE)], sem).wait()
        return carry

    lax.fori_loop(0, found, wait, 0)
    picked = jnp.dot(select, held[...], preferred_element_type=jnp.float32)
    x_ref[...] = picked.astype(jnp.bfloat16)
    w_copy.wait()


def fetch_kernel(after_ref, far_ref, near_ref, sem):
    copy = pltpu.make_async_copy(far_ref, near_ref, sem)
    copy.start()
    copy.wait()


def fetch(after, array):
    return pl.pallas_call(
        fetch_kernel,
        out_shape=pltpu.VMEM(array.shape, array.dtype),
        in_specs=[ANY] * 2,
        out_specs=VMEM,
        scratch_shapes=[pltpu.SemaphoreType.DMA],
        cost_estimate=pl.CostEstimate(
            flops=0, bytes_accessed=2 * array.size * array.dtype.itemsize, transcendentals=0
        ),
        compiler_params=pltpu.CompilerParams(vmem_limit_bytes=4 << 20),
        name="fetch",
    )(after, in_hbm(array))


def project_kernel(x_ref, gain_ref, w_ref, out_ref):
    tokens = x_ref.shape[0]
    count = out_ref.shape[0] // BLOCK
    own = tokens // count
    x = x_ref[...].astype(jnp.float32)
    squares = jnp.sum(x * x, axis=1, keepdims=True)
    scaled = (x * gain_ref[...]).astype(jnp.bfloat16)
    partial = jnp.dot(scaled, w_ref[...], preferred_element_type=jnp.float32)
    lane = lax.broadcasted_iota(jnp.int32, (count, LANES), 1)
    last = jnp.zeros((count, LANES), jnp.float32)
    for k in range(own):
        part = slice(k * count, (k + 1) * count)
        for b in range(SUB + 2):
            line = k * SUB + b if b < SUB else (own * (b - SUB) + own * SUB + k)
            out_ref[pl.ds(line, count, stride=BLOCK)] = partial[part, b * LANES : (b + 1) * LANES]
        last = jnp.where(lane // SPAN == k, squares[part], last)
    out_ref[pl.ds(BLOCK - 2, count, stride=BLOCK)] = last
    out_ref[pl.ds(BLOCK - 1, count, stride=BLOCK)] = jnp.zeros((count, LANES), jnp.float32)


def finish_kernel(parts_ref, rope_ref, out_ref):
    count, block, head_dim = parts_ref.shape
    own = block // SUB - 1
    summed = parts_ref[0]
    for j in range(1, count):
        summed = summed + parts_ref[j]
    inverse = lax.rsqrt(summed[block - 2 : block - 1] / D + epsilon)
    line = lax.broadcasted_iota(jnp.int32, (block, head_dim), 0)
    scale = jnp.zeros((block, head_dim), jnp.float32)
    for k in range(own):
        here = (line // SUB == k) | (line == own * SUB + k) | (line == own * SUB + own + k)
        here = here & ((line < own * SUB) | (line % SUB < 2 * own))
        scale = jnp.where(here, inverse[:, k * SPAN : k * SPAN + 1], scale)
    normed = summed * scale
    turned = normed * rope_ref[:block] + pltpu.roll(normed, head_dim // 2, 1) * rope_ref[block:]
    turned = jnp.where(line < own * SUB, turned * head_dim ** (-0.5), turned).astype(jnp.bfloat16)
    for j in range(out_ref.shape[0]):
        out_ref[j] = turned


def attend_kernel(limits_ref, rows_ref, k_ref, v_ref, out_ref, scores_ref):
    row_count, cache_dev, head_dim = k_ref.shape
    count = rows_ref.shape[0]
    per_row = 2 * SUB
    near = LANES // per_row
    groups = row_count // near
    chunk = 512
    me = lax.axis_index("seq")
    lane = lax.broadcasted_iota(jnp.int32, (1, LANES), 1)
    position = lax.broadcasted_iota(jnp.int32, (chunk, LANES), 0)
    slot = lax.broadcasted_iota(jnp.int32, (LANES, LANES), 0)
    rows = rows_ref[...].astype(jnp.float32)
    new_keys = rows[:, groups * SUB :].reshape(count * SUB, head_dim)
    new_values = pltpu.roll(new_keys, LANES - groups, 0).astype(jnp.bfloat16)
    new_keys = new_keys.astype(jnp.bfloat16)

    def score(g):
        turned = rows[:, g * SUB : (g + 1) * SUB].reshape(count * SUB, head_dim).T
        blocks = [
            jnp.where(lane // per_row == r, turned, 0.0).astype(jnp.bfloat16) for r in range(near)
        ]
        weights = jnp.concatenate(blocks, axis=0)
        limit = limits_ref[g : g + 1]
        fresh = jnp.dot(new_keys, turned.astype(jnp.bfloat16), preferred_element_type=jnp.float32)
        seen = (
            (slot % SUB == g)
            & (slot // per_row == lane // per_row)
            & (slot // SUB <= lane // SUB)
            & (me == 0)
        )
        fresh = jnp.where(seen, fresh, negative)
        top = jnp.max(fresh, axis=0, keepdims=True)
        for c in range(cache_dev // chunk):
            keys = jnp.concatenate(
                [k_ref[g * near + r, pl.ds(c * chunk, chunk)] for r in range(near)], axis=1
            )
            scores = jnp.dot(keys, weights, preferred_element_type=jnp.float32)
            scores = jnp.where(position < limit - c * chunk, scores, negative)
            scores_ref[g, pl.ds(c * chunk, chunk)] = scores
            top = jnp.maximum(top, jnp.max(scores, axis=0, keepdims=True))
        return top, fresh

    def weigh(g, top, fresh):
        fresh = jnp.exp(fresh - top)
        total = jnp.sum(fresh, axis=0, keepdims=True)
        parts = []
        for c in range(cache_dev // chunk):
            weight = jnp.exp(scores_ref[g, pl.ds(c * chunk, chunk)] - top)
            total = total + jnp.sum(weight, axis=0, keepdims=True)
            parts.append(weight.astype(jnp.bfloat16).T)
        parts = jnp.concatenate(parts, axis=1)
        value = jnp.concatenate(
            [
                jnp.dot(
                    parts[r * per_row : (r + 1) * per_row],
                    v_ref[g * near + r],
                    preferred_element_type=jnp.float32,
                )
                for r in range(near)
            ],
            axis=0,
        ) + jnp.dot(fresh.T.astype(jnp.bfloat16), new_values, preferred_element_type=jnp.float32)
        for j in range(count):
            out_ref[j, pl.ds(g * SUB, SUB)] = value[j * SUB : (j + 1) * SUB]
        return total

    tops, totals = [], []
    ready = score(0)
    for g in range(groups):
        later = score(g + 1) if g + 1 < groups else None
        tops.append(ready[0])
        totals.append(weigh(g, *ready))
        ready = later
    spare = jnp.zeros((SUB - 2 * groups, LANES), jnp.float32)
    stats = jnp.concatenate(tops + totals + [spare], axis=0)
    for j in range(count):
        turn = (LANES - SUB * j) % LANES
        out_ref[j, pl.ds(groups * SUB, SUB)] = pltpu.roll(stats, turn, 1) if turn else stats


def merge_kernel(parts_ref, out_ref):
    count, rows, head_dim = parts_ref.shape
    groups = rows // SUB - 1
    stats = parts_ref[:, groups * SUB :]
    top = stats[0]
    for j in range(1, count):
        top = jnp.maximum(top, stats[j])
    factors = [jnp.exp(stats[j] - top) for j in range(count)]
    denominator = factors[0] * pltpu.roll(stats[0], SUB - groups, 0)
    for j in range(1, count):
        denominator = denominator + factors[j] * pltpu.roll(stats[j], SUB - groups, 0)
    shares = jnp.concatenate([factor / denominator for factor in factors], axis=0).T[:SUB]
    merged = []
    for g in range(groups):
        total = jnp.zeros((SUB, head_dim), jnp.float32)
        for j in range(count):
            column = j * SUB + g
            total = total + parts_ref[j, pl.ds(g * SUB, SUB)] * shares[:, column : column + 1]
        merged.append(total)
    merged = jnp.concatenate(merged, axis=1).astype(jnp.bfloat16)
    for j in range(out_ref.shape[0]):
        out_ref[j] = merged


def output_kernel(attention_ref, w_ref, other_w_ref, out_ref, held):
    groups, lines, head_dim = held.shape
    heads = attention_ref.shape[1]
    count = lines // heads
    mine = lax.axis_index("head") // 4

    def terms(place, weights):
        for j in range(count):
            part = attention_ref[2 * j + place].astype(jnp.float32)
            for g in range(groups):
                held[g, pl.ds(j * heads, heads)] = part[:, g * head_dim : (g + 1) * head_dim]
        left = jnp.concatenate(
            [
                jnp.concatenate(
                    [
                        held[g, pl.ds(step * heads + i, count // 2, stride=2 * heads)]
                        for i in range(heads)
                    ],
                    axis=1,
                )
                for step in range(2)
                for g in range(groups)
            ],
            axis=0,
        )
        return jnp.dot(left.astype(jnp.bfloat16), weights, preferred_element_type=jnp.float32)

    out_ref[...] = terms(mine, w_ref[...]) + terms(1 - mine, other_w_ref[...])


def partner(array, mask, size):
    return lax.ppermute(array, "head", [(i, i ^ mask) for i in range(size)])


def swap_with_pairs(array, n_seq, n_head):
    groups = [
        [s * n_head + i for s in range(n_seq) for i in sorted((first, first ^ FAR))]
        for first in range(n_head)
        if first < first ^ FAR
    ]
    return lax.all_to_all(
        array, ("seq", "head"), 0, 0, axis_index_groups=groups, tiled=True
    )


def body(token_ids, lengths, embedding, norm_gain, w_qkv, k_cache, v_cache, w_out):
    n_seq, n_head = lax.axis_size("seq"), lax.axis_size("head")
    feat = embedding.shape[1]
    row_count, _, cache_dev, head_dim = k_cache.shape
    tokens = 2 * row_count
    own = tokens // n_seq
    width = w_qkv.shape[2]

    picked, rope, limits, w_near = pl.pallas_call(
        functools.partial(pick_kernel, cache_dev),
        out_shape=[
            jax.ShapeDtypeStruct((tokens, feat), jnp.bfloat16),
            jax.ShapeDtypeStruct((2 * BLOCK, LANES), jnp.float32),
            jax.ShapeDtypeStruct((SUB, LANES), jnp.int32),
            pltpu.VMEM((feat, width), jnp.bfloat16),
        ],
        in_specs=[SMEM, SMEM, VMEM, ANY, ANY],
        out_specs=[VMEM] * 4,
        scratch_shapes=[
            pltpu.VMEM((tokens * TILE, feat), jnp.bfloat16),
            pltpu.SemaphoreType.DMA,
            pltpu.SemaphoreType.DMA,
        ],
        compiler_params=pltpu.CompilerParams(vmem_limit_bytes=8 << 20),
        name="pick",
    )(
        in_hbm(token_ids),
        in_hbm(lengths),
        rope_frequency(head_dim),
        in_hbm(embedding),
        in_hbm(w_qkv.reshape(feat, width)),
    )
    picked = picked + partner(picked, CORE, n_head)
    picked = picked + partner(picked, FAR, n_head)
    w_mine = fetch(picked, w_out[0])
    w_other = partner(w_mine, FAR, n_head)
    picked = picked + partner(picked, NEAR, n_head)
    gain = norm_gain.astype(jnp.float32).reshape(1, feat)

    partial = call(
        project_kernel, "project", ((n_seq * BLOCK, head_dim), jnp.float32), [VMEM] * 3
    )(picked, gain, in_vmem(w_near))
    partial = swap(partial.reshape(n_seq, BLOCK, head_dim), "seq")
    rows = call(finish_kernel, "finish", ((n_seq, BLOCK, head_dim), jnp.bfloat16), [VMEM] * 2)(
        partial, rope
    )
    rows = swap(rows, "seq")

    partial = call(
        attend_kernel,
        "attend",
        ((n_seq, BLOCK, head_dim), jnp.float32),
        [VMEM] * 4,
        [pltpu.VMEM((own, cache_dev, LANES), jnp.float32)],
        8,
    )(limits, rows, in_vmem(k_cache[:, 0]), in_vmem(v_cache[:, 0]))
    partial = swap(partial, "seq")
    attention = call(merge_kernel, "merge", ((2 * n_seq, SUB, own * head_dim), jnp.bfloat16), [VMEM])(
        partial
    )
    attention = swap_with_pairs(attention, n_seq, n_head)

    terms = call(
        output_kernel,
        "output",
        ((tokens, w_out.shape[2]), jnp.float32),
        [VMEM] * 3,
        [pltpu.VMEM((own, n_seq * SUB, head_dim), jnp.float32)],
    )(attention, in_vmem(w_mine), in_vmem(w_other))
    terms = terms + partner(terms, NEAR, n_head)
    terms = terms + partner(terms, CORE, n_head)
    return terms.astype(jnp.bfloat16).reshape(2, row_count, -1)


def solution(mesh):
    return jax.shard_map(
        body,
        mesh=mesh,
        in_specs=(
            P(),
            P(),
            P("head", "seq"),
            P("seq"),
            P("seq", "head", None),
            P(None, "head", "seq", None),
            P(None, "head", "seq", None),
            P("head", None, "seq"),
        ),
        out_specs=P(None, None, "seq"),
        check_vma=False,
    )
```

```python
import functools

import jax
import jax.numpy as jnp
from jax import lax
from jax.experimental import pallas as pl
from jax.experimental.pallas import tpu as pltpu
from jax.sharding import PartitionSpec as P

D = 8192
TILE = 16
LANES = 128
SUB = 8
BLOCK = 32
SPAN = 32

rope_base = 500000.0
epsilon = 1e-05
negative = -1e30

VMEM = pl.BlockSpec(memory_space=pltpu.VMEM)
SMEM = pl.BlockSpec(memory_space=pltpu.SMEM)
ANY = pl.BlockSpec(memory_space=pl.ANY)


def in_vmem(array):
    return pltpu.with_memory_space_constraint(array, pltpu.VMEM)


def in_hbm(array):
    return pltpu.with_memory_space_constraint(array, pltpu.HBM)


def call(kernel, name, out, in_specs, scratch=(), limit=4):
    return pl.pallas_call(
        kernel,
        out_shape=jax.ShapeDtypeStruct(*out),
        in_specs=in_specs,
        out_specs=VMEM,
        scratch_shapes=list(scratch),
        compiler_params=pltpu.CompilerParams(vmem_limit_bytes=limit << 20),
        name=name,
    )


def swap(array, axis_name):
    return lax.all_to_all(array, axis_name, 0, 0, tiled=True)


def rope_frequency(head_dim):
    exponent = jnp.arange(head_dim // 2, dtype=jnp.float32) * (2.0 / head_dim)
    frequency = jnp.power(jnp.float32(rope_base), -exponent)
    return jnp.concatenate([frequency, frequency])[None, :]


def cos_sin(angles):
    turn = jnp.floor(angles * 0.6366197723675814 + 0.5)
    rest = ((angles - turn * 1.5703125) - turn * 0.00048351287841796875) - turn * 3.13916478589249e-07
    square = rest * rest
    sine = ((-1.9515295891e-4 * square + 8.3321608736e-3) * square - 1.6666654611e-1) * square
    sine = sine * rest + rest
    cosine = (2.443315711809948e-5 * square - 1.388731625493765e-3) * square
    cosine = (cosine + 4.166664568298827e-2) * square * square - 0.5 * square + 1.0
    quarter = turn.astype(jnp.int32) & 3
    odd = (quarter & 1) == 1
    first, second = jnp.where(odd, sine, cosine), jnp.where(odd, cosine, sine)
    return (
        jnp.where((quarter == 1) | (quarter == 2), -first, first),
        jnp.where(quarter >= 2, -second, second),
    )


def pick_kernel(
    cache_dev, ids_ref, lengths_ref, frequency_ref, table_ref, far_w_ref,
    x_ref, rope_ref, limits_ref, w_ref, held, sem, w_sem,
):
    vocab_dev, feat = table_ref.shape
    steps, rows = ids_ref.shape
    tokens = steps * rows
    first = lax.axis_index("head") * vocab_dev
    held[...] = jnp.zeros_like(held)
    places = []
    found = 0
    for i in range(tokens):
        local = ids_ref[i // rows, i % rows] - first
        inside = (local >= 0) & (local < vocab_dev)
        local = jnp.clip(local, 0, vocab_dev - 1)
        within = local & (TILE - 1)

        @pl.when(inside)
        def _(start=local - within, i=i):
            pltpu.make_async_copy(
                table_ref.at[pl.ds(pl.multiple_of(start, TILE), TILE)],
                held.at[pl.ds(i * TILE, TILE)],
                sem,
            ).start(priority=1)

        found = found + inside.astype(jnp.int32)
        places.append(jnp.where(inside, i * TILE + within, -1))
    w_copy = pltpu.make_async_copy(far_w_ref, w_ref, w_sem)
    w_copy.start(priority=1)

    me = lax.axis_index("seq")
    near = LANES // (2 * SUB)
    sub = lax.broadcasted_iota(jnp.int32, (SUB, LANES), 0)
    lane = lax.broadcasted_iota(jnp.int32, (SUB, LANES), 1)
    own = rows // near
    block = rope_ref.shape[0] // 2
    line = lax.broadcasted_iota(jnp.int32, (block, LANES), 0)
    position = jnp.zeros((block, LANES), jnp.int32)
    limits = jnp.zeros((SUB, LANES), jnp.int32)
    for g in range(own):
        here = (line // SUB == g) | (line == own * SUB + g)
        position = jnp.where(here, lengths_ref[g * near + me // 2] + me % 2, position)
        for r in range(near):
            here = (sub == g) & (lane // (2 * SUB) == r)
            limits = jnp.where(here, lengths_ref[g * near + r], limits)
    limits_ref[...] = limits - me * cache_dev
    cosine, sine = cos_sin(position.astype(jnp.float32) * frequency_ref[...])
    turned = line < own * SUB + own
    first_half = lax.broadcasted_iota(jnp.int32, (block, LANES), 1) < LANES // 2
    rope_ref[:block] = jnp.where(turned, cosine, 1.0)
    rope_ref[block:] = jnp.where(turned, jnp.where(first_half, -sine, sine), 0.0)

    row = lax.broadcasted_iota(jnp.int32, (tokens, 1), 0)
    choice = jnp.full((tokens, 1), -1, jnp.int32)
    for i in range(tokens):
        step, r = i // rows, i % rows
        choice = jnp.where(row == r // near * 2 * near + r % near * 2 + step, places[i], choice)
    column = lax.broadcasted_iota(jnp.int32, (tokens, tokens * TILE), 1)
    select = jnp.where(column == choice, 1.0, 0.0).astype(jnp.bfloat16)
    def wait(i, carry):
        pltpu.make_async_copy(table_ref.at[pl.ds(0, TILE)], held.at[pl.ds(0, TILE)], sem).wait()
        return carry

    lax.fori_loop(0, found, wait, 0)
    picked = jnp.dot(select, held[...], preferred_element_type=jnp.float32)
    x_ref[...] = picked.astype(jnp.bfloat16)
    w_copy.wait()


def project_kernel(x_ref, gain_ref, w_ref, out_ref):
    tokens = x_ref.shape[0]
    count = out_ref.shape[0] // BLOCK
    own = tokens // count
    x = x_ref[...].astype(jnp.float32)
    squares = jnp.sum(x * x, axis=1, keepdims=True)
    scaled = (x * gain_ref[...]).astype(jnp.bfloat16)
    partial = jnp.dot(scaled, w_ref[...], preferred_element_type=jnp.float32)
    lane = lax.broadcasted_iota(jnp.int32, (count, LANES), 1)
    last = jnp.zeros((count, LANES), jnp.float32)
    for k in range(own):
        part = slice(k * count, (k + 1) * count)
        for b in range(SUB + 2):
            line = k * SUB + b if b < SUB else (own * (b - SUB) + own * SUB + k)
            out_ref[pl.ds(line, count, stride=BLOCK)] = partial[part, b * LANES : (b + 1) * LANES]
        last = jnp.where(lane // SPAN == k, squares[part], last)
    out_ref[pl.ds(BLOCK - 2, count, stride=BLOCK)] = last
    out_ref[pl.ds(BLOCK - 1, count, stride=BLOCK)] = jnp.zeros((count, LANES), jnp.float32)


def finish_kernel(parts_ref, rope_ref, out_ref):
    count, block, head_dim = parts_ref.shape
    own = block // SUB - 1
    summed = parts_ref[0]
    for j in range(1, count):
        summed = summed + parts_ref[j]
    inverse = lax.rsqrt(summed[block - 2 : block - 1] / D + epsilon)
    line = lax.broadcasted_iota(jnp.int32, (block, head_dim), 0)
    scale = jnp.zeros((block, head_dim), jnp.float32)
    for k in range(own):
        here = (line // SUB == k) | (line == own * SUB + k) | (line == own * SUB + own + k)
        here = here & ((line < own * SUB) | (line % SUB < 2 * own))
        scale = jnp.where(here, inverse[:, k * SPAN : k * SPAN + 1], scale)
    normed = summed * scale
    turned = normed * rope_ref[:block] + pltpu.roll(normed, head_dim // 2, 1) * rope_ref[block:]
    turned = jnp.where(line < own * SUB, turned * head_dim ** (-0.5), turned).astype(jnp.bfloat16)
    for j in range(out_ref.shape[0]):
        out_ref[j] = turned


def attend_kernel(limits_ref, rows_ref, k_ref, v_ref, out_ref, scores_ref):
    row_count, cache_dev, head_dim = k_ref.shape
    count = rows_ref.shape[0]
    per_row = 2 * SUB
    near = LANES // per_row
    groups = row_count // near
    chunk = 256
    me = lax.axis_index("seq")
    lane = lax.broadcasted_iota(jnp.int32, (1, LANES), 1)
    position = lax.broadcasted_iota(jnp.int32, (chunk, LANES), 0)
    slot = lax.broadcasted_iota(jnp.int32, (LANES, LANES), 0)
    rows = rows_ref[...].astype(jnp.float32)
    new_keys = rows[:, groups * SUB :].reshape(count * SUB, head_dim)
    new_values = pltpu.roll(new_keys, LANES - groups, 0).astype(jnp.bfloat16)
    new_keys = new_keys.astype(jnp.bfloat16)

    chunks = cache_dev // chunk
    queries, tops, fresh, totals, parts, values = {}, {}, {}, {}, {}, {}

    def begin(g):
        turned = rows[:, g * SUB : (g + 1) * SUB].reshape(count * SUB, head_dim).T
        blocks = [
            jnp.where(lane // per_row == r, turned, 0.0).astype(jnp.bfloat16) for r in range(near)
        ]
        queries[g] = jnp.concatenate(blocks, axis=0)
        new = jnp.dot(new_keys, turned.astype(jnp.bfloat16), preferred_element_type=jnp.float32)
        seen = (
            (slot % SUB == g)
            & (slot // per_row == lane // per_row)
            & (slot // SUB <= lane // SUB)
            & (me == 0)
        )
        fresh[g] = jnp.where(seen, new, negative)
        tops[g] = jnp.max(fresh[g], axis=0, keepdims=True)

    def score(g, c):
        keys = jnp.concatenate(
            [k_ref[g * near + r, pl.ds(c * chunk, chunk)] for r in range(near)], axis=1
        )
        scores = jnp.dot(keys, queries[g], preferred_element_type=jnp.float32)
        scores = jnp.where(position < limits_ref[g : g + 1] - c * chunk, scores, negative)
        scores_ref[g, pl.ds(c * chunk, chunk)] = scores
        tops[g] = jnp.maximum(tops[g], jnp.max(scores, axis=0, keepdims=True))

    def weigh(g, c):
        if c == 0:
            fresh[g] = jnp.exp(fresh[g] - tops[g])
            totals[g] = jnp.sum(fresh[g], axis=0, keepdims=True)
            parts[g] = []
        weight = jnp.exp(scores_ref[g, pl.ds(c * chunk, chunk)] - tops[g])
        totals[g] = totals[g] + jnp.sum(weight, axis=0, keepdims=True)
        parts[g].append(weight.astype(jnp.bfloat16).T)

    def add_up(g, c):
        if c == 0:
            parts[g] = jnp.concatenate(parts[g], axis=1)
            values[g] = []
        for r in range(c * near // chunks, (c + 1) * near // chunks):
            part = parts[g][r * per_row : (r + 1) * per_row]
            values[g].append(
                jnp.dot(part, v_ref[g * near + r], preferred_element_type=jnp.float32)
            )

    def end(g):
        value = jnp.concatenate(values[g], axis=0) + jnp.dot(
            fresh[g].T.astype(jnp.bfloat16), new_values, preferred_element_type=jnp.float32
        )
        for j in range(count):
            out_ref[j, pl.ds(g * SUB, SUB)] = value[j * SUB : (j + 1) * SUB]

    for g in range(groups + 2):
        if g < groups:
            begin(g)
        for c in range(chunks):
            if g < groups:
                score(g, c)
            if 0 <= g - 1 < groups:
                weigh(g - 1, c)
            if 0 <= g - 2:
                add_up(g - 2, c)
        if 0 <= g - 2:
            end(g - 2)
    tops = [tops[g] for g in range(groups)]
    totals = [totals[g] for g in range(groups)]
    spare = jnp.zeros((SUB - 2 * groups, LANES), jnp.float32)
    stats = jnp.concatenate(tops + totals + [spare], axis=0)
    for j in range(count):
        turn = (LANES - SUB * j) % LANES
        out_ref[j, pl.ds(groups * SUB, SUB)] = pltpu.roll(stats, turn, 1) if turn else stats


def merge_kernel(parts_ref, out_ref):
    count, rows, head_dim = parts_ref.shape
    groups = rows // SUB - 1
    stats = parts_ref[:, groups * SUB :]
    top = stats[0]
    for j in range(1, count):
        top = jnp.maximum(top, stats[j])
    factors = [jnp.exp(stats[j] - top) for j in range(count)]
    denominator = factors[0] * pltpu.roll(stats[0], SUB - groups, 0)
    for j in range(1, count):
        denominator = denominator + factors[j] * pltpu.roll(stats[j], SUB - groups, 0)
    shares = jnp.concatenate([factor / denominator for factor in factors], axis=0).T[:SUB]
    merged = []
    for g in range(groups):
        total = jnp.zeros((SUB, head_dim), jnp.float32)
        for j in range(count):
            column = j * SUB + g
            total = total + parts_ref[j, pl.ds(g * SUB, SUB)] * shares[:, column : column + 1]
        merged.append(total)
    merged = jnp.concatenate(merged, axis=1).astype(jnp.bfloat16)
    for j in range(out_ref.shape[0]):
        out_ref[j] = merged


def output_kernel(attention_ref, w_ref, out_ref, held):
    count, heads, width = attention_ref.shape
    groups, _, head_dim = held.shape
    for g in range(groups):
        part = attention_ref[:, :, g * head_dim : (g + 1) * head_dim]
        held[g] = part.astype(jnp.float32).reshape(count * heads, head_dim)
    left = jnp.concatenate(
        [
            jnp.concatenate(
                [
                    held[g, pl.ds(step * heads + i, count // 2, stride=2 * heads)]
                    for i in range(heads)
                ],
                axis=1,
            )
            for step in range(2)
            for g in range(groups)
        ],
        axis=0,
    )
    out_ref[...] = jnp.dot(left.astype(jnp.bfloat16), w_ref[...], preferred_element_type=jnp.float32)


def double(array, axis_name, mask, size):
    pairs = [(i, i ^ mask) for i in range(size)]
    return array + lax.ppermute(array, axis_name, pairs)


def body(token_ids, lengths, embedding, norm_gain, w_qkv, k_cache, v_cache, w_out):
    n_seq, n_head = lax.axis_size("seq"), lax.axis_size("head")
    feat = embedding.shape[1]
    row_count, _, cache_dev, head_dim = k_cache.shape
    tokens = 2 * row_count
    own = tokens // n_seq
    width = w_qkv.shape[2]

    picked, rope, limits, w_near = pl.pallas_call(
        functools.partial(pick_kernel, cache_dev),
        out_shape=[
            jax.ShapeDtypeStruct((tokens, feat), jnp.bfloat16),
            jax.ShapeDtypeStruct((2 * BLOCK, LANES), jnp.float32),
            jax.ShapeDtypeStruct((SUB, LANES), jnp.int32),
            pltpu.VMEM((feat, width), jnp.bfloat16),
        ],
        in_specs=[SMEM, SMEM, VMEM, ANY, ANY],
        out_specs=[VMEM] * 4,
        scratch_shapes=[
            pltpu.VMEM((tokens * TILE, feat), jnp.bfloat16),
            pltpu.SemaphoreType.DMA,
            pltpu.SemaphoreType.DMA,
        ],
        compiler_params=pltpu.CompilerParams(vmem_limit_bytes=8 << 20),
        name="pick",
    )(
        in_hbm(token_ids),
        in_hbm(lengths),
        rope_frequency(head_dim),
        in_hbm(embedding),
        in_hbm(w_qkv.reshape(feat, width)),
    )
    for mask in (1, 6, 2):
        picked = double(picked, "head", mask, n_head)
    gain = norm_gain.astype(jnp.float32).reshape(1, feat)

    partial = call(
        project_kernel, "project", ((n_seq * BLOCK, head_dim), jnp.float32), [VMEM] * 3
    )(picked, gain, in_vmem(w_near))
    partial = swap(partial.reshape(n_seq, BLOCK, head_dim), "seq")
    rows = call(finish_kernel, "finish", ((n_seq, BLOCK, head_dim), jnp.bfloat16), [VMEM] * 2)(
        partial, rope
    )
    rows = swap(rows, "seq")

    partial = call(
        attend_kernel,
        "attend",
        ((n_seq, BLOCK, head_dim), jnp.float32),
        [VMEM] * 4,
        [pltpu.VMEM((own, cache_dev, LANES), jnp.float32)],
        8,
    )(limits, rows, in_vmem(k_cache[:, 0]), in_vmem(v_cache[:, 0]))
    partial = swap(partial, "seq")
    attention = call(merge_kernel, "merge", ((n_seq, SUB, own * head_dim), jnp.bfloat16), [VMEM])(
        partial
    )
    attention = swap(attention, "seq")

    terms = call(
        output_kernel,
        "output",
        ((tokens, w_out.shape[2]), jnp.float32),
        [VMEM] * 2,
        [pltpu.VMEM((own, n_seq * SUB, head_dim), jnp.float32)],
    )(attention, in_vmem(w_out[0]))
    for mask in (6, 2, 1):
        terms = double(terms, "head", mask, n_head)
    return terms.astype(jnp.bfloat16).reshape(2, row_count, -1)


def solution(mesh):
    return jax.shard_map(
        body,
        mesh=mesh,
        in_specs=(
            P(),
            P(),
            P("head", "seq"),
            P("seq"),
            P("seq", "head", None),
            P(None, "head", "seq", None),
            P(None, "head", "seq", None),
            P("head", None, "seq"),
        ),
        out_specs=P(None, None, "seq"),
        check_vma=False,
    )
```

```python
import functools

import jax
import jax.numpy as jnp
from jax import lax
from jax.experimental import pallas as pl
from jax.experimental.pallas import tpu as pltpu
from jax.sharding import PartitionSpec as P

D = 8192
TILE = 16
LANES = 128
SUB = 8
BLOCK = 32
SPAN = 32

rope_base = 500000.0
epsilon = 1e-05
negative = -1e30

VMEM = pl.BlockSpec(memory_space=pltpu.VMEM)
SMEM = pl.BlockSpec(memory_space=pltpu.SMEM)
ANY = pl.BlockSpec(memory_space=pl.ANY)


def in_vmem(array):
    return pltpu.with_memory_space_constraint(array, pltpu.VMEM)


def in_hbm(array):
    return pltpu.with_memory_space_constraint(array, pltpu.HBM)


def call(kernel, name, out, in_specs, scratch=(), limit=4):
    return pl.pallas_call(
        kernel,
        out_shape=jax.ShapeDtypeStruct(*out),
        in_specs=in_specs,
        out_specs=VMEM,
        scratch_shapes=list(scratch),
        compiler_params=pltpu.CompilerParams(vmem_limit_bytes=limit << 20),
        name=name,
    )


def swap(array, axis_name):
    return lax.all_to_all(array, axis_name, 0, 0, tiled=True)


def rope_frequency(head_dim):
    exponent = jnp.arange(head_dim // 2, dtype=jnp.float32) * (2.0 / head_dim)
    frequency = jnp.power(jnp.float32(rope_base), -exponent)
    return jnp.concatenate([frequency, frequency])[None, :]


def cos_sin(angles):
    turn = jnp.floor(angles * 0.6366197723675814 + 0.5)
    rest = ((angles - turn * 1.5703125) - turn * 0.00048351287841796875) - turn * 3.13916478589249e-07
    square = rest * rest
    sine = ((-1.9515295891e-4 * square + 8.3321608736e-3) * square - 1.6666654611e-1) * square
    sine = sine * rest + rest
    cosine = (2.443315711809948e-5 * square - 1.388731625493765e-3) * square
    cosine = (cosine + 4.166664568298827e-2) * square * square - 0.5 * square + 1.0
    quarter = turn.astype(jnp.int32) & 3
    odd = (quarter & 1) == 1
    first, second = jnp.where(odd, sine, cosine), jnp.where(odd, cosine, sine)
    return (
        jnp.where((quarter == 1) | (quarter == 2), -first, first),
        jnp.where(quarter >= 2, -second, second),
    )


def pick_kernel(
    cache_dev, ids_ref, lengths_ref, frequency_ref, table_ref,
    x_ref, rope_ref, limits_ref, held, sem,
):
    vocab_dev, feat = table_ref.shape
    steps, rows = ids_ref.shape
    tokens = steps * rows
    first = lax.axis_index("head") * vocab_dev
    held[...] = jnp.zeros_like(held)
    places = []
    found = 0
    for i in range(tokens):
        local = ids_ref[i // rows, i % rows] - first
        inside = (local >= 0) & (local < vocab_dev)
        local = jnp.clip(local, 0, vocab_dev - 1)
        within = local & (TILE - 1)

        @pl.when(inside)
        def _(start=local - within, i=i):
            pltpu.make_async_copy(
                table_ref.at[pl.ds(pl.multiple_of(start, TILE), TILE)],
                held.at[pl.ds(i * TILE, TILE)],
                sem,
            ).start(priority=1)

        found = found + inside.astype(jnp.int32)
        places.append(jnp.where(inside, i * TILE + within, -1))

    me = lax.axis_index("seq")
    near = LANES // (2 * SUB)
    sub = lax.broadcasted_iota(jnp.int32, (SUB, LANES), 0)
    lane = lax.broadcasted_iota(jnp.int32, (SUB, LANES), 1)
    own = rows // near
    block = rope_ref.shape[0] // 2
    line = lax.broadcasted_iota(jnp.int32, (block, LANES), 0)
    position = jnp.zeros((block, LANES), jnp.int32)
    limits = jnp.zeros((SUB, LANES), jnp.int32)
    for g in range(own):
        here = (line // SUB == g) | (line == own * SUB + g)
        position = jnp.where(here, lengths_ref[g * near + me // 2] + me % 2, position)
        for r in range(near):
            here = (sub == g) & (lane // (2 * SUB) == r)
            limits = jnp.where(here, lengths_ref[g * near + r], limits)
    limits_ref[...] = limits - me * cache_dev
    cosine, sine = cos_sin(position.astype(jnp.float32) * frequency_ref[...])
    turned = line < own * SUB + own
    first_half = lax.broadcasted_iota(jnp.int32, (block, LANES), 1) < LANES // 2
    rope_ref[:block] = jnp.where(turned, cosine, 1.0)
    rope_ref[block:] = jnp.where(turned, jnp.where(first_half, -sine, sine), 0.0)

    row = lax.broadcasted_iota(jnp.int32, (tokens, 1), 0)
    choice = jnp.full((tokens, 1), -1, jnp.int32)
    for i in range(tokens):
        step, r = i // rows, i % rows
        choice = jnp.where(row == r // near * 2 * near + r % near * 2 + step, places[i], choice)
    column = lax.broadcasted_iota(jnp.int32, (tokens, tokens * TILE), 1)
    select = jnp.where(column == choice, 1.0, 0.0).astype(jnp.bfloat16)
    def wait(i, carry):
        pltpu.make_async_copy(table_ref.at[pl.ds(0, TILE)], held.at[pl.ds(0, TILE)], sem).wait()
        return carry

    lax.fori_loop(0, found, wait, 0)
    picked = jnp.dot(select, held[...], preferred_element_type=jnp.float32)
    x_ref[...] = picked.astype(jnp.bfloat16)


def fetch_kernel(after_ref, far_ref, near_ref, sem):
    copy = pltpu.make_async_copy(far_ref, near_ref, sem)
    copy.start()
    copy.wait()


def fetch(after, array):
    return pl.pallas_call(
        fetch_kernel,
        out_shape=pltpu.VMEM(array.shape, array.dtype),
        in_specs=[ANY] * 2,
        out_specs=VMEM,
        scratch_shapes=[pltpu.SemaphoreType.DMA],
        cost_estimate=pl.CostEstimate(
            flops=0, bytes_accessed=2 * array.size * array.dtype.itemsize, transcendentals=0
        ),
        compiler_params=pltpu.CompilerParams(vmem_limit_bytes=4 << 20),
        name="fetch",
    )(after, in_hbm(array))


def project_kernel(x_ref, gain_ref, w_ref, out_ref):
    tokens = x_ref.shape[0]
    count = out_ref.shape[0] // BLOCK
    own = tokens // count
    x = x_ref[...].astype(jnp.float32)
    squares = jnp.sum(x * x, axis=1, keepdims=True)
    scaled = (x * gain_ref[...]).astype(jnp.bfloat16)
    partial = jnp.dot(scaled, w_ref[...], preferred_element_type=jnp.float32)
    lane = lax.broadcasted_iota(jnp.int32, (count, LANES), 1)
    last = jnp.zeros((count, LANES), jnp.float32)
    for k in range(own):
        part = slice(k * count, (k + 1) * count)
        for b in range(SUB + 2):
            line = k * SUB + b if b < SUB else (own * (b - SUB) + own * SUB + k)
            out_ref[pl.ds(line, count, stride=BLOCK)] = partial[part, b * LANES : (b + 1) * LANES]
        last = jnp.where(lane // SPAN == k, squares[part], last)
    out_ref[pl.ds(BLOCK - 2, count, stride=BLOCK)] = last
    out_ref[pl.ds(BLOCK - 1, count, stride=BLOCK)] = jnp.zeros((count, LANES), jnp.float32)


def finish_kernel(parts_ref, rope_ref, out_ref):
    count, block, head_dim = parts_ref.shape
    own = block // SUB - 1
    summed = parts_ref[0]
    for j in range(1, count):
        summed = summed + parts_ref[j]
    inverse = lax.rsqrt(summed[block - 2 : block - 1] / D + epsilon)
    line = lax.broadcasted_iota(jnp.int32, (block, head_dim), 0)
    scale = jnp.zeros((block, head_dim), jnp.float32)
    for k in range(own):
        here = (line // SUB == k) | (line == own * SUB + k) | (line == own * SUB + own + k)
        here = here & ((line < own * SUB) | (line % SUB < 2 * own))
        scale = jnp.where(here, inverse[:, k * SPAN : k * SPAN + 1], scale)
    normed = summed * scale
    turned = normed * rope_ref[:block] + pltpu.roll(normed, head_dim // 2, 1) * rope_ref[block:]
    turned = jnp.where(line < own * SUB, turned * head_dim ** (-0.5), turned).astype(jnp.bfloat16)
    for j in range(out_ref.shape[0]):
        out_ref[j] = turned


def attend_kernel(limits_ref, rows_ref, k_ref, v_ref, out_ref, scores_ref):
    row_count, cache_dev, head_dim = k_ref.shape
    count = rows_ref.shape[0]
    per_row = 2 * SUB
    near = LANES // per_row
    groups = row_count // near
    chunk = 512
    me = lax.axis_index("seq")
    lane = lax.broadcasted_iota(jnp.int32, (1, LANES), 1)
    position = lax.broadcasted_iota(jnp.int32, (chunk, LANES), 0)
    slot = lax.broadcasted_iota(jnp.int32, (LANES, LANES), 0)
    rows = rows_ref[...].astype(jnp.float32)
    new_keys = rows[:, groups * SUB :].reshape(count * SUB, head_dim)
    new_values = pltpu.roll(new_keys, LANES - groups, 0).astype(jnp.bfloat16)
    new_keys = new_keys.astype(jnp.bfloat16)

    def score(g):
        turned = rows[:, g * SUB : (g + 1) * SUB].reshape(count * SUB, head_dim).T
        blocks = [
            jnp.where(lane // per_row == r, turned, 0.0).astype(jnp.bfloat16) for r in range(near)
        ]
        weights = jnp.concatenate(blocks, axis=0)
        limit = limits_ref[g : g + 1]
        fresh = jnp.dot(new_keys, turned.astype(jnp.bfloat16), preferred_element_type=jnp.float32)
        seen = (
            (slot % SUB == g)
            & (slot // per_row == lane // per_row)
            & (slot // SUB <= lane // SUB)
            & (me == 0)
        )
        fresh = jnp.where(seen, fresh, negative)
        top = jnp.max(fresh, axis=0, keepdims=True)
        for c in range(cache_dev // chunk):
            keys = jnp.concatenate(
                [k_ref[g * near + r, pl.ds(c * chunk, chunk)] for r in range(near)], axis=1
            )
            scores = jnp.dot(keys, weights, preferred_element_type=jnp.float32)
            scores = jnp.where(position < limit - c * chunk, scores, negative)
            scores_ref[g, pl.ds(c * chunk, chunk)] = scores
            top = jnp.maximum(top, jnp.max(scores, axis=0, keepdims=True))
        return top, fresh

    def weigh(g, top, fresh):
        fresh = jnp.exp(fresh - top)
        total = jnp.sum(fresh, axis=0, keepdims=True)
        parts = []
        for c in range(cache_dev // chunk):
            weight = jnp.exp(scores_ref[g, pl.ds(c * chunk, chunk)] - top)
            total = total + jnp.sum(weight, axis=0, keepdims=True)
            parts.append(weight.astype(jnp.bfloat16).T)
        parts = jnp.concatenate(parts, axis=1)
        value = jnp.concatenate(
            [
                jnp.dot(
                    parts[r * per_row : (r + 1) * per_row],
                    v_ref[g * near + r],
                    preferred_element_type=jnp.float32,
                )
                for r in range(near)
            ],
            axis=0,
        ) + jnp.dot(fresh.T.astype(jnp.bfloat16), new_values, preferred_element_type=jnp.float32)
        for j in range(count):
            out_ref[j, pl.ds(g * SUB, SUB)] = value[j * SUB : (j + 1) * SUB]
        return total

    tops, totals = [], []
    ready = score(0)
    for g in range(groups):
        later = score(g + 1) if g + 1 < groups else None
        tops.append(ready[0])
        totals.append(weigh(g, *ready))
        ready = later
    spare = jnp.zeros((SUB - 2 * groups, LANES), jnp.float32)
    stats = jnp.concatenate(tops + totals + [spare], axis=0)
    for j in range(count):
        turn = (LANES - SUB * j) % LANES
        out_ref[j, pl.ds(groups * SUB, SUB)] = pltpu.roll(stats, turn, 1) if turn else stats


def merge_kernel(parts_ref, out_ref):
    count, rows, head_dim = parts_ref.shape
    groups = rows // SUB - 1
    stats = parts_ref[:, groups * SUB :]
    top = stats[0]
    for j in range(1, count):
        top = jnp.maximum(top, stats[j])
    factors = [jnp.exp(stats[j] - top) for j in range(count)]
    denominator = factors[0] * pltpu.roll(stats[0], SUB - groups, 0)
    for j in range(1, count):
        denominator = denominator + factors[j] * pltpu.roll(stats[j], SUB - groups, 0)
    shares = jnp.concatenate([factor / denominator for factor in factors], axis=0).T[:SUB]
    merged = []
    for g in range(groups):
        total = jnp.zeros((SUB, head_dim), jnp.float32)
        for j in range(count):
            column = j * SUB + g
            total = total + parts_ref[j, pl.ds(g * SUB, SUB)] * shares[:, column : column + 1]
        merged.append(total)
    merged = jnp.concatenate(merged, axis=1).astype(jnp.bfloat16)
    for j in range(out_ref.shape[0]):
        out_ref[j] = merged


def output_kernel(attention_ref, w_ref, out_ref, held):
    count, heads, width = attention_ref.shape
    groups, _, head_dim = held.shape
    for g in range(groups):
        part = attention_ref[:, :, g * head_dim : (g + 1) * head_dim]
        held[g] = part.astype(jnp.float32).reshape(count * heads, head_dim)
    left = jnp.concatenate(
        [
            jnp.concatenate(
                [
                    held[g, pl.ds(step * heads + i, count // 2, stride=2 * heads)]
                    for i in range(heads)
                ],
                axis=1,
            )
            for step in range(2)
            for g in range(groups)
        ],
        axis=0,
    )
    out_ref[...] = jnp.dot(left.astype(jnp.bfloat16), w_ref[...], preferred_element_type=jnp.float32)


def double(array, axis_name, mask, size):
    pairs = [(i, i ^ mask) for i in range(size)]
    return array + lax.ppermute(array, axis_name, pairs)


def body(token_ids, lengths, embedding, norm_gain, w_qkv, k_cache, v_cache, w_out):
    n_seq, n_head = lax.axis_size("seq"), lax.axis_size("head")
    feat = embedding.shape[1]
    row_count, _, cache_dev, head_dim = k_cache.shape
    tokens = 2 * row_count
    own = tokens // n_seq
    width = w_qkv.shape[2]

    picked, rope, limits = pl.pallas_call(
        functools.partial(pick_kernel, cache_dev),
        out_shape=[
            jax.ShapeDtypeStruct((tokens, feat), jnp.bfloat16),
            jax.ShapeDtypeStruct((2 * BLOCK, LANES), jnp.float32),
            jax.ShapeDtypeStruct((SUB, LANES), jnp.int32),
        ],
        in_specs=[SMEM, SMEM, VMEM, ANY],
        out_specs=[VMEM] * 3,
        scratch_shapes=[
            pltpu.VMEM((tokens * TILE, feat), jnp.bfloat16),
            pltpu.SemaphoreType.DMA,
        ],
        compiler_params=pltpu.CompilerParams(vmem_limit_bytes=8 << 20),
        name="pick",
    )(
        in_hbm(token_ids),
        in_hbm(lengths),
        rope_frequency(head_dim),
        in_hbm(embedding),
    )
    w_near = fetch(picked, w_qkv.reshape(feat, width))
    for mask in (1, 2, 6):
        picked = double(picked, "head", mask, n_head)
    gain = norm_gain.astype(jnp.float32).reshape(1, feat)

    partial = call(
        project_kernel, "project", ((n_seq * BLOCK, head_dim), jnp.float32), [VMEM] * 3
    )(picked, gain, in_vmem(w_near))
    partial = swap(partial.reshape(n_seq, BLOCK, head_dim), "seq")
    rows = call(finish_kernel, "finish", ((n_seq, BLOCK, head_dim), jnp.bfloat16), [VMEM] * 2)(
        partial, rope
    )
    rows = swap(rows, "seq")

    partial = call(
        attend_kernel,
        "attend",
        ((n_seq, BLOCK, head_dim), jnp.float32),
        [VMEM] * 4,
        [pltpu.VMEM((own, cache_dev, LANES), jnp.float32)],
        8,
    )(limits, rows, in_vmem(k_cache[:, 0]), in_vmem(v_cache[:, 0]))
    partial = swap(partial, "seq")
    attention = call(merge_kernel, "merge", ((n_seq, SUB, own * head_dim), jnp.bfloat16), [VMEM])(
        partial
    )
    attention = swap(attention, "seq")

    terms = call(
        output_kernel,
        "output",
        ((tokens, w_out.shape[2]), jnp.float32),
        [VMEM] * 2,
        [pltpu.VMEM((own, n_seq * SUB, head_dim), jnp.float32)],
    )(attention, in_vmem(w_out[0]))
    for mask in (2, 6, 1):
        terms = double(terms, "head", mask, n_head)
    return terms.astype(jnp.bfloat16).reshape(2, row_count, -1)


def solution(mesh):
    return jax.shard_map(
        body,
        mesh=mesh,
        in_specs=(
            P(),
            P(),
            P("head", "seq"),
            P("seq"),
            P("seq", "head", None),
            P(None, "head", "seq", None),
            P(None, "head", "seq", None),
            P("head", None, "seq"),
        ),
        out_specs=P(None, None, "seq"),
        check_vma=False,
    )
```

```python
import functools

import jax
import jax.numpy as jnp
from jax import lax
from jax.experimental import pallas as pl
from jax.experimental.pallas import tpu as pltpu
from jax.sharding import PartitionSpec as P

D = 8192
TILE = 16
LANES = 128
SUB = 8
BLOCK = 32
SPAN = 32

rope_base = 500000.0
epsilon = 1e-05
negative = -1e30

VMEM = pl.BlockSpec(memory_space=pltpu.VMEM)
SMEM = pl.BlockSpec(memory_space=pltpu.SMEM)
ANY = pl.BlockSpec(memory_space=pl.ANY)


def in_vmem(array):
    return pltpu.with_memory_space_constraint(array, pltpu.VMEM)


def in_hbm(array):
    return pltpu.with_memory_space_constraint(array, pltpu.HBM)


def call(kernel, name, out, in_specs, scratch=(), limit=4):
    return pl.pallas_call(
        kernel,
        out_shape=jax.ShapeDtypeStruct(*out),
        in_specs=in_specs,
        out_specs=VMEM,
        scratch_shapes=list(scratch),
        compiler_params=pltpu.CompilerParams(vmem_limit_bytes=limit << 20),
        name=name,
    )


def swap(array, axis_name):
    return lax.all_to_all(array, axis_name, 0, 0, tiled=True)


def rope_frequency(head_dim):
    exponent = jnp.arange(head_dim // 2, dtype=jnp.float32) * (2.0 / head_dim)
    frequency = jnp.power(jnp.float32(rope_base), -exponent)
    return jnp.concatenate([frequency, frequency])[None, :]


def cos_sin(angles):
    turn = jnp.floor(angles * 0.6366197723675814 + 0.5)
    rest = ((angles - turn * 1.5703125) - turn * 0.00048351287841796875) - turn * 3.13916478589249e-07
    square = rest * rest
    sine = ((-1.9515295891e-4 * square + 8.3321608736e-3) * square - 1.6666654611e-1) * square
    sine = sine * rest + rest
    cosine = (2.443315711809948e-5 * square - 1.388731625493765e-3) * square
    cosine = (cosine + 4.166664568298827e-2) * square * square - 0.5 * square + 1.0
    quarter = turn.astype(jnp.int32) & 3
    odd = (quarter & 1) == 1
    first, second = jnp.where(odd, sine, cosine), jnp.where(odd, cosine, sine)
    return (
        jnp.where((quarter == 1) | (quarter == 2), -first, first),
        jnp.where(quarter >= 2, -second, second),
    )


def pick_kernel(ids_ref, table_ref, x_ref, held, sem):
    vocab_dev, feat = table_ref.shape
    steps, rows = ids_ref.shape
    tokens = steps * rows
    first = lax.axis_index("head") * vocab_dev
    held[...] = jnp.zeros_like(held)
    places = []
    found = 0
    for i in range(tokens):
        local = ids_ref[i // rows, i % rows] - first
        inside = (local >= 0) & (local < vocab_dev)
        local = jnp.clip(local, 0, vocab_dev - 1)
        within = local & (TILE - 1)

        @pl.when(inside)
        def _(start=local - within, i=i):
            pltpu.make_async_copy(
                table_ref.at[pl.ds(pl.multiple_of(start, TILE), TILE)],
                held.at[pl.ds(i * TILE, TILE)],
                sem,
            ).start(priority=1)

        found = found + inside.astype(jnp.int32)
        places.append(jnp.where(inside, i * TILE + within, -1))

    near = LANES // (2 * SUB)
    row = lax.broadcasted_iota(jnp.int32, (tokens, 1), 0)
    choice = jnp.full((tokens, 1), -1, jnp.int32)
    for i in range(tokens):
        step, r = i // rows, i % rows
        choice = jnp.where(row == r // near * 2 * near + r % near * 2 + step, places[i], choice)
    column = lax.broadcasted_iota(jnp.int32, (tokens, tokens * TILE), 1)
    select = jnp.where(column == choice, 1.0, 0.0).astype(jnp.bfloat16)
    def wait(i, carry):
        pltpu.make_async_copy(table_ref.at[pl.ds(0, TILE)], held.at[pl.ds(0, TILE)], sem).wait()
        return carry

    lax.fori_loop(0, found, wait, 0)
    picked = jnp.dot(select, held[...], preferred_element_type=jnp.float32)
    x_ref[...] = picked.astype(jnp.bfloat16)


def prepare_kernel(
    cache_dev, after_ref, lengths_ref, frequency_ref, far_w_ref, rope_ref, limits_ref, w_ref, sem
):
    copy = pltpu.make_async_copy(far_w_ref, w_ref, sem)
    copy.start()
    rows = lengths_ref.shape[0]
    me = lax.axis_index("seq")
    near = LANES // (2 * SUB)
    sub = lax.broadcasted_iota(jnp.int32, (SUB, LANES), 0)
    lane = lax.broadcasted_iota(jnp.int32, (SUB, LANES), 1)
    own = rows // near
    block = rope_ref.shape[0] // 2
    line = lax.broadcasted_iota(jnp.int32, (block, LANES), 0)
    position = jnp.zeros((block, LANES), jnp.int32)
    limits = jnp.zeros((SUB, LANES), jnp.int32)
    for g in range(own):
        here = (line // SUB == g) | (line == own * SUB + g)
        position = jnp.where(here, lengths_ref[g * near + me // 2] + me % 2, position)
        for r in range(near):
            here = (sub == g) & (lane // (2 * SUB) == r)
            limits = jnp.where(here, lengths_ref[g * near + r], limits)
    limits_ref[...] = limits - me * cache_dev
    cosine, sine = cos_sin(position.astype(jnp.float32) * frequency_ref[...])
    turned = line < own * SUB + own
    first_half = lax.broadcasted_iota(jnp.int32, (block, LANES), 1) < LANES // 2
    rope_ref[:block] = jnp.where(turned, cosine, 1.0)
    rope_ref[block:] = jnp.where(turned, jnp.where(first_half, -sine, sine), 0.0)
    copy.wait()


def prepare(after, lengths, frequency, w, cache_dev):
    return pl.pallas_call(
        functools.partial(prepare_kernel, cache_dev),
        out_shape=[
            jax.ShapeDtypeStruct((2 * BLOCK, LANES), jnp.float32),
            jax.ShapeDtypeStruct((SUB, LANES), jnp.int32),
            pltpu.VMEM(w.shape, w.dtype),
        ],
        in_specs=[ANY, SMEM, VMEM, ANY],
        out_specs=[VMEM] * 3,
        scratch_shapes=[pltpu.SemaphoreType.DMA],
        cost_estimate=pl.CostEstimate(
            flops=0, bytes_accessed=2 * w.size * w.dtype.itemsize, transcendentals=0
        ),
        compiler_params=pltpu.CompilerParams(vmem_limit_bytes=4 << 20),
        name="prepare",
    )(after, in_hbm(lengths), frequency, in_hbm(w))


def project_kernel(x_ref, gain_ref, w_ref, out_ref):
    tokens = x_ref.shape[0]
    count = out_ref.shape[0] // BLOCK
    own = tokens // count
    x = x_ref[...].astype(jnp.float32)
    squares = jnp.sum(x * x, axis=1, keepdims=True)
    scaled = (x * gain_ref[...]).astype(jnp.bfloat16)
    partial = jnp.dot(scaled, w_ref[...], preferred_element_type=jnp.float32)
    lane = lax.broadcasted_iota(jnp.int32, (count, LANES), 1)
    last = jnp.zeros((count, LANES), jnp.float32)
    for k in range(own):
        part = slice(k * count, (k + 1) * count)
        for b in range(SUB + 2):
            line = k * SUB + b if b < SUB else (own * (b - SUB) + own * SUB + k)
            out_ref[pl.ds(line, count, stride=BLOCK)] = partial[part, b * LANES : (b + 1) * LANES]
        last = jnp.where(lane // SPAN == k, squares[part], last)
    out_ref[pl.ds(BLOCK - 2, count, stride=BLOCK)] = last
    out_ref[pl.ds(BLOCK - 1, count, stride=BLOCK)] = jnp.zeros((count, LANES), jnp.float32)


def finish_kernel(parts_ref, rope_ref, out_ref):
    count, block, head_dim = parts_ref.shape
    own = block // SUB - 1
    summed = parts_ref[0]
    for j in range(1, count):
        summed = summed + parts_ref[j]
    inverse = lax.rsqrt(summed[block - 2 : block - 1] / D + epsilon)
    line = lax.broadcasted_iota(jnp.int32, (block, head_dim), 0)
    scale = jnp.zeros((block, head_dim), jnp.float32)
    for k in range(own):
        here = (line // SUB == k) | (line == own * SUB + k) | (line == own * SUB + own + k)
        here = here & ((line < own * SUB) | (line % SUB < 2 * own))
        scale = jnp.where(here, inverse[:, k * SPAN : k * SPAN + 1], scale)
    normed = summed * scale
    turned = normed * rope_ref[:block] + pltpu.roll(normed, head_dim // 2, 1) * rope_ref[block:]
    turned = jnp.where(line < own * SUB, turned * head_dim ** (-0.5), turned).astype(jnp.bfloat16)
    for j in range(out_ref.shape[0]):
        out_ref[j] = turned


def attend_kernel(limits_ref, rows_ref, k_ref, v_ref, out_ref, scores_ref):
    row_count, cache_dev, head_dim = k_ref.shape
    count = rows_ref.shape[0]
    per_row = 2 * SUB
    near = LANES // per_row
    groups = row_count // near
    chunk = 512
    me = lax.axis_index("seq")
    lane = lax.broadcasted_iota(jnp.int32, (1, LANES), 1)
    position = lax.broadcasted_iota(jnp.int32, (chunk, LANES), 0)
    slot = lax.broadcasted_iota(jnp.int32, (LANES, LANES), 0)
    rows = rows_ref[...].astype(jnp.float32)
    new_keys = rows[:, groups * SUB :].reshape(count * SUB, head_dim)
    new_values = pltpu.roll(new_keys, LANES - groups, 0).astype(jnp.bfloat16)
    new_keys = new_keys.astype(jnp.bfloat16)

    def score(g):
        turned = rows[:, g * SUB : (g + 1) * SUB].reshape(count * SUB, head_dim).T
        blocks = [
            jnp.where(lane // per_row == r, turned, 0.0).astype(jnp.bfloat16) for r in range(near)
        ]
        weights = jnp.concatenate(blocks, axis=0)
        limit = limits_ref[g : g + 1]
        fresh = jnp.dot(new_keys, turned.astype(jnp.bfloat16), preferred_element_type=jnp.float32)
        seen = (
            (slot % SUB == g)
            & (slot // per_row == lane // per_row)
            & (slot // SUB <= lane // SUB)
            & (me == 0)
        )
        fresh = jnp.where(seen, fresh, negative)
        top = jnp.max(fresh, axis=0, keepdims=True)
        for c in range(cache_dev // chunk):
            keys = jnp.concatenate(
                [k_ref[g * near + r, pl.ds(c * chunk, chunk)] for r in range(near)], axis=1
            )
            scores = jnp.dot(keys, weights, preferred_element_type=jnp.float32)
            scores = jnp.where(position < limit - c * chunk, scores, negative)
            scores_ref[g, pl.ds(c * chunk, chunk)] = scores
            top = jnp.maximum(top, jnp.max(scores, axis=0, keepdims=True))
        return top, fresh

    def weigh(g, top, fresh):
        fresh = jnp.exp(fresh - top)
        total = jnp.sum(fresh, axis=0, keepdims=True)
        parts = []
        for c in range(cache_dev // chunk):
            weight = jnp.exp(scores_ref[g, pl.ds(c * chunk, chunk)] - top)
            total = total + jnp.sum(weight, axis=0, keepdims=True)
            parts.append(weight.astype(jnp.bfloat16).T)
        parts = jnp.concatenate(parts, axis=1)
        value = jnp.concatenate(
            [
                jnp.dot(
                    parts[r * per_row : (r + 1) * per_row],
                    v_ref[g * near + r],
                    preferred_element_type=jnp.float32,
                )
                for r in range(near)
            ],
            axis=0,
        ) + jnp.dot(fresh.T.astype(jnp.bfloat16), new_values, preferred_element_type=jnp.float32)
        for j in range(count):
            out_ref[j, pl.ds(g * SUB, SUB)] = value[j * SUB : (j + 1) * SUB]
        return total

    tops, totals = [], []
    ready = score(0)
    for g in range(groups):
        later = score(g + 1) if g + 1 < groups else None
        tops.append(ready[0])
        totals.append(weigh(g, *ready))
        ready = later
    spare = jnp.zeros((SUB - 2 * groups, LANES), jnp.float32)
    stats = jnp.concatenate(tops + totals + [spare], axis=0)
    for j in range(count):
        turn = (LANES - SUB * j) % LANES
        out_ref[j, pl.ds(groups * SUB, SUB)] = pltpu.roll(stats, turn, 1) if turn else stats


def merge_kernel(parts_ref, out_ref):
    count, rows, head_dim = parts_ref.shape
    groups = rows // SUB - 1
    stats = parts_ref[:, groups * SUB :]
    top = stats[0]
    for j in range(1, count):
        top = jnp.maximum(top, stats[j])
    factors = [jnp.exp(stats[j] - top) for j in range(count)]
    denominator = factors[0] * pltpu.roll(stats[0], SUB - groups, 0)
    for j in range(1, count):
        denominator = denominator + factors[j] * pltpu.roll(stats[j], SUB - groups, 0)
    shares = jnp.concatenate([factor / denominator for factor in factors], axis=0).T[:SUB]
    merged = []
    for g in range(groups):
        total = jnp.zeros((SUB, head_dim), jnp.float32)
        for j in range(count):
            column = j * SUB + g
            total = total + parts_ref[j, pl.ds(g * SUB, SUB)] * shares[:, column : column + 1]
        merged.append(total)
    merged = jnp.concatenate(merged, axis=1).astype(jnp.bfloat16)
    for j in range(out_ref.shape[0]):
        out_ref[j] = merged


def output_kernel(attention_ref, w_ref, out_ref, held):
    count, heads, width = attention_ref.shape
    groups, _, head_dim = held.shape
    for g in range(groups):
        part = attention_ref[:, :, g * head_dim : (g + 1) * head_dim]
        held[g] = part.astype(jnp.float32).reshape(count * heads, head_dim)
    left = jnp.concatenate(
        [
            jnp.concatenate(
                [
                    held[g, pl.ds(step * heads + i, count // 2, stride=2 * heads)]
                    for i in range(heads)
                ],
                axis=1,
            )
            for step in range(2)
            for g in range(groups)
        ],
        axis=0,
    )
    out_ref[...] = jnp.dot(left.astype(jnp.bfloat16), w_ref[...], preferred_element_type=jnp.float32)


def double(array, axis_name, mask, size):
    pairs = [(i, i ^ mask) for i in range(size)]
    return array + lax.ppermute(array, axis_name, pairs)


def body(token_ids, lengths, embedding, norm_gain, w_qkv, k_cache, v_cache, w_out):
    n_seq, n_head = lax.axis_size("seq"), lax.axis_size("head")
    feat = embedding.shape[1]
    row_count, _, cache_dev, head_dim = k_cache.shape
    tokens = 2 * row_count
    own = tokens // n_seq
    width = w_qkv.shape[2]

    picked = call(
        pick_kernel,
        "pick",
        ((tokens, feat), jnp.bfloat16),
        [SMEM, ANY],
        [pltpu.VMEM((tokens * TILE, feat), jnp.bfloat16), pltpu.SemaphoreType.DMA],
        8,
    )(in_hbm(token_ids), in_hbm(embedding))
    rope, limits, w_near = prepare(
        picked, lengths, rope_frequency(head_dim), w_qkv.reshape(feat, width), cache_dev
    )
    for mask in (1, 2, 6):
        picked = double(picked, "head", mask, n_head)
    gain = norm_gain.astype(jnp.float32).reshape(1, feat)

    partial = call(
        project_kernel, "project", ((n_seq * BLOCK, head_dim), jnp.float32), [VMEM] * 3
    )(picked, gain, in_vmem(w_near))
    partial = swap(partial.reshape(n_seq, BLOCK, head_dim), "seq")
    rows = call(finish_kernel, "finish", ((n_seq, BLOCK, head_dim), jnp.bfloat16), [VMEM] * 2)(
        partial, rope
    )
    rows = swap(rows, "seq")

    partial = call(
        attend_kernel,
        "attend",
        ((n_seq, BLOCK, head_dim), jnp.float32),
        [VMEM] * 4,
        [pltpu.VMEM((own, cache_dev, LANES), jnp.float32)],
        8,
    )(limits, rows, in_vmem(k_cache[:, 0]), in_vmem(v_cache[:, 0]))
    partial = swap(partial, "seq")
    attention = call(merge_kernel, "merge", ((n_seq, SUB, own * head_dim), jnp.bfloat16), [VMEM])(
        partial
    )
    attention = swap(attention, "seq")

    terms = call(
        output_kernel,
        "output",
        ((tokens, w_out.shape[2]), jnp.float32),
        [VMEM] * 2,
        [pltpu.VMEM((own, n_seq * SUB, head_dim), jnp.float32)],
    )(attention, in_vmem(w_out[0]))
    for mask in (2, 6, 1):
        terms = double(terms, "head", mask, n_head)
    return terms.astype(jnp.bfloat16).reshape(2, row_count, -1)


def solution(mesh):
    return jax.shard_map(
        body,
        mesh=mesh,
        in_specs=(
            P(),
            P(),
            P("head", "seq"),
            P("seq"),
            P("seq", "head", None),
            P(None, "head", "seq", None),
            P(None, "head", "seq", None),
            P("head", None, "seq"),
        ),
        out_specs=P(None, None, "seq"),
        check_vma=False,
    )
```

```python
import functools

import jax
import jax.numpy as jnp
from jax import lax
from jax.experimental import pallas as pl
from jax.experimental.pallas import tpu as pltpu
from jax.sharding import PartitionSpec as P

D = 8192
TILE = 16
LANES = 128
SUB = 8
BLOCK = 32
SPAN = 32

rope_base = 500000.0
epsilon = 1e-05
negative = -1e30

VMEM = pl.BlockSpec(memory_space=pltpu.VMEM)
SMEM = pl.BlockSpec(memory_space=pltpu.SMEM)
ANY = pl.BlockSpec(memory_space=pl.ANY)


def in_vmem(array):
    return pltpu.with_memory_space_constraint(array, pltpu.VMEM)


def in_hbm(array):
    return pltpu.with_memory_space_constraint(array, pltpu.HBM)


def call(kernel, name, out, in_specs, scratch=(), limit=4):
    return pl.pallas_call(
        kernel,
        out_shape=jax.ShapeDtypeStruct(*out),
        in_specs=in_specs,
        out_specs=VMEM,
        scratch_shapes=list(scratch),
        compiler_params=pltpu.CompilerParams(vmem_limit_bytes=limit << 20),
        name=name,
    )


def swap(array, axis_name):
    return lax.all_to_all(array, axis_name, 0, 0, tiled=True)


def rope_frequency(head_dim):
    exponent = jnp.arange(head_dim // 2, dtype=jnp.float32) * (2.0 / head_dim)
    frequency = jnp.power(jnp.float32(rope_base), -exponent)
    return jnp.concatenate([frequency, frequency])[None, :]


def cos_sin(angles):
    turn = jnp.floor(angles * 0.6366197723675814 + 0.5)
    rest = ((angles - turn * 1.5703125) - turn * 0.00048351287841796875) - turn * 3.13916478589249e-07
    square = rest * rest
    sine = ((-1.9515295891e-4 * square + 8.3321608736e-3) * square - 1.6666654611e-1) * square
    sine = sine * rest + rest
    cosine = (2.443315711809948e-5 * square - 1.388731625493765e-3) * square
    cosine = (cosine + 4.166664568298827e-2) * square * square - 0.5 * square + 1.0
    quarter = turn.astype(jnp.int32) & 3
    odd = (quarter & 1) == 1
    first, second = jnp.where(odd, sine, cosine), jnp.where(odd, cosine, sine)
    return (
        jnp.where((quarter == 1) | (quarter == 2), -first, first),
        jnp.where(quarter >= 2, -second, second),
    )


def pick_kernel(
    cache_dev, ids_ref, lengths_ref, frequency_ref, table_ref,
    x_ref, rope_ref, limits_ref, held, sem,
):
    vocab_dev, feat = table_ref.shape
    steps, rows = ids_ref.shape
    tokens = steps * rows
    first = lax.axis_index("head") * vocab_dev
    held[...] = jnp.zeros_like(held)
    places = []
    found = 0
    for i in range(tokens):
        local = ids_ref[i // rows, i % rows] - first
        inside = (local >= 0) & (local < vocab_dev)
        local = jnp.clip(local, 0, vocab_dev - 1)
        within = local & (TILE - 1)

        @pl.when(inside)
        def _(start=local - within, i=i):
            pltpu.make_async_copy(
                table_ref.at[pl.ds(pl.multiple_of(start, TILE), TILE)],
                held.at[pl.ds(i * TILE, TILE)],
                sem,
            ).start(priority=1)

        found = found + inside.astype(jnp.int32)
        places.append(jnp.where(inside, i * TILE + within, -1))

    me = lax.axis_index("seq")
    near = LANES // (2 * SUB)
    sub = lax.broadcasted_iota(jnp.int32, (SUB, LANES), 0)
    lane = lax.broadcasted_iota(jnp.int32, (SUB, LANES), 1)
    own = rows // near
    block = rope_ref.shape[0] // 2
    line = lax.broadcasted_iota(jnp.int32, (block, LANES), 0)
    position = jnp.zeros((block, LANES), jnp.int32)
    limits = jnp.zeros((SUB, LANES), jnp.int32)
    for g in range(own):
        here = (line // SUB == g) | (line == own * SUB + g)
        position = jnp.where(here, lengths_ref[g * near + me // 2] + me % 2, position)
        for r in range(near):
            here = (sub == g) & (lane // (2 * SUB) == r)
            limits = jnp.where(here, lengths_ref[g * near + r], limits)
    limits_ref[...] = limits - me * cache_dev
    cosine, sine = cos_sin(position.astype(jnp.float32) * frequency_ref[...])
    turned = line < own * SUB + own
    first_half = lax.broadcasted_iota(jnp.int32, (block, LANES), 1) < LANES // 2
    rope_ref[:block] = jnp.where(turned, cosine, 1.0)
    rope_ref[block:] = jnp.where(turned, jnp.where(first_half, -sine, sine), 0.0)

    row = lax.broadcasted_iota(jnp.int32, (tokens, 1), 0)
    choice = jnp.full((tokens, 1), -1, jnp.int32)
    for i in range(tokens):
        step, r = i // rows, i % rows
        choice = jnp.where(row == r // near * 2 * near + r % near * 2 + step, places[i], choice)
    column = lax.broadcasted_iota(jnp.int32, (tokens, tokens * TILE), 1)
    select = jnp.where(column == choice, 1.0, 0.0).astype(jnp.bfloat16)
    def wait(i, carry):
        pltpu.make_async_copy(table_ref.at[pl.ds(0, TILE)], held.at[pl.ds(0, TILE)], sem).wait()
        return carry

    lax.fori_loop(0, found, wait, 0)
    picked = jnp.dot(select, held[...], preferred_element_type=jnp.float32)
    x_ref[...] = picked.astype(jnp.bfloat16)


def fetch_kernel(after_ref, far_ref, near_ref, sem):
    copy = pltpu.make_async_copy(far_ref, near_ref, sem)
    copy.start()
    copy.wait()


def fetch(after, array):
    return pl.pallas_call(
        fetch_kernel,
        out_shape=pltpu.VMEM(array.shape, array.dtype),
        in_specs=[ANY] * 2,
        out_specs=VMEM,
        scratch_shapes=[pltpu.SemaphoreType.DMA],
        cost_estimate=pl.CostEstimate(
            flops=0, bytes_accessed=2 * array.size * array.dtype.itemsize, transcendentals=0
        ),
        compiler_params=pltpu.CompilerParams(vmem_limit_bytes=4 << 20),
        name="fetch",
    )(after, in_hbm(array))


def project_kernel(x_ref, gain_ref, w_ref, out_ref):
    tokens = x_ref.shape[0]
    count = out_ref.shape[0] // BLOCK
    own = tokens // count
    x = x_ref[...].astype(jnp.float32)
    squares = jnp.sum(x * x, axis=1, keepdims=True)
    scaled = (x * gain_ref[...]).astype(jnp.bfloat16)
    partial = jnp.dot(scaled, w_ref[...], preferred_element_type=jnp.float32)
    lane = lax.broadcasted_iota(jnp.int32, (count, LANES), 1)
    last = jnp.zeros((count, LANES), jnp.float32)
    for k in range(own):
        part = slice(k * count, (k + 1) * count)
        for b in range(SUB + 2):
            line = k * SUB + b if b < SUB else (own * (b - SUB) + own * SUB + k)
            out_ref[pl.ds(line, count, stride=BLOCK)] = partial[part, b * LANES : (b + 1) * LANES]
        last = jnp.where(lane // SPAN == k, squares[part], last)
    out_ref[pl.ds(BLOCK - 2, count, stride=BLOCK)] = last
    out_ref[pl.ds(BLOCK - 1, count, stride=BLOCK)] = jnp.zeros((count, LANES), jnp.float32)


def finish_kernel(parts_ref, rope_ref, out_ref):
    count, block, head_dim = parts_ref.shape
    own = block // SUB - 1
    summed = parts_ref[0]
    for j in range(1, count):
        summed = summed + parts_ref[j]
    inverse = lax.rsqrt(summed[block - 2 : block - 1] / D + epsilon)
    line = lax.broadcasted_iota(jnp.int32, (block, head_dim), 0)
    scale = jnp.zeros((block, head_dim), jnp.float32)
    for k in range(own):
        here = (line // SUB == k) | (line == own * SUB + k) | (line == own * SUB + own + k)
        here = here & ((line < own * SUB) | (line % SUB < 2 * own))
        scale = jnp.where(here, inverse[:, k * SPAN : k * SPAN + 1], scale)
    normed = summed * scale
    turned = normed * rope_ref[:block] + pltpu.roll(normed, head_dim // 2, 1) * rope_ref[block:]
    turned = jnp.where(line < own * SUB, turned * head_dim ** (-0.5), turned).astype(jnp.bfloat16)
    for j in range(out_ref.shape[0]):
        out_ref[j] = turned


def attend_kernel(
    limits_ref, rows_ref, k_ref, v_ref, out_ref, scores_ref, held_ref, stats_ref
):
    row_count, cache_dev, head_dim = k_ref.shape
    count = rows_ref.shape[0]
    per_row = 2 * SUB
    near = LANES // per_row
    groups = row_count // near
    chunk = 512
    me = lax.axis_index("seq")
    lane = lax.broadcasted_iota(jnp.int32, (1, LANES), 1)
    position = lax.broadcasted_iota(jnp.int32, (chunk, LANES), 0)
    slot = lax.broadcasted_iota(jnp.int32, (LANES, LANES), 0)
    held_ref[...] = rows_ref[...].astype(jnp.float32)
    new_keys = held_ref[:, groups * SUB :].reshape(count * SUB, head_dim)
    new_values = pltpu.roll(new_keys, LANES - groups, 0).astype(jnp.bfloat16)
    new_keys = new_keys.astype(jnp.bfloat16)
    stats_ref[...] = jnp.zeros_like(stats_ref)

    def attend_group(g, carry):
        own_rows = pl.ds(pl.multiple_of(g * SUB, SUB), SUB)
        turned = held_ref[:, own_rows].reshape(count * SUB, head_dim).T
        blocks = [
            jnp.where(lane // per_row == r, turned, 0.0).astype(jnp.bfloat16) for r in range(near)
        ]
        weights = jnp.concatenate(blocks, axis=0)
        limit = limits_ref[pl.ds(g, 1)]
        fresh = jnp.dot(new_keys, turned.astype(jnp.bfloat16), preferred_element_type=jnp.float32)
        seen = (
            (slot % SUB == g)
            & (slot // per_row == lane // per_row)
            & (slot // SUB <= lane // SUB)
            & (me == 0)
        )
        fresh = jnp.where(seen, fresh, negative)
        top = jnp.max(fresh, axis=0, keepdims=True)
        for c in range(cache_dev // chunk):
            keys = jnp.concatenate(
                [k_ref[g * near + r, pl.ds(c * chunk, chunk)] for r in range(near)], axis=1
            )
            scores = jnp.dot(keys, weights, preferred_element_type=jnp.float32)
            scores = jnp.where(position < limit - c * chunk, scores, negative)
            scores_ref[pl.ds(c * chunk, chunk)] = scores
            top = jnp.maximum(top, jnp.max(scores, axis=0, keepdims=True))
        fresh = jnp.exp(fresh - top)
        total = jnp.sum(fresh, axis=0, keepdims=True)
        parts = []
        for c in range(cache_dev // chunk):
            weight = jnp.exp(scores_ref[pl.ds(c * chunk, chunk)] - top)
            total = total + jnp.sum(weight, axis=0, keepdims=True)
            parts.append(weight.astype(jnp.bfloat16).T)
        parts = jnp.concatenate(parts, axis=1)
        value = jnp.concatenate(
            [
                jnp.dot(
                    parts[r * per_row : (r + 1) * per_row],
                    v_ref[g * near + r],
                    preferred_element_type=jnp.float32,
                )
                for r in range(near)
            ],
            axis=0,
        ) + jnp.dot(fresh.T.astype(jnp.bfloat16), new_values, preferred_element_type=jnp.float32)
        for j in range(count):
            out_ref[j, own_rows] = value[j * SUB : (j + 1) * SUB]
        stats_ref[pl.ds(g, 1)] = top
        stats_ref[pl.ds(groups + g, 1)] = total
        return carry

    lax.fori_loop(0, groups, attend_group, 0)
    stats = stats_ref[...]
    for j in range(count):
        turn = (LANES - SUB * j) % LANES
        out_ref[j, pl.ds(groups * SUB, SUB)] = pltpu.roll(stats, turn, 1) if turn else stats


def merge_kernel(parts_ref, out_ref):
    count, rows, head_dim = parts_ref.shape
    groups = rows // SUB - 1
    stats = parts_ref[:, groups * SUB :]
    top = stats[0]
    for j in range(1, count):
        top = jnp.maximum(top, stats[j])
    factors = [jnp.exp(stats[j] - top) for j in range(count)]
    denominator = factors[0] * pltpu.roll(stats[0], SUB - groups, 0)
    for j in range(1, count):
        denominator = denominator + factors[j] * pltpu.roll(stats[j], SUB - groups, 0)
    shares = jnp.concatenate([factor / denominator for factor in factors], axis=0).T[:SUB]
    merged = []
    for g in range(groups):
        total = jnp.zeros((SUB, head_dim), jnp.float32)
        for j in range(count):
            column = j * SUB + g
            total = total + parts_ref[j, pl.ds(g * SUB, SUB)] * shares[:, column : column + 1]
        merged.append(total)
    merged = jnp.concatenate(merged, axis=1).astype(jnp.bfloat16)
    for j in range(out_ref.shape[0]):
        out_ref[j] = merged


def output_kernel(attention_ref, w_ref, out_ref, held):
    count, heads, width = attention_ref.shape
    groups, _, head_dim = held.shape
    for g in range(groups):
        part = attention_ref[:, :, g * head_dim : (g + 1) * head_dim]
        held[g] = part.astype(jnp.float32).reshape(count * heads, head_dim)
    left = jnp.concatenate(
        [
            jnp.concatenate(
                [
                    held[g, pl.ds(step * heads + i, count // 2, stride=2 * heads)]
                    for i in range(heads)
                ],
                axis=1,
            )
            for step in range(2)
            for g in range(groups)
        ],
        axis=0,
    )
    out_ref[...] = jnp.dot(left.astype(jnp.bfloat16), w_ref[...], preferred_element_type=jnp.float32)


def double(array, axis_name, mask, size):
    pairs = [(i, i ^ mask) for i in range(size)]
    return array + lax.ppermute(array, axis_name, pairs)


def body(token_ids, lengths, embedding, norm_gain, w_qkv, k_cache, v_cache, w_out):
    n_seq, n_head = lax.axis_size("seq"), lax.axis_size("head")
    feat = embedding.shape[1]
    row_count, _, cache_dev, head_dim = k_cache.shape
    tokens = 2 * row_count
    own = tokens // n_seq
    width = w_qkv.shape[2]

    picked, rope, limits = pl.pallas_call(
        functools.partial(pick_kernel, cache_dev),
        out_shape=[
            jax.ShapeDtypeStruct((tokens, feat), jnp.bfloat16),
            jax.ShapeDtypeStruct((2 * BLOCK, LANES), jnp.float32),
            jax.ShapeDtypeStruct((SUB, LANES), jnp.int32),
        ],
        in_specs=[SMEM, SMEM, VMEM, ANY],
        out_specs=[VMEM] * 3,
        scratch_shapes=[
            pltpu.VMEM((tokens * TILE, feat), jnp.bfloat16),
            pltpu.SemaphoreType.DMA,
        ],
        compiler_params=pltpu.CompilerParams(vmem_limit_bytes=8 << 20),
        name="pick",
    )(
        in_hbm(token_ids),
        in_hbm(lengths),
        rope_frequency(head_dim),
        in_hbm(embedding),
    )
    w_near = fetch(picked, w_qkv.reshape(feat, width))
    for mask in (1, 2, 6):
        picked = double(picked, "head", mask, n_head)
    gain = norm_gain.astype(jnp.float32).reshape(1, feat)

    partial = call(
        project_kernel, "project", ((n_seq * BLOCK, head_dim), jnp.float32), [VMEM] * 3
    )(picked, gain, in_vmem(w_near))
    partial = swap(partial.reshape(n_seq, BLOCK, head_dim), "seq")
    rows = call(finish_kernel, "finish", ((n_seq, BLOCK, head_dim), jnp.bfloat16), [VMEM] * 2)(
        partial, rope
    )
    rows = swap(rows, "seq")

    partial = call(
        attend_kernel,
        "attend",
        ((n_seq, BLOCK, head_dim), jnp.float32),
        [VMEM] * 4,
        [
            pltpu.VMEM((cache_dev, LANES), jnp.float32),
            pltpu.VMEM((n_seq, BLOCK, head_dim), jnp.float32),
            pltpu.VMEM((SUB, LANES), jnp.float32),
        ],
        8,
    )(limits, rows, in_vmem(k_cache[:, 0]), in_vmem(v_cache[:, 0]))
    partial = swap(partial, "seq")
    attention = call(merge_kernel, "merge", ((n_seq, SUB, own * head_dim), jnp.bfloat16), [VMEM])(
        partial
    )
    attention = swap(attention, "seq")

    terms = call(
        output_kernel,
        "output",
        ((tokens, w_out.shape[2]), jnp.float32),
        [VMEM] * 2,
        [pltpu.VMEM((own, n_seq * SUB, head_dim), jnp.float32)],
    )(attention, in_vmem(w_out[0]))
    for mask in (2, 6, 1):
        terms = double(terms, "head", mask, n_head)
    return terms.astype(jnp.bfloat16).reshape(2, row_count, -1)


def solution(mesh):
    return jax.shard_map(
        body,
        mesh=mesh,
        in_specs=(
            P(),
            P(),
            P("head", "seq"),
            P("seq"),
            P("seq", "head", None),
            P(None, "head", "seq", None),
            P(None, "head", "seq", None),
            P("head", None, "seq"),
        ),
        out_specs=P(None, None, "seq"),
        check_vma=False,
    )
```

```python
import functools

import jax
import jax.numpy as jnp
from jax import lax
from jax.experimental import pallas as pl
from jax.experimental.pallas import tpu as pltpu
from jax.sharding import PartitionSpec as P

D = 8192
TILE = 16
LANES = 128
SUB = 8
BLOCK = 32
SPAN = 32
HALF = 4

rope_base = 500000.0
epsilon = 1e-05
negative = -1e30

VMEM = pl.BlockSpec(memory_space=pltpu.VMEM)
SMEM = pl.BlockSpec(memory_space=pltpu.SMEM)
ANY = pl.BlockSpec(memory_space=pl.ANY)


def in_vmem(array):
    return pltpu.with_memory_space_constraint(array, pltpu.VMEM)


def in_hbm(array):
    return pltpu.with_memory_space_constraint(array, pltpu.HBM)


def call(kernel, name, out, in_specs, scratch=(), limit=4):
    return pl.pallas_call(
        kernel,
        out_shape=jax.ShapeDtypeStruct(*out),
        in_specs=in_specs,
        out_specs=VMEM,
        scratch_shapes=list(scratch),
        compiler_params=pltpu.CompilerParams(vmem_limit_bytes=limit << 20),
        name=name,
    )


def swap(array, axis_name):
    return lax.all_to_all(array, axis_name, 0, 0, tiled=True)


def rope_frequency(head_dim):
    exponent = jnp.arange(head_dim // 2, dtype=jnp.float32) * (2.0 / head_dim)
    frequency = jnp.power(jnp.float32(rope_base), -exponent)
    return jnp.concatenate([frequency, frequency])[None, :]


def cos_sin(angles):
    turn = jnp.floor(angles * 0.6366197723675814 + 0.5)
    rest = ((angles - turn * 1.5703125) - turn * 0.00048351287841796875) - turn * 3.13916478589249e-07
    square = rest * rest
    sine = ((-1.9515295891e-4 * square + 8.3321608736e-3) * square - 1.6666654611e-1) * square
    sine = sine * rest + rest
    cosine = (2.443315711809948e-5 * square - 1.388731625493765e-3) * square
    cosine = (cosine + 4.166664568298827e-2) * square * square - 0.5 * square + 1.0
    quarter = turn.astype(jnp.int32) & 3
    odd = (quarter & 1) == 1
    first, second = jnp.where(odd, sine, cosine), jnp.where(odd, cosine, sine)
    return (
        jnp.where((quarter == 1) | (quarter == 2), -first, first),
        jnp.where(quarter >= 2, -second, second),
    )


def pick_kernel(
    cache_dev, ids_ref, lengths_ref, frequency_ref, table_ref,
    x_ref, rope_ref, limits_ref, held, sem,
):
    vocab_dev, feat = table_ref.shape
    steps, rows = ids_ref.shape
    tokens = steps * rows
    first = lax.axis_index("head") * vocab_dev
    held[...] = jnp.zeros_like(held)
    places = []
    found = 0
    for i in range(tokens):
        local = ids_ref[i // rows, i % rows] - first
        inside = (local >= 0) & (local < vocab_dev)
        local = jnp.clip(local, 0, vocab_dev - 1)
        within = local & (TILE - 1)

        @pl.when(inside)
        def _(start=local - within, i=i):
            pltpu.make_async_copy(
                table_ref.at[pl.ds(pl.multiple_of(start, TILE), TILE)],
                held.at[pl.ds(i * TILE, TILE)],
                sem,
            ).start(priority=1)

        found = found + inside.astype(jnp.int32)
        places.append(jnp.where(inside, i * TILE + within, -1))

    me = lax.axis_index("seq")
    near = LANES // (2 * SUB)
    sub = lax.broadcasted_iota(jnp.int32, (SUB, LANES), 0)
    lane = lax.broadcasted_iota(jnp.int32, (SUB, LANES), 1)
    own = rows // near
    block = rope_ref.shape[0] // 2
    line = lax.broadcasted_iota(jnp.int32, (block, LANES), 0)
    position = jnp.zeros((block, LANES), jnp.int32)
    limits = jnp.zeros((SUB, LANES), jnp.int32)
    for g in range(own):
        here = (line // SUB == g) | (line == own * SUB + g)
        position = jnp.where(here, lengths_ref[g * near + me // 2] + me % 2, position)
        for r in range(near):
            here = (sub == g) & (lane // (2 * SUB) == r)
            limits = jnp.where(here, lengths_ref[g * near + r], limits)
    limits_ref[...] = limits - me * cache_dev
    cosine, sine = cos_sin(position.astype(jnp.float32) * frequency_ref[...])
    turned = line < own * SUB + own
    first_half = lax.broadcasted_iota(jnp.int32, (block, LANES), 1) < LANES // 2
    rope_ref[:block] = jnp.where(turned, cosine, 1.0)
    rope_ref[block:] = jnp.where(turned, jnp.where(first_half, -sine, sine), 0.0)

    row = lax.broadcasted_iota(jnp.int32, (tokens, 1), 0)
    choice = jnp.full((tokens, 1), -1, jnp.int32)
    for i in range(tokens):
        step, r = i // rows, i % rows
        choice = jnp.where(row == r // near * 2 * near + r % near * 2 + step, places[i], choice)
    column = lax.broadcasted_iota(jnp.int32, (tokens, tokens * TILE), 1)
    select = jnp.where(column == choice, 1.0, 0.0).astype(jnp.bfloat16)
    def wait(i, carry):
        pltpu.make_async_copy(table_ref.at[pl.ds(0, TILE)], held.at[pl.ds(0, TILE)], sem).wait()
        return carry

    lax.fori_loop(0, found, wait, 0)
    picked = jnp.dot(select, held[...], preferred_element_type=jnp.float32)
    x_ref[...] = picked.astype(jnp.bfloat16)


def fetch_kernel(after_ref, far_ref, near_ref, sem):
    copy = pltpu.make_async_copy(far_ref, near_ref, sem)
    copy.start()
    copy.wait()


def fetch(after, array):
    return pl.pallas_call(
        fetch_kernel,
        out_shape=pltpu.VMEM(array.shape, array.dtype),
        in_specs=[ANY] * 2,
        out_specs=VMEM,
        scratch_shapes=[pltpu.SemaphoreType.DMA],
        cost_estimate=pl.CostEstimate(
            flops=0, bytes_accessed=2 * array.size * array.dtype.itemsize, transcendentals=0
        ),
        compiler_params=pltpu.CompilerParams(vmem_limit_bytes=4 << 20),
        name="fetch",
    )(after, in_hbm(array))


def project_kernel(x_ref, gain_ref, w_ref, out_ref):
    tokens = x_ref.shape[0]
    count = out_ref.shape[0] // BLOCK
    own = tokens // count
    x = x_ref[...].astype(jnp.float32)
    squares = jnp.sum(x * x, axis=1, keepdims=True)
    scaled = (x * gain_ref[...]).astype(jnp.bfloat16)
    partial = jnp.dot(scaled, w_ref[...], preferred_element_type=jnp.float32)
    lane = lax.broadcasted_iota(jnp.int32, (count, LANES), 1)
    last = jnp.zeros((count, LANES), jnp.float32)
    for k in range(own):
        part = slice(k * count, (k + 1) * count)
        for b in range(SUB + 2):
            line = k * SUB + b if b < SUB else (own * (b - SUB) + own * SUB + k)
            out_ref[pl.ds(line, count, stride=BLOCK)] = partial[part, b * LANES : (b + 1) * LANES]
        last = jnp.where(lane // SPAN == k, squares[part], last)
    out_ref[pl.ds(BLOCK - 2, count, stride=BLOCK)] = last
    out_ref[pl.ds(BLOCK - 1, count, stride=BLOCK)] = jnp.zeros((count, LANES), jnp.float32)


def finish_kernel(parts_ref, rope_ref, out_ref):
    count, block, head_dim = parts_ref.shape
    own = block // SUB - 1
    summed = parts_ref[0]
    for j in range(1, count):
        summed = summed + parts_ref[j]
    inverse = lax.rsqrt(summed[block - 2 : block - 1] / D + epsilon)
    line = lax.broadcasted_iota(jnp.int32, (block, head_dim), 0)
    scale = jnp.zeros((block, head_dim), jnp.float32)
    for k in range(own):
        here = (line // SUB == k) | (line == own * SUB + k) | (line == own * SUB + own + k)
        here = here & ((line < own * SUB) | (line % SUB < 2 * own))
        scale = jnp.where(here, inverse[:, k * SPAN : k * SPAN + 1], scale)
    normed = summed * scale
    turned = normed * rope_ref[:block] + pltpu.roll(normed, head_dim // 2, 1) * rope_ref[block:]
    turned = jnp.where(line < own * SUB, turned * head_dim ** (-0.5), turned).astype(jnp.bfloat16)
    for j in range(out_ref.shape[0]):
        out_ref[j] = turned


def attend_kernel(limits_ref, rows_ref, k_ref, v_ref, out_ref, scores_ref):
    row_count, cache_dev, head_dim = k_ref.shape
    count = rows_ref.shape[0]
    per_row = 2 * SUB
    near = LANES // per_row
    groups = row_count // near
    chunk = 512
    me = lax.axis_index("seq")
    lane = lax.broadcasted_iota(jnp.int32, (1, LANES), 1)
    position = lax.broadcasted_iota(jnp.int32, (chunk, LANES), 0)
    slot = lax.broadcasted_iota(jnp.int32, (LANES, LANES), 0)
    rows = rows_ref[...].astype(jnp.float32)
    new_keys = rows[:, groups * SUB :].reshape(count * SUB, head_dim)
    new_values = pltpu.roll(new_keys, LANES - groups, 0).astype(jnp.bfloat16)
    new_keys = new_keys.astype(jnp.bfloat16)

    def score(g):
        turned = rows[:, g * SUB : (g + 1) * SUB].reshape(count * SUB, head_dim).T
        blocks = [
            jnp.where(lane // per_row == r, turned, 0.0).astype(jnp.bfloat16) for r in range(near)
        ]
        weights = jnp.concatenate(blocks, axis=0)
        limit = limits_ref[g : g + 1]
        fresh = jnp.dot(new_keys, turned.astype(jnp.bfloat16), preferred_element_type=jnp.float32)
        seen = (
            (slot % SUB == g)
            & (slot // per_row == lane // per_row)
            & (slot // SUB <= lane // SUB)
            & (me == 0)
        )
        fresh = jnp.where(seen, fresh, negative)
        top = jnp.max(fresh, axis=0, keepdims=True)
        for c in range(cache_dev // chunk):
            keys = jnp.concatenate(
                [k_ref[g * near + r, pl.ds(c * chunk, chunk)] for r in range(near)], axis=1
            )
            scores = jnp.dot(keys, weights, preferred_element_type=jnp.float32)
            scores = jnp.where(position < limit - c * chunk, scores, negative)
            scores_ref[g, pl.ds(c * chunk, chunk)] = scores
            top = jnp.maximum(top, jnp.max(scores, axis=0, keepdims=True))
        return top, fresh

    def weigh(g, top, fresh):
        fresh = jnp.exp(fresh - top)
        total = jnp.sum(fresh, axis=0, keepdims=True)
        parts = []
        for c in range(cache_dev // chunk):
            weight = jnp.exp(scores_ref[g, pl.ds(c * chunk, chunk)] - top)
            total = total + jnp.sum(weight, axis=0, keepdims=True)
            parts.append(weight.astype(jnp.bfloat16).T)
        parts = jnp.concatenate(parts, axis=1)
        value = jnp.concatenate(
            [
                jnp.dot(
                    parts[r * per_row : (r + 1) * per_row],
                    v_ref[g * near + r],
                    preferred_element_type=jnp.float32,
                )
                for r in range(near)
            ],
            axis=0,
        ) + jnp.dot(fresh.T.astype(jnp.bfloat16), new_values, preferred_element_type=jnp.float32)
        for j in range(count):
            for h in range(2):
                start = j * SUB + h * HALF
                out_ref[j, 2 * g + h] = value[start : start + HALF]
        return total

    tops, totals = [], []
    ready = score(0)
    for g in range(groups):
        later = score(g + 1) if g + 1 < groups else None
        tops.append(ready[0])
        totals.append(weigh(g, *ready))
        ready = later
    spare = jnp.zeros((SUB - groups, LANES), jnp.float32)
    tops = jnp.concatenate(tops + [spare], axis=0)
    totals = pltpu.roll(jnp.concatenate(totals + [spare], axis=0), SUB, 1)
    for j in range(count):
        turn = (LANES - SUB * j) % LANES
        both = jnp.where(
            lane < SUB,
            pltpu.roll(tops, turn, 1) if turn else tops,
            pltpu.roll(totals, turn, 1) if turn else totals,
        )
        out_ref[j, 2 * groups] = both[:HALF]


def merge_kernel(parts_ref, out_ref):
    count, pieces, _, head_dim = parts_ref.shape
    groups = pieces // 2
    stats = [parts_ref[j, 2 * groups] for j in range(count)]
    top = stats[0]
    for j in range(1, count):
        top = jnp.maximum(top, stats[j])
    factors = [jnp.exp(jnp.minimum(stats[j] - top, 0.0)) for j in range(count)]
    denominator = jnp.zeros((HALF, head_dim), jnp.float32)
    for j in range(count):
        denominator = denominator + factors[j] * pltpu.roll(stats[j], head_dim - SUB, 1)
    shares = jnp.concatenate([factor / denominator for factor in factors], axis=0)
    shares = jnp.concatenate([shares, jnp.zeros_like(shares)], axis=0).T[:SUB]
    merged = []
    for g in range(groups):
        total = jnp.zeros((SUB, head_dim), jnp.float32)
        for j in range(count):
            column = j * HALF + g
            part = jnp.concatenate([parts_ref[j, 2 * g], parts_ref[j, 2 * g + 1]], axis=0)
            total = total + part * shares[:, column : column + 1]
        merged.append(total)
    merged = jnp.concatenate(merged, axis=1).astype(jnp.bfloat16)
    for j in range(out_ref.shape[0]):
        out_ref[j] = merged


def output_kernel(attention_ref, w_ref, out_ref, held):
    count, heads, width = attention_ref.shape
    groups, _, head_dim = held.shape
    for g in range(groups):
        part = attention_ref[:, :, g * head_dim : (g + 1) * head_dim]
        held[g] = part.astype(jnp.float32).reshape(count * heads, head_dim)
    left = jnp.concatenate(
        [
            jnp.concatenate(
                [
                    held[g, pl.ds(step * heads + i, count // 2, stride=2 * heads)]
                    for i in range(heads)
                ],
                axis=1,
            )
            for step in range(2)
            for g in range(groups)
        ],
        axis=0,
    )
    out_ref[...] = jnp.dot(left.astype(jnp.bfloat16), w_ref[...], preferred_element_type=jnp.float32)


def double(array, axis_name, mask, size):
    pairs = [(i, i ^ mask) for i in range(size)]
    return array + lax.ppermute(array, axis_name, pairs)


def body(token_ids, lengths, embedding, norm_gain, w_qkv, k_cache, v_cache, w_out):
    n_seq, n_head = lax.axis_size("seq"), lax.axis_size("head")
    feat = embedding.shape[1]
    row_count, _, cache_dev, head_dim = k_cache.shape
    tokens = 2 * row_count
    own = tokens // n_seq
    width = w_qkv.shape[2]

    picked, rope, limits = pl.pallas_call(
        functools.partial(pick_kernel, cache_dev),
        out_shape=[
            jax.ShapeDtypeStruct((tokens, feat), jnp.bfloat16),
            jax.ShapeDtypeStruct((2 * BLOCK, LANES), jnp.float32),
            jax.ShapeDtypeStruct((SUB, LANES), jnp.int32),
        ],
        in_specs=[SMEM, SMEM, VMEM, ANY],
        out_specs=[VMEM] * 3,
        scratch_shapes=[
            pltpu.VMEM((tokens * TILE, feat), jnp.bfloat16),
            pltpu.SemaphoreType.DMA,
        ],
        compiler_params=pltpu.CompilerParams(vmem_limit_bytes=8 << 20),
        name="pick",
    )(
        in_hbm(token_ids),
        in_hbm(lengths),
        rope_frequency(head_dim),
        in_hbm(embedding),
    )
    w_near = fetch(picked, w_qkv.reshape(feat, width))
    for mask in (1, 2, 6):
        picked = double(picked, "head", mask, n_head)
    gain = norm_gain.astype(jnp.float32).reshape(1, feat)

    partial = call(
        project_kernel, "project", ((n_seq * BLOCK, head_dim), jnp.float32), [VMEM] * 3
    )(picked, gain, in_vmem(w_near))
    partial = swap(partial.reshape(n_seq, BLOCK, head_dim), "seq")
    rows = call(finish_kernel, "finish", ((n_seq, BLOCK, head_dim), jnp.bfloat16), [VMEM] * 2)(
        partial, rope
    )
    rows = swap(rows, "seq")

    partial = call(
        attend_kernel,
        "attend",
        ((n_seq, 2 * own + 1, HALF, head_dim), jnp.float32),
        [VMEM] * 4,
        [pltpu.VMEM((own, cache_dev, LANES), jnp.float32)],
        8,
    )(limits, rows, in_vmem(k_cache[:, 0]), in_vmem(v_cache[:, 0]))
    partial = swap(partial, "seq")
    attention = call(merge_kernel, "merge", ((n_seq, SUB, own * head_dim), jnp.bfloat16), [VMEM])(
        partial
    )
    attention = swap(attention, "seq")

    terms = call(
        output_kernel,
        "output",
        ((tokens, w_out.shape[2]), jnp.float32),
        [VMEM] * 2,
        [pltpu.VMEM((own, n_seq * SUB, head_dim), jnp.float32)],
    )(attention, in_vmem(w_out[0]))
    for mask in (2, 6, 1):
        terms = double(terms, "head", mask, n_head)
    return terms.astype(jnp.bfloat16).reshape(2, row_count, -1)


def solution(mesh):
    return jax.shard_map(
        body,
        mesh=mesh,
        in_specs=(
            P(),
            P(),
            P("head", "seq"),
            P("seq"),
            P("seq", "head", None),
            P(None, "head", "seq", None),
            P(None, "head", "seq", None),
            P("head", None, "seq"),
        ),
        out_specs=P(None, None, "seq"),
        check_vma=False,
    )
```

```python
import functools

import jax
import jax.numpy as jnp
from jax import lax
from jax.experimental import pallas as pl
from jax.experimental.pallas import tpu as pltpu
from jax.sharding import PartitionSpec as P

D = 8192
TILE = 16
LANES = 128
SUB = 8
BLOCK = 32
SPAN = 32
HALF = 4

rope_base = 500000.0
epsilon = 1e-05
negative = -1e30

VMEM = pl.BlockSpec(memory_space=pltpu.VMEM)
SMEM = pl.BlockSpec(memory_space=pltpu.SMEM)
ANY = pl.BlockSpec(memory_space=pl.ANY)


def in_vmem(array):
    return pltpu.with_memory_space_constraint(array, pltpu.VMEM)


def in_hbm(array):
    return pltpu.with_memory_space_constraint(array, pltpu.HBM)


def call(kernel, name, out, in_specs, scratch=(), limit=4):
    return pl.pallas_call(
        kernel,
        out_shape=jax.ShapeDtypeStruct(*out),
        in_specs=in_specs,
        out_specs=VMEM,
        scratch_shapes=list(scratch),
        compiler_params=pltpu.CompilerParams(vmem_limit_bytes=limit << 20),
        name=name,
    )


def swap(array, axis_name):
    return lax.all_to_all(array, axis_name, 0, 0, tiled=True)


def rope_frequency(head_dim):
    exponent = jnp.arange(head_dim // 2, dtype=jnp.float32) * (2.0 / head_dim)
    frequency = jnp.power(jnp.float32(rope_base), -exponent)
    return jnp.concatenate([frequency, frequency])[None, :]


def cos_sin(angles):
    turn = jnp.floor(angles * 0.6366197723675814 + 0.5)
    rest = ((angles - turn * 1.5703125) - turn * 0.00048351287841796875) - turn * 3.13916478589249e-07
    square = rest * rest
    sine = ((-1.9515295891e-4 * square + 8.3321608736e-3) * square - 1.6666654611e-1) * square
    sine = sine * rest + rest
    cosine = (2.443315711809948e-5 * square - 1.388731625493765e-3) * square
    cosine = (cosine + 4.166664568298827e-2) * square * square - 0.5 * square + 1.0
    quarter = turn.astype(jnp.int32) & 3
    odd = (quarter & 1) == 1
    first, second = jnp.where(odd, sine, cosine), jnp.where(odd, cosine, sine)
    return (
        jnp.where((quarter == 1) | (quarter == 2), -first, first),
        jnp.where(quarter >= 2, -second, second),
    )


def pick_kernel(ids_ref, table_ref, x_ref, held, sem):
    vocab_dev, feat = table_ref.shape
    steps, rows = ids_ref.shape
    tokens = steps * rows
    first = lax.axis_index("head") * vocab_dev
    held[...] = jnp.zeros_like(held)
    places = []
    found = 0
    for i in range(tokens):
        local = ids_ref[i // rows, i % rows] - first
        inside = (local >= 0) & (local < vocab_dev)
        local = jnp.clip(local, 0, vocab_dev - 1)
        within = local & (TILE - 1)

        @pl.when(inside)
        def _(start=local - within, i=i):
            pltpu.make_async_copy(
                table_ref.at[pl.ds(pl.multiple_of(start, TILE), TILE)],
                held.at[pl.ds(i * TILE, TILE)],
                sem,
            ).start(priority=1)

        found = found + inside.astype(jnp.int32)
        places.append(jnp.where(inside, i * TILE + within, -1))

    near = LANES // (2 * SUB)
    row = lax.broadcasted_iota(jnp.int32, (tokens, 1), 0)
    choice = jnp.full((tokens, 1), -1, jnp.int32)
    for i in range(tokens):
        step, r = i // rows, i % rows
        choice = jnp.where(row == r // near * 2 * near + r % near * 2 + step, places[i], choice)
    column = lax.broadcasted_iota(jnp.int32, (tokens, tokens * TILE), 1)
    select = jnp.where(column == choice, 1.0, 0.0).astype(jnp.bfloat16)
    def wait(i, carry):
        pltpu.make_async_copy(table_ref.at[pl.ds(0, TILE)], held.at[pl.ds(0, TILE)], sem).wait()
        return carry

    lax.fori_loop(0, found, wait, 0)
    picked = jnp.dot(select, held[...], preferred_element_type=jnp.float32)
    x_ref[...] = picked.astype(jnp.bfloat16)


def prepare_kernel(
    cache_dev, after_ref, lengths_ref, frequency_ref, far_w_ref, rope_ref, limits_ref, w_ref, sem
):
    copy = pltpu.make_async_copy(far_w_ref, w_ref, sem)
    copy.start()
    rows = lengths_ref.shape[0]
    me = lax.axis_index("seq")
    near = LANES // (2 * SUB)
    sub = lax.broadcasted_iota(jnp.int32, (SUB, LANES), 0)
    lane = lax.broadcasted_iota(jnp.int32, (SUB, LANES), 1)
    own = rows // near
    block = rope_ref.shape[0] // 2
    line = lax.broadcasted_iota(jnp.int32, (block, LANES), 0)
    position = jnp.zeros((block, LANES), jnp.int32)
    limits = jnp.zeros((SUB, LANES), jnp.int32)
    for g in range(own):
        here = (line // SUB == g) | (line == own * SUB + g)
        position = jnp.where(here, lengths_ref[g * near + me // 2] + me % 2, position)
        for r in range(near):
            here = (sub == g) & (lane // (2 * SUB) == r)
            limits = jnp.where(here, lengths_ref[g * near + r], limits)
    limits_ref[...] = limits - me * cache_dev
    cosine, sine = cos_sin(position.astype(jnp.float32) * frequency_ref[...])
    turned = line < own * SUB + own
    first_half = lax.broadcasted_iota(jnp.int32, (block, LANES), 1) < LANES // 2
    rope_ref[:block] = jnp.where(turned, cosine, 1.0)
    rope_ref[block:] = jnp.where(turned, jnp.where(first_half, -sine, sine), 0.0)
    copy.wait()


def prepare(after, lengths, frequency, w, cache_dev):
    return pl.pallas_call(
        functools.partial(prepare_kernel, cache_dev),
        out_shape=[
            jax.ShapeDtypeStruct((2 * BLOCK, LANES), jnp.float32),
            jax.ShapeDtypeStruct((SUB, LANES), jnp.int32),
            pltpu.VMEM(w.shape, w.dtype),
        ],
        in_specs=[ANY, SMEM, VMEM, ANY],
        out_specs=[VMEM] * 3,
        scratch_shapes=[pltpu.SemaphoreType.DMA],
        cost_estimate=pl.CostEstimate(
            flops=0, bytes_accessed=2 * w.size * w.dtype.itemsize, transcendentals=0
        ),
        compiler_params=pltpu.CompilerParams(vmem_limit_bytes=4 << 20),
        name="prepare",
    )(after, in_hbm(lengths), frequency, in_hbm(w))


def project_kernel(x_ref, gain_ref, w_ref, out_ref):
    tokens = x_ref.shape[0]
    count = out_ref.shape[0] // BLOCK
    own = tokens // count
    x = x_ref[...].astype(jnp.float32)
    squares = jnp.sum(x * x, axis=1, keepdims=True)
    scaled = (x * gain_ref[...]).astype(jnp.bfloat16)
    partial = jnp.dot(scaled, w_ref[...], preferred_element_type=jnp.float32)
    lane = lax.broadcasted_iota(jnp.int32, (count, LANES), 1)
    last = jnp.zeros((count, LANES), jnp.float32)
    for k in range(own):
        part = slice(k * count, (k + 1) * count)
        for b in range(SUB + 2):
            line = k * SUB + b if b < SUB else (own * (b - SUB) + own * SUB + k)
            out_ref[pl.ds(line, count, stride=BLOCK)] = partial[part, b * LANES : (b + 1) * LANES]
        last = jnp.where(lane // SPAN == k, squares[part], last)
    out_ref[pl.ds(BLOCK - 2, count, stride=BLOCK)] = last
    out_ref[pl.ds(BLOCK - 1, count, stride=BLOCK)] = jnp.zeros((count, LANES), jnp.float32)


def finish_kernel(parts_ref, rope_ref, out_ref):
    count, block, head_dim = parts_ref.shape
    own = block // SUB - 1
    summed = parts_ref[0]
    for j in range(1, count):
        summed = summed + parts_ref[j]
    inverse = lax.rsqrt(summed[block - 2 : block - 1] / D + epsilon)
    line = lax.broadcasted_iota(jnp.int32, (block, head_dim), 0)
    scale = jnp.zeros((block, head_dim), jnp.float32)
    for k in range(own):
        here = (line // SUB == k) | (line == own * SUB + k) | (line == own * SUB + own + k)
        here = here & ((line < own * SUB) | (line % SUB < 2 * own))
        scale = jnp.where(here, inverse[:, k * SPAN : k * SPAN + 1], scale)
    normed = summed * scale
    turned = normed * rope_ref[:block] + pltpu.roll(normed, head_dim // 2, 1) * rope_ref[block:]
    turned = jnp.where(line < own * SUB, turned * head_dim ** (-0.5), turned).astype(jnp.bfloat16)
    for j in range(out_ref.shape[0]):
        out_ref[j] = turned


def attend_kernel(limits_ref, rows_ref, k_ref, v_ref, out_ref, scores_ref):
    row_count, cache_dev, head_dim = k_ref.shape
    count = rows_ref.shape[0]
    per_row = 2 * SUB
    near = LANES // per_row
    groups = row_count // near
    chunk = 512
    me = lax.axis_index("seq")
    lane = lax.broadcasted_iota(jnp.int32, (1, LANES), 1)
    position = lax.broadcasted_iota(jnp.int32, (chunk, LANES), 0)
    slot = lax.broadcasted_iota(jnp.int32, (LANES, LANES), 0)
    rows = rows_ref[...].astype(jnp.float32)
    new_keys = rows[:, groups * SUB :].reshape(count * SUB, head_dim)
    new_values = pltpu.roll(new_keys, LANES - groups, 0).astype(jnp.bfloat16)
    new_keys = new_keys.astype(jnp.bfloat16)

    def score(g):
        turned = rows[:, g * SUB : (g + 1) * SUB].reshape(count * SUB, head_dim).T
        blocks = [
            jnp.where(lane // per_row == r, turned, 0.0).astype(jnp.bfloat16) for r in range(near)
        ]
        weights = jnp.concatenate(blocks, axis=0)
        limit = limits_ref[g : g + 1]
        fresh = jnp.dot(new_keys, turned.astype(jnp.bfloat16), preferred_element_type=jnp.float32)
        seen = (
            (slot % SUB == g)
            & (slot // per_row == lane // per_row)
            & (slot // SUB <= lane // SUB)
            & (me == 0)
        )
        fresh = jnp.where(seen, fresh, negative)
        top = jnp.max(fresh, axis=0, keepdims=True)
        for c in range(cache_dev // chunk):
            keys = jnp.concatenate(
                [k_ref[g * near + r, pl.ds(c * chunk, chunk)] for r in range(near)], axis=1
            )
            scores = jnp.dot(keys, weights, preferred_element_type=jnp.float32)
            scores = jnp.where(position < limit - c * chunk, scores, negative)
            scores_ref[g, pl.ds(c * chunk, chunk)] = scores
            top = jnp.maximum(top, jnp.max(scores, axis=0, keepdims=True))
        return top, fresh

    def weigh(g, top, fresh):
        fresh = jnp.exp(fresh - top)
        total = jnp.sum(fresh, axis=0, keepdims=True)
        parts = []
        for c in range(cache_dev // chunk):
            weight = jnp.exp(scores_ref[g, pl.ds(c * chunk, chunk)] - top)
            total = total + jnp.sum(weight, axis=0, keepdims=True)
            parts.append(weight.astype(jnp.bfloat16).T)
        parts = jnp.concatenate(parts, axis=1)
        value = jnp.concatenate(
            [
                jnp.dot(
                    parts[r * per_row : (r + 1) * per_row],
                    v_ref[g * near + r],
                    preferred_element_type=jnp.float32,
                )
                for r in range(near)
            ],
            axis=0,
        ) + jnp.dot(fresh.T.astype(jnp.bfloat16), new_values, preferred_element_type=jnp.float32)
        for j in range(count):
            for h in range(2):
                start = j * SUB + h * HALF
                out_ref[j, 2 * g + h] = value[start : start + HALF]
        return total

    tops, totals = [], []
    ready = score(0)
    for g in range(groups):
        later = score(g + 1) if g + 1 < groups else None
        tops.append(ready[0])
        totals.append(weigh(g, *ready))
        ready = later
    spare = jnp.zeros((SUB - groups, LANES), jnp.float32)
    tops = jnp.concatenate(tops + [spare], axis=0)
    totals = pltpu.roll(jnp.concatenate(totals + [spare], axis=0), SUB, 1)
    for j in range(count):
        turn = (LANES - SUB * j) % LANES
        both = jnp.where(
            lane < SUB,
            pltpu.roll(tops, turn, 1) if turn else tops,
            pltpu.roll(totals, turn, 1) if turn else totals,
        )
        out_ref[j, 2 * groups] = both[:HALF]


def merge_kernel(parts_ref, out_ref):
    count, pieces, _, head_dim = parts_ref.shape
    groups = pieces // 2
    stats = [parts_ref[j, 2 * groups] for j in range(count)]
    top = stats[0]
    for j in range(1, count):
        top = jnp.maximum(top, stats[j])
    factors = [jnp.exp(jnp.minimum(stats[j] - top, 0.0)) for j in range(count)]
    denominator = jnp.zeros((HALF, head_dim), jnp.float32)
    for j in range(count):
        denominator = denominator + factors[j] * pltpu.roll(stats[j], head_dim - SUB, 1)
    shares = jnp.concatenate([factor / denominator for factor in factors], axis=0)
    shares = jnp.concatenate([shares, jnp.zeros_like(shares)], axis=0).T[:SUB]
    merged = []
    for g in range(groups):
        total = jnp.zeros((SUB, head_dim), jnp.float32)
        for j in range(count):
            column = j * HALF + g
            part = jnp.concatenate([parts_ref[j, 2 * g], parts_ref[j, 2 * g + 1]], axis=0)
            total = total + part * shares[:, column : column + 1]
        merged.append(total)
    merged = jnp.concatenate(merged, axis=1).astype(jnp.bfloat16)
    for j in range(out_ref.shape[0]):
        out_ref[j] = merged


def output_kernel(attention_ref, w_ref, out_ref, held):
    count, heads, width = attention_ref.shape
    groups, _, head_dim = held.shape
    for g in range(groups):
        part = attention_ref[:, :, g * head_dim : (g + 1) * head_dim]
        held[g] = part.astype(jnp.float32).reshape(count * heads, head_dim)
    left = jnp.concatenate(
        [
            jnp.concatenate(
                [
                    held[g, pl.ds(step * heads + i, count // 2, stride=2 * heads)]
                    for i in range(heads)
                ],
                axis=1,
            )
            for step in range(2)
            for g in range(groups)
        ],
        axis=0,
    )
    out_ref[...] = jnp.dot(left.astype(jnp.bfloat16), w_ref[...], preferred_element_type=jnp.float32)


def double(array, axis_name, mask, size):
    pairs = [(i, i ^ mask) for i in range(size)]
    return array + lax.ppermute(array, axis_name, pairs)


def body(token_ids, lengths, embedding, norm_gain, w_qkv, k_cache, v_cache, w_out):
    n_seq, n_head = lax.axis_size("seq"), lax.axis_size("head")
    feat = embedding.shape[1]
    row_count, _, cache_dev, head_dim = k_cache.shape
    tokens = 2 * row_count
    own = tokens // n_seq
    width = w_qkv.shape[2]

    picked = call(
        pick_kernel,
        "pick",
        ((tokens, feat), jnp.bfloat16),
        [SMEM, ANY],
        [pltpu.VMEM((tokens * TILE, feat), jnp.bfloat16), pltpu.SemaphoreType.DMA],
        8,
    )(in_hbm(token_ids), in_hbm(embedding))
    rope, limits, w_near = prepare(
        picked, lengths, rope_frequency(head_dim), w_qkv.reshape(feat, width), cache_dev
    )
    for mask in (1, 2, 6):
        picked = double(picked, "head", mask, n_head)
    gain = norm_gain.astype(jnp.float32).reshape(1, feat)

    partial = call(
        project_kernel, "project", ((n_seq * BLOCK, head_dim), jnp.float32), [VMEM] * 3
    )(picked, gain, in_vmem(w_near))
    partial = swap(partial.reshape(n_seq, BLOCK, head_dim), "seq")
    rows = call(finish_kernel, "finish", ((n_seq, BLOCK, head_dim), jnp.bfloat16), [VMEM] * 2)(
        partial, rope
    )
    rows = swap(rows, "seq")

    partial = call(
        attend_kernel,
        "attend",
        ((n_seq, 2 * own + 1, HALF, head_dim), jnp.float32),
        [VMEM] * 4,
        [pltpu.VMEM((own, cache_dev, LANES), jnp.float32)],
        8,
    )(limits, rows, in_vmem(k_cache[:, 0]), in_vmem(v_cache[:, 0]))
    partial = swap(partial, "seq")
    attention = call(merge_kernel, "merge", ((n_seq, SUB, own * head_dim), jnp.bfloat16), [VMEM])(
        partial
    )
    attention = swap(attention, "seq")

    terms = call(
        output_kernel,
        "output",
        ((tokens, w_out.shape[2]), jnp.float32),
        [VMEM] * 2,
        [pltpu.VMEM((own, n_seq * SUB, head_dim), jnp.float32)],
    )(attention, in_vmem(w_out[0]))
    for mask in (2, 6, 1):
        terms = double(terms, "head", mask, n_head)
    return terms.astype(jnp.bfloat16).reshape(2, row_count, -1)


def solution(mesh):
    return jax.shard_map(
        body,
        mesh=mesh,
        in_specs=(
            P(),
            P(),
            P("head", "seq"),
            P("seq"),
            P("seq", "head", None),
            P(None, "head", "seq", None),
            P(None, "head", "seq", None),
            P("head", None, "seq"),
        ),
        out_specs=P(None, None, "seq"),
        check_vma=False,
    )
```
